512 devices in a mesh: dp: 64 (over z, x), ctx: 8 (over y, core).
Axes of the slice: x: 4, y: 4, z: 16, core: 2. Of those that a mesh axis runs over, the one named last changes fastest.
Arguments:
- events: bfloat16 [64, 1024, 512], P('dp', 'ctx'), may hold values from -6 to 6
- keep: int32 [64, 1024], P('dp', 'ctx'), may hold values 0 or 1
- lengths: int32 [64], P('dp'), may hold values from 1 to 1024, as said below
- cotangent: bfloat16 [64, 1024, 512], P('dp', 'ctx'), may hold values from -6 to 6
- w_in: bfloat16 [512, 2048], replicated, may hold values from -0.25 to 0.25
- w_out: bfloat16 [512, 512], replicated, may hold values from -0.25 to 0.25
Outputs:
- output: bfloat16 [64, 1024, 512], P('dp', 'ctx')
- grad_events: bfloat16 [64, 1024, 512], P('dp', 'ctx')
- grad_w_out: float32 [512, 512], P('dp')
The draws below stay inside these ranges and needn't reach their ends.
Inputs may be any that keep to these rules, and one draw needn't show every extreme that they name: `lengths`: some history has length exactly 1024.
All inputs are finite; a program needn't handle non-finite values. No bound on the sum of `keep` on one device may be relied on, other than what follows from the above.
Results may differ from the reference program's by a relative error of at most 0.0074.
Values may be sent and summed in bfloat16 or wider, within the bound.
A program may use at most 64 MiB of HBM per device.

```python
import math
import jax
import jax.numpy as jnp
from jax import lax

D = 512
HEADS = 4
DH = 128
ATT = 512
L = 1024
HIST = 64
TOKENS = 65536


def draw_lengths(key, part):
    key = jax.random.fold_in(key, 7)
    first_key, second_key = jax.random.split(key)
    shifts = jax.random.randint(first_key, (HIST,), 0, 4)
    ceilings = jnp.right_shift(jnp.full((HIST,), L, jnp.int32), shifts)
    removed = jax.random.randint(second_key, (HIST,), 0, 1 << 20) % (ceilings // 2)
    drawn = ceilings - removed
    return drawn.at[0].set(L).astype(jnp.int32)


def touch_ends(values, key, low, largest):
    place = [jax.random.randint(jax.random.fold_in(key, axis), (), 0, length) for axis, length in enumerate(values.shape)]
    widest = values.shape.index(max(values.shape))
    next_to = place[:widest] + [(place[widest] + 1) % values.shape[widest]] + place[widest + 1:]
    return values.at[tuple(place)].set(low).at[tuple(next_to)].set(largest)


def block_levels(stream_key, extent, pieces, low, top_value):
    level, own = 1.0, jax.random.fold_in(stream_key, 6)
    for axis_at, parts in pieces:
        draws = jnp.exp(jax.random.uniform(jax.random.fold_in(own, axis_at), (parts,), jnp.float32, low / len(pieces), top_value / len(pieces)))
        level = level * jnp.repeat(draws, extent[axis_at] // parts).reshape([-1 if axis == axis_at else 1 for axis in range(len(extent))])
    return level


def scatter_about(key, extent, width, bound, cuts=(), kind=jnp.bfloat16):
    array = jax.random.normal(key, extent, jnp.float32) * width
    if len(cuts) > 0:
        array = block_levels(key, extent, cuts, -0.22, 0.18) * array
    return jnp.clip(array, min=-bound, max=bound).astype(kind)


def setup_inputs(seed: int = 0) -> dict:
    splits = jax.random.split(jax.random.key(seed), 7)
    return {
        "events": scatter_about(splits[0], (HIST, L, D), 1.0, 6.0, ((0, 64), (1, 8))),
        "keep": touch_ends((jax.random.randint(splits[1], (HIST, L), 0, 4) < 3).astype(jnp.int32), jax.random.fold_in(splits[1], 1), 0, 1),
        "lengths": draw_lengths(jax.random.fold_in(splits[6], 71), 0),
        "cotangent": scatter_about(splits[3], (HIST, L, D), 1.0, 6.0, ((0, 64), (1, 8))),
        "w_in": scatter_about(splits[4], (D, 4 * ATT), D ** -0.5, 0.25),
        "w_out": scatter_about(splits[5], (ATT, D), ATT ** -0.5, 0.25),
    }


EPSILON = 1e-06

def silu_slope(inputs_in):
    sigmoid_part = jax.nn.sigmoid(inputs_in)
    return sigmoid_part * (1.0 + inputs_in * (1.0 - sigmoid_part))

def one_history(events, keep, length, cotangent, w_in, w_out):
    count = events.shape[0]
    att_width = HEADS * DH
    positions = jnp.arange(count, dtype=jnp.int32)
    live_float = ((keep == 1) & (positions < length)).astype(jnp.float32)
    proj = jnp.dot(events, w_in, preferred_element_type=jnp.float32)
    act = jax.nn.silu(proj).astype(jnp.bfloat16)
    gate_u = act[:, 0:att_width].astype(jnp.float32)
    values = act[:, att_width:2 * att_width].astype(jnp.float32).reshape(count, HEADS, DH)
    queries = act[:, 2 * att_width:3 * att_width].astype(jnp.float32).reshape(count, HEADS, DH)
    keys = act[:, 3 * att_width:].astype(jnp.float32).reshape(count, HEADS, DH)
    score_scale = 1.0 / math.sqrt(DH)
    scores = jnp.einsum('qhd,khd->hqk', queries, keys) * score_scale
    allowed = (positions[:, None] >= positions[None, :]).astype(jnp.float32) * live_float[:, None] * live_float[None, :]
    attn = (jax.nn.silu(scores) * allowed[None]).astype(jnp.bfloat16).astype(jnp.float32)
    attended = jnp.einsum('hqk,khd->qhd', attn, values).reshape(count, att_width)
    centre = lax.optimization_barrier(jnp.mean(attended, axis=1, keepdims=True))
    centered = attended - centre
    inverse = lax.rsqrt(lax.optimization_barrier(jnp.mean(centered * centered, axis=1, keepdims=True)) + EPSILON)
    normed = centered * inverse
    gated = (normed * gate_u).astype(jnp.bfloat16)
    output = jnp.dot(gated, w_out, preferred_element_type=jnp.float32).astype(jnp.bfloat16)
    grad_gated = jnp.dot(cotangent, w_out.T, preferred_element_type=jnp.float32)
    grad_normed = grad_gated * gate_u
    grad_u = grad_gated * normed
    grad_attended = (grad_normed - lax.optimization_barrier(jnp.mean(grad_normed, axis=1, keepdims=True)) - normed * lax.optimization_barrier(jnp.mean(grad_normed * normed, axis=1, keepdims=True))) * inverse * live_float[:, None]
    grad_attended = grad_attended.astype(jnp.bfloat16).astype(jnp.float32).reshape(count, HEADS, DH)
    grad_v = jnp.einsum('hqk,qhd->khd', attn, grad_attended)
    grad_weights = jnp.einsum('qhd,khd->hqk', grad_attended, values)
    grad_scores = (grad_weights * silu_slope(scores) * allowed[None] * score_scale).astype(jnp.bfloat16).astype(jnp.float32)
    grad_q = jnp.einsum('hqk,khd->qhd', grad_scores, keys)
    grad_k = jnp.einsum('hqk,qhd->khd', grad_scores, queries)
    grad_act = jnp.concatenate([grad_u, grad_v.reshape(count, att_width), grad_q.reshape(count, att_width), grad_k.reshape(count, att_width)], axis=1)
    grad_proj = (grad_act * silu_slope(proj)).astype(jnp.bfloat16)
    grad_events = jnp.dot(grad_proj, w_in.T, preferred_element_type=jnp.float32).astype(jnp.bfloat16)
    gram = jnp.dot(gated.T, cotangent, preferred_element_type=jnp.float32)
    return (output, grad_events, gram)

def reference(events, keep, lengths, cotangent, w_in, w_out):

    def single(items):
        return one_history(items[0], items[1], items[2], items[3], w_in, w_out)
    output, grad_events, grams = lax.map(single, (events, keep, lengths, cotangent))
    grad_w_out = lax.optimization_barrier(jnp.sum(grams, axis=0)) * (1.0 / math.sqrt(TOKENS))
    return (output, grad_events, grad_w_out)
```

```python
import functools
import math

import jax
import jax.numpy as jnp
from jax import lax
from jax.experimental import pallas as pl
from jax.experimental.pallas import tpu as pltpu
from jax.sharding import PartitionSpec as P

HEADS = 4
DH = 128
WIDTH = HEADS * DH
X_CHIPS = 4
EPSILON = 1e-06
MESH = pl.DeviceIdType.MESH
F32 = jnp.float32
BF16 = jnp.bfloat16
U_COL, V_COL, Q_COL, K_COL = 0, WIDTH, 2 * WIDTH, 3 * WIDTH


def silu_parts(v):
    s = 0.5 * jnp.tanh(0.5 * v) + 0.5
    a = v * s
    return a, s + a * (1.0 - s)


def mul(a, b):
    return jnp.dot(a, b, preferred_element_type=F32)


def mul_t(a, b):
    return lax.dot_general(a, b, (((1,), (1,)), ((), ())), preferred_element_type=F32)


def kernel(
    Z, X, Y,
    events, keep, lengths, cotangent, w_in, w_out,
    out, grad_events, grad_w_out,
    e_all, act_all, do_all, cot_all, w_in_v, w_out_v, slope_v, gg_v, gu_v, att_v, dq_v, dk_v, dv_v, ge_v,
    g_v, p_v, out_v, gev_v, gt_send, gt_all, z_send, z_recv, c_recv, gram_v,
    local_sem, e_ssem, e_rsem, d_ssem, d_rsem, cot_ssem, cot_rsem, gt_ssem, gt_rsem, z_ssem, z_rsem, c_ssem, c_rsem,
):
    R = events.shape[0]
    D = events.shape[1]
    PAIR = 2 * R
    S = 2 * X
    ZH = Z // 2
    RD = D // (Z * X)
    scale = 1.0 / math.sqrt(DH)
    dp, ctx = lax.axis_index("dp"), lax.axis_index("ctx")
    z, x = dp // X, dp % X
    y, core = ctx // 2, ctx % 2
    other = 1 - core
    sib = y * 2 + other
    mine = x * 2 + core

    def block(b):
        return pl.ds(pl.multiple_of(b * R, R), R)

    def pair(c):
        return pl.ds(pl.multiple_of(c * PAIR, PAIR), PAIR)

    rows = block(ctx)

    ev_copy = pltpu.make_async_copy(events, e_all.at[rows], local_sem.at[0])
    ev_copy.start()
    cot_copy = pltpu.make_async_copy(cotangent, cot_all.at[block(mine)], local_sem.at[1])
    cot_copy.start()
    w_copies = []
    for g in range(4):
        cols = pl.ds(g * WIDTH, WIDTH)
        w_copies.append(pltpu.make_async_copy(w_in.at[:, cols], w_in_v.at[:, cols], local_sem.at[2 + g]))
    for copy in w_copies:
        copy.start()
    wo_copy = pltpu.make_async_copy(w_out, w_out_v, local_sem.at[6])
    wo_copy.start()

    barrier = pltpu.get_barrier_semaphore()

    def greet(dp_to, ctx_to):
        pl.semaphore_signal(barrier, inc=1, device_id=(dp_to, ctx_to), device_id_type=MESH)

    def greet_ctx(k, _):
        greet(dp, (ctx + k) % (2 * Y))
        return _

    def greet_x(k, _):
        greet(z * X + (x + k) % X, ctx)
        greet(z * X + (x + k) % X, sib)
        return _

    def greet_z(k, _):
        greet(((z + k) % Z) * X + x, ctx)
        return _

    lax.fori_loop(1, 2 * Y, greet_ctx, 0)
    lax.fori_loop(1, X, greet_x, 0)
    lax.fori_loop(1, Z, greet_z, 0)

    ev_copy.wait()
    lane = lax.broadcasted_iota(jnp.int32, (1, R), 1)
    live_row = jnp.where((keep[...] == 1) & (ctx * R + lane < lengths[0]), 1.0, 0.0)
    eye = lax.broadcasted_iota(jnp.int32, (R, R), 0) == lax.broadcasted_iota(jnp.int32, (R, R), 1)
    live = jnp.sum(jnp.where(eye, live_row, 0.0), axis=1, keepdims=True)
    e_all[rows, :] = (e_all[rows, :].astype(F32) * live).astype(BF16)
    pl.semaphore_wait(barrier, (2 * Y - 1) + 2 * (X - 1) + (Z - 1))

    def remote(buf, b, ssem, rsem, ctx_to):
        return pltpu.make_async_remote_copy(
            src_ref=buf.at[block(b)], dst_ref=buf.at[block(b)], send_sem=ssem, recv_sem=rsem.at[b],
            device_id=(dp, ctx_to), device_id_type=MESH,
        )

    def e_out(d):
        return remote(e_all, ctx, e_ssem.at[d], e_rsem, ((y + d) % Y) * 2 + core)

    e_order = [1, 3, 2] if Y == 4 else list(range(1, Y))
    remote(e_all, ctx, e_ssem.at[0], e_rsem, sib).start()
    for d in e_order:
        e_out(d).start()

    def hand_over(buf, c, ssem, rsem):
        return remote(buf, c * 2 + core, ssem.at[Y + c], rsem, sib)

    def arrived(buf, b, ssem, rsem):
        remote(buf, b, ssem.at[0], rsem, sib).wait_recv()

    cot_copy.wait()

    def cot_out(k):
        s = (mine + k) % S
        return pltpu.make_async_remote_copy(
            src_ref=cot_all.at[block(mine)], dst_ref=cot_all.at[block(mine)],
            send_sem=cot_ssem.at[k], recv_sem=cot_rsem.at[mine],
            device_id=(z * X + s // 2, y * 2 + s % 2), device_id_type=MESH,
        )

    def cot_in(k):
        s = (mine + k) % S
        return pltpu.make_async_remote_copy(
            src_ref=cot_all.at[block(s)], dst_ref=cot_all.at[block(s)],
            send_sem=cot_ssem.at[k], recv_sem=cot_rsem.at[s],
            device_id=(z * X + s // 2, y * 2 + s % 2), device_id_type=MESH,
        )

    def each(low, high, body):
        def step(k, _):
            body(k)
            return _
        lax.fori_loop(low, high, step, 0)

    each(1, S, lambda k: cot_out(k).start())

    own = e_all[rows, :]
    for g in range(4):
        w_copies[g].wait()
        for half in range(2):
            cols = pl.ds(g * WIDTH + half * 256, 256)
            a, slope = silu_parts(mul(own, w_in_v[:, cols]))
            act_all[rows, cols] = a.astype(BF16)
            slope_v[:, cols] = slope
    wo_copy.wait()
    gg_v[...] = mul_t(cot_all[block(mine), :], w_out_v[...])

    def project(row_slice, first, count, stride):
        def body(n):
            off = pl.multiple_of(first + (n % 2) * 256 + (n // 2) * stride, 256)
            a, _ = silu_parts(mul(e_all[row_slice, :], w_in_v[:, pl.ds(off, 256)]))
            act_all[row_slice, pl.ds(off, 256)] = a.astype(BF16)
        each(0, count, body)

    def head(base, h):
        return pl.ds(base + h * DH, DH)

    def allowed(query_major):
        first = lax.broadcasted_iota(jnp.int32, (R, PAIR), 0) + core * R
        second = lax.broadcasted_iota(jnp.int32, (R, PAIR), 1)
        return first >= second if query_major else second >= first

    def forward(c, masked):
        for h in range(HEADS):
            s = mul_t(act_all[rows, head(Q_COL, h)], act_all[pair(c), head(K_COL, h)]) * scale
            a, slope = silu_parts(s)
            slope = slope * scale
            if masked:
                ok = allowed(True)
                a, slope = jnp.where(ok, a, 0.0), jnp.where(ok, slope, 0.0)
            g_v[c, h] = slope
            part = mul(a.astype(BF16), act_all[pair(c), head(V_COL, h)])
            if masked:
                att_v[:, head(0, h)] = part
            else:
                att_v[:, head(0, h)] += part

    def prepare(c, masked):
        for h in range(HEADS):
            s = mul_t(act_all[rows, head(K_COL, h)], act_all[pair(c), head(Q_COL, h)]) * scale
            a, slope = silu_parts(s)
            slope = slope * scale
            if masked:
                ok = allowed(False)
                a, slope = jnp.where(ok, a, 0.0), jnp.where(ok, slope, 0.0)
            g_v[c + 1, h] = slope
            p_v[c, h] = a.astype(BF16)

    def take_e(c):
        arrived(e_all, c * 2 + core, e_ssem, e_rsem)
        hand_over(e_all, c, e_ssem, e_rsem).start()

    arrived(e_all, sib, e_ssem, e_rsem)
    project(block(sib), V_COL, 6, 512)
    for d in e_order[:2]:
        take_e((y + d) % Y)
    forward(y, True)
    prepare(y, True)

    def chip_step(t):
        c = (y + 1 + (2 * t) % (Y - 1 if Y > 2 else 1)) % Y
        arrived(e_all, c * 2 + other, e_ssem, e_rsem)

        @pl.when(c < y)
        def _():
            project(pair(c), V_COL, 4, 1024)
            forward(c, False)

        @pl.when(c > y)
        def _():
            project(pair(c), Q_COL, 2, 512)
            prepare(c, False)

        if Y == 4:
            @pl.when(t == 0)
            def _():
                take_e((y + 2) % Y)

    each(0, Y - 1, chip_step)

    att = att_v[...]
    cen = att - jnp.mean(att, axis=1, keepdims=True)
    inv = lax.rsqrt(jnp.mean(cen * cen, axis=1, keepdims=True) + EPSILON)
    normed = cen * inv
    gate = act_all[rows, pl.ds(U_COL, WIDTH)].astype(F32)
    gated = normed * gate
    gg = gg_v[...]
    gn = gg * gate
    grad_att = (
        gn - jnp.mean(gn, axis=1, keepdims=True) - normed * jnp.mean(gn * normed, axis=1, keepdims=True)
    ) * inv * live
    do_all[rows, :] = grad_att.astype(BF16)

    def d_out(c):
        return remote(do_all, ctx, d_ssem.at[c], d_rsem, c * 2 + core)

    d_sib = remote(do_all, ctx, d_ssem.at[y], d_rsem, sib)
    d_sib.start()
    each(0, y, lambda c: d_out(c).start())

    turned = jnp.transpose(gated).reshape(Z, X, RD, R)
    for to in range(X):
        gt_send[to] = turned[:, to].reshape(Z * RD, R).astype(BF16)

    def gt_part(s):
        return gt_all.at[:, block(s)]

    def gt_piece(s):
        return pl.ds(pl.multiple_of((s % 2) * (ZH * RD), ZH * RD), ZH * RD)

    def gt_out(k):
        s = (mine + k) % S
        return pltpu.make_async_remote_copy(
            src_ref=gt_send.at[s // 2, gt_piece(s)], dst_ref=gt_part(mine),
            send_sem=gt_ssem.at[k], recv_sem=gt_rsem.at[mine],
            device_id=(z * X + s // 2, y * 2 + s % 2), device_id_type=MESH,
        )

    def gt_in(k):
        s = (mine + k) % S
        return pltpu.make_async_remote_copy(
            src_ref=gt_send.at[s // 2, gt_piece(s)], dst_ref=gt_part(s),
            send_sem=gt_ssem.at[k], recv_sem=gt_rsem.at[s],
            device_id=(z * X + s // 2, y * 2 + s % 2), device_id_type=MESH,
        )

    each(1, S, lambda k: gt_out(k).start())
    gt_all[:, block(mine)] = gt_send[x, gt_piece(mine), :]
    out_v[...] = mul(gated.astype(BF16), w_out_v[...]).astype(BF16)
    out_copy = pltpu.make_async_copy(out_v, out, local_sem.at[7])
    out_copy.start()
    gu_v[...] = gg * normed

    dq_v[...] = jnp.zeros_like(dq_v)
    dk_v[...] = jnp.zeros_like(dk_v)
    dv_v[...] = jnp.zeros_like(dv_v)

    def query_step(c):
        for h in range(HEADS):
            gw = mul_t(do_all[rows, head(0, h)], act_all[pair(c), head(V_COL, h)])
            gs = (gw * g_v[c, h]).astype(BF16)
            dq_v[:, head(0, h)] += mul(gs, act_all[pair(c), head(K_COL, h)])

    each(0, y + 1, query_step)

    each(1, S, lambda k: cot_in(k).wait_recv())
    each(1, S, lambda k: gt_in(k).wait_recv())
    gram = mul(gt_all[...], cot_all[...]).reshape(ZH, RD, D)
    z_send[...] = jnp.concatenate([gram[:, :, : D // 2], gram[:, :, D // 2 :]], axis=1).astype(BF16)

    def z_out(k):
        return pltpu.make_async_remote_copy(
            src_ref=z_send.at[k], dst_ref=z_recv.at[z], send_sem=z_ssem.at[k], recv_sem=z_rsem.at[z],
            device_id=((core * ZH + k) * X + x, ctx), device_id_type=MESH,
        )

    def z_in(k):
        return pltpu.make_async_remote_copy(
            src_ref=z_send.at[0], dst_ref=z_recv.at[k], send_sem=z_ssem.at[0], recv_sem=z_rsem.at[k],
            device_id=(k * X + x, ctx), device_id_type=MESH,
        )

    def z_start(k):
        @pl.when(core * ZH + k != z)
        def _():
            z_out(k).start()

    each(0, ZH, z_start)

    def back(grad, base):
        cols = pl.ds(base, WIDTH)
        return mul_t((grad * slope_v[:, cols]).astype(BF16), w_in_v[:, cols])

    ge_v[...] = back(gu_v[...], U_COL) + back(dq_v[...], Q_COL)

    def key_step(c):
        for h in range(HEADS):
            do_h = do_all[pair(c), head(0, h)]
            gw = mul_t(act_all[rows, head(V_COL, h)], do_h)
            gs = (gw * g_v[c + 1, h]).astype(BF16)
            dv_v[:, head(0, h)] += mul(p_v[c, h], do_h)
            dk_v[:, head(0, h)] += mul(gs, act_all[pair(c), head(Q_COL, h)])

    arrived(do_all, sib, d_ssem, d_rsem)
    key_step(y)

    def later_chip(c):
        arrived(do_all, c * 2 + core, d_ssem, d_rsem)
        hand_over(do_all, c, d_ssem, d_rsem).start()
        arrived(do_all, c * 2 + other, d_ssem, d_rsem)
        key_step(c)

    each(y + 1, Y, later_chip)

    gev_v[...] = (ge_v[...] + back(dv_v[...], V_COL) + back(dk_v[...], K_COL)).astype(BF16)
    gev_copy = pltpu.make_async_copy(gev_v, grad_events, local_sem.at[8])
    gev_copy.start()

    holder = z // ZH

    def c_out(k):
        return pltpu.make_async_remote_copy(
            src_ref=c_recv.at[y], dst_ref=c_recv.at[y], send_sem=c_ssem.at[k], recv_sem=c_rsem.at[y],
            device_id=(dp, (ctx + k) % (2 * Y)), device_id_type=MESH,
        )

    def c_in(k):
        return pltpu.make_async_remote_copy(
            src_ref=c_recv.at[k], dst_ref=c_recv.at[k], send_sem=c_ssem.at[0], recv_sem=c_rsem.at[k],
            device_id=(dp, sib), device_id_type=MESH,
        )

    @pl.when(core == holder)
    def _():
        z_recv[z] = z_send[z % ZH]

        def wait_z(k):
            @pl.when(k != z)
            def _():
                z_in(k).wait_recv()

        each(0, Z, wait_z)
        total = jnp.sum(z_recv[...].astype(F32), axis=0)
        c_recv[y] = jnp.concatenate([total[:RD], total[RD:]], axis=1)
        each(1, 2 * Y, lambda k: c_out(k).start())

    def wait_c(k):
        @pl.when(k * 2 + holder != ctx)
        def _():
            c_in(k).wait_recv()

    each(0, Y, wait_c)
    tokens = R * 2 * Y * Z * X
    gram_v[...] = jnp.sum(c_recv[...], axis=0) * (1.0 / math.sqrt(tokens))
    gram_copy = pltpu.make_async_copy(gram_v, grad_w_out, local_sem.at[9])
    gram_copy.start()

    remote(e_all, ctx, e_ssem.at[0], e_rsem, sib).wait_send()

    def e_done(d):
        e_out(d).wait_send()
        hand_over(e_all, (y + d) % Y, e_ssem, e_rsem).wait_send()

    each(1, Y, e_done)
    each(1, S, lambda k: cot_out(k).wait_send())
    d_sib.wait_send()
    each(0, y, lambda c: d_out(c).wait_send())
    each(y + 1, Y, lambda c: hand_over(do_all, c, d_ssem, d_rsem).wait_send())
    each(1, S, lambda k: gt_out(k).wait_send())

    def z_done(k):
        @pl.when(core * ZH + k != z)
        def _():
            z_out(k).wait_send()

    each(0, ZH, z_done)

    @pl.when(core == holder)
    def _():
        each(1, 2 * Y, lambda k: c_out(k).wait_send())

    out_copy.wait()
    gev_copy.wait()
    gram_copy.wait()


def build(mesh, X):
    Z, Y = mesh.shape["dp"] // X, mesh.shape["ctx"] // 2

    def per_device(events, keep, lengths, cotangent, w_in, w_out):
        R, D = events.shape[1:]
        L = R * 2 * Y
        S = 2 * X
        ZH, RD = Z // 2, D // (Z * X)
        anywhere = pl.BlockSpec(memory_space=pl.ANY)
        dma = pltpu.SemaphoreType.DMA
        output, grad_events, grad_w_out = pl.pallas_call(
            functools.partial(kernel, Z, X, Y),
            out_shape=(
                jax.ShapeDtypeStruct((R, D), BF16),
                jax.ShapeDtypeStruct((R, D), BF16),
                jax.ShapeDtypeStruct((RD, D), F32),
            ),
            in_specs=[
                anywhere,
                pl.BlockSpec(memory_space=pltpu.VMEM),
                pl.BlockSpec(memory_space=pltpu.SMEM),
                anywhere, anywhere, anywhere,
            ],
            out_specs=(anywhere, anywhere, anywhere),
            scratch_shapes=[
                pltpu.VMEM((L, D), BF16),
                pltpu.VMEM((L, 4 * WIDTH), BF16),
                pltpu.VMEM((L, WIDTH), BF16),
                pltpu.VMEM((S * R, D), BF16),
                pltpu.VMEM((D, 4 * WIDTH), BF16),
                pltpu.VMEM((WIDTH, D), BF16),
                pltpu.VMEM((R, 4 * WIDTH), F32),
                pltpu.VMEM((R, WIDTH), F32),
                pltpu.VMEM((R, WIDTH), F32),
                pltpu.VMEM((R, WIDTH), F32),
                pltpu.VMEM((R, WIDTH), F32),
                pltpu.VMEM((R, WIDTH), F32),
                pltpu.VMEM((R, WIDTH), F32),
                pltpu.VMEM((R, D), F32),
                pltpu.VMEM((Y + 1, HEADS, R, 2 * R), F32),
                pltpu.VMEM((Y, HEADS, R, 2 * R), BF16),
                pltpu.VMEM((R, D), BF16),
                pltpu.VMEM((R, D), BF16),
                pltpu.VMEM((X, Z * RD, R), BF16),
                pltpu.VMEM((ZH * RD, S * R), BF16),
                pltpu.VMEM((ZH, 2 * RD, D // 2), BF16),
                pltpu.VMEM((Z, 2 * RD, D // 2), BF16),
                pltpu.VMEM((Y, RD, D), F32),
                pltpu.VMEM((RD, D), F32),
                dma((10,)),
                dma((2 * Y,)), dma((2 * Y,)),
                dma((2 * Y,)), dma((2 * Y,)),
                dma((S,)), dma((S,)),
                dma((S,)), dma((S,)),
                dma((ZH,)), dma((Z,)),
                dma((2 * Y,)), dma((Y,)),
            ],
            compiler_params=pltpu.CompilerParams(
                collective_id=0, has_side_effects=True, vmem_limit_bytes=48 * 1024 * 1024
            ),
            name="layer",
        )(events[0], keep, lengths, cotangent[0], w_in, w_out)
        return (output[None], grad_events[None], grad_w_out)

    return jax.shard_map(
        per_device,
        mesh=mesh,
        in_specs=(P("dp", "ctx", None), P("dp", "ctx"), P("dp"), P("dp", "ctx", None), P(), P()),
        out_specs=(P("dp", "ctx", None), P("dp", "ctx", None), P("dp", None)),
        check_vma=False,
    )


def solution(mesh):
    return build(mesh, X_CHIPS)
```

```python
import functools
import math

import jax
import jax.numpy as jnp
from jax import lax
from jax.experimental import pallas as pl
from jax.experimental.pallas import tpu as pltpu
from jax.sharding import PartitionSpec as P

HEADS = 4
DH = 128
WIDTH = HEADS * DH
X_CHIPS = 4
EPSILON = 1e-06
MESH = pl.DeviceIdType.MESH
F32 = jnp.float32
BF16 = jnp.bfloat16
U_COL, V_COL, Q_COL, K_COL = 0, WIDTH, 2 * WIDTH, 3 * WIDTH


def silu_parts(v):
    s = 0.5 * jnp.tanh(0.5 * v) + 0.5
    a = v * s
    return a, s + a * (1.0 - s)


def mul(a, b):
    return jnp.dot(a, b, preferred_element_type=F32)


def mul_t(a, b):
    return lax.dot_general(a, b, (((1,), (1,)), ((), ())), preferred_element_type=F32)


def kernel(
    Z, X, Y,
    events, keep, lengths, cotangent, w_in, w_out,
    out, grad_events, grad_w_out,
    keep_v, lengths_s, e_all, act_all, do_all, cot_all, w_in_v, w_out_v, slope_v, gg_v, gu_v, att_v, dq_v, dk_v, dv_v, ge_v,
    g_v, p_v, out_v, gev_v, gt_send, gt_all, z_send, z_recv, c_recv, gram_v,
    local_sem, e_ssem, e_rsem, d_ssem, d_rsem, cot_ssem, cot_rsem, gt_ssem, gt_rsem, z_ssem, z_rsem, c_ssem, c_rsem,
):
    R = events.shape[0]
    D = events.shape[1]
    PAIR = 2 * R
    S = 2 * X
    ZH = Z // 2
    RD = D // (Z * X)
    scale = 1.0 / math.sqrt(DH)
    dp, ctx = lax.axis_index("dp"), lax.axis_index("ctx")
    z, x = dp // X, dp % X
    y, core = ctx // 2, ctx % 2
    other = 1 - core
    sib = y * 2 + other
    mine = x * 2 + core

    def block(b):
        return pl.ds(pl.multiple_of(b * R, R), R)

    def pair(c):
        return pl.ds(pl.multiple_of(c * PAIR, PAIR), PAIR)

    rows = block(ctx)

    ev_copy = pltpu.make_async_copy(events, e_all.at[rows], local_sem.at[0])
    ev_copy.start()
    keep_copy = pltpu.make_async_copy(keep, keep_v, local_sem.at[10])
    keep_copy.start()
    lengths_copy = pltpu.make_async_copy(lengths, lengths_s, local_sem.at[11])
    lengths_copy.start()
    cot_copy = pltpu.make_async_copy(cotangent, cot_all.at[block(mine)], local_sem.at[1])
    cot_copy.start()
    w_copies = []
    for g in range(4):
        cols = pl.ds(g * WIDTH, WIDTH)
        w_copies.append(pltpu.make_async_copy(w_in.at[:, cols], w_in_v.at[:, cols], local_sem.at[2 + g]))
    for copy in w_copies:
        copy.start()
    wo_copy = pltpu.make_async_copy(w_out, w_out_v, local_sem.at[6])
    wo_copy.start()

    barrier = pltpu.get_barrier_semaphore()

    def greet(dp_to, ctx_to):
        pl.semaphore_signal(barrier, inc=1, device_id=(dp_to, ctx_to), device_id_type=MESH)

    def greet_ctx(k, _):
        greet(dp, (ctx + k) % (2 * Y))
        return _

    def greet_x(k, _):
        greet(z * X + (x + k) % X, ctx)
        greet(z * X + (x + k) % X, sib)
        return _

    def greet_z(k, _):
        greet(((z + k) % Z) * X + x, ctx)
        return _

    lax.fori_loop(1, 2 * Y, greet_ctx, 0)
    lax.fori_loop(1, X, greet_x, 0)
    lax.fori_loop(1, Z, greet_z, 0)

    ev_copy.wait()
    keep_copy.wait()
    lengths_copy.wait()
    lane = lax.broadcasted_iota(jnp.int32, (1, R), 1)
    live_row = jnp.where((keep_v[...] == 1) & (ctx * R + lane < lengths_s[0]), 1.0, 0.0)
    eye = lax.broadcasted_iota(jnp.int32, (R, R), 0) == lax.broadcasted_iota(jnp.int32, (R, R), 1)
    live = jnp.sum(jnp.where(eye, live_row, 0.0), axis=1, keepdims=True)
    e_all[rows, :] = (e_all[rows, :].astype(F32) * live).astype(BF16)
    pl.semaphore_wait(barrier, (2 * Y - 1) + 2 * (X - 1) + (Z - 1))

    def remote(buf, b, ssem, rsem, ctx_to):
        return pltpu.make_async_remote_copy(
            src_ref=buf.at[block(b)], dst_ref=buf.at[block(b)], send_sem=ssem, recv_sem=rsem.at[b],
            device_id=(dp, ctx_to), device_id_type=MESH,
        )

    def e_out(d):
        return remote(e_all, ctx, e_ssem.at[d], e_rsem, ((y + d) % Y) * 2 + core)

    e_order = [1, 3, 2] if Y == 4 else list(range(1, Y))
    remote(e_all, ctx, e_ssem.at[0], e_rsem, sib).start()
    for d in e_order:
        e_out(d).start()

    def hand_over(buf, c, ssem, rsem):
        return remote(buf, c * 2 + core, ssem.at[Y + c], rsem, sib)

    def arrived(buf, b, ssem, rsem):
        remote(buf, b, ssem.at[0], rsem, sib).wait_recv()

    cot_copy.wait()

    def cot_out(k):
        s = (mine + k) % S
        return pltpu.make_async_remote_copy(
            src_ref=cot_all.at[block(mine)], dst_ref=cot_all.at[block(mine)],
            send_sem=cot_ssem.at[k], recv_sem=cot_rsem.at[mine],
            device_id=(z * X + s // 2, y * 2 + s % 2), device_id_type=MESH,
        )

    def cot_in(k):
        s = (mine + k) % S
        return pltpu.make_async_remote_copy(
            src_ref=cot_all.at[block(s)], dst_ref=cot_all.at[block(s)],
            send_sem=cot_ssem.at[k], recv_sem=cot_rsem.at[s],
            device_id=(z * X + s // 2, y * 2 + s % 2), device_id_type=MESH,
        )

    def each(low, high, body):
        def step(k, _):
            body(k)
            return _
        lax.fori_loop(low, high, step, 0)

    each(1, S, lambda k: cot_out(k).start())

    own = e_all[rows, :]
    for g in range(4):
        w_copies[g].wait()
        for half in range(2):
            cols = pl.ds(g * WIDTH + half * 256, 256)
            a, slope = silu_parts(mul(own, w_in_v[:, cols]))
            act_all[rows, cols] = a.astype(BF16)
            slope_v[:, cols] = slope
    wo_copy.wait()
    gg_v[...] = mul_t(cot_all[block(mine), :], w_out_v[...])

    def project(row_slice, first, count, stride):
        def body(n):
            off = pl.multiple_of(first + (n % 2) * 256 + (n // 2) * stride, 256)
            a, _ = silu_parts(mul(e_all[row_slice, :], w_in_v[:, pl.ds(off, 256)]))
            act_all[row_slice, pl.ds(off, 256)] = a.astype(BF16)
        each(0, count, body)

    def head(base, h):
        return pl.ds(base + h * DH, DH)

    def allowed(query_major):
        first = lax.broadcasted_iota(jnp.int32, (R, PAIR), 0) + core * R
        second = lax.broadcasted_iota(jnp.int32, (R, PAIR), 1)
        return first >= second if query_major else second >= first

    def forward(c, masked):
        for h in range(HEADS):
            s = mul_t(act_all[rows, head(Q_COL, h)], act_all[pair(c), head(K_COL, h)]) * scale
            a, slope = silu_parts(s)
            slope = slope * scale
            if masked:
                ok = allowed(True)
                a, slope = jnp.where(ok, a, 0.0), jnp.where(ok, slope, 0.0)
            g_v[c, h] = slope
            part = mul(a.astype(BF16), act_all[pair(c), head(V_COL, h)])
            if masked:
                att_v[:, head(0, h)] = part
            else:
                att_v[:, head(0, h)] += part

    def prepare(c, masked):
        for h in range(HEADS):
            s = mul_t(act_all[rows, head(K_COL, h)], act_all[pair(c), head(Q_COL, h)]) * scale
            a, slope = silu_parts(s)
            slope = slope * scale
            if masked:
                ok = allowed(False)
                a, slope = jnp.where(ok, a, 0.0), jnp.where(ok, slope, 0.0)
            g_v[c + 1, h] = slope
            p_v[c, h] = a.astype(BF16)

    def take_e(c):
        arrived(e_all, c * 2 + core, e_ssem, e_rsem)
        hand_over(e_all, c, e_ssem, e_rsem).start()

    arrived(e_all, sib, e_ssem, e_rsem)
    project(block(sib), V_COL, 6, 512)
    for d in e_order[:2]:
        take_e((y + d) % Y)
    forward(y, True)
    prepare(y, True)

    def chip_step(t):
        c = (y + 1 + (2 * t) % (Y - 1 if Y > 2 else 1)) % Y
        arrived(e_all, c * 2 + other, e_ssem, e_rsem)

        @pl.when(c < y)
        def _():
            project(pair(c), V_COL, 4, 1024)
            forward(c, False)

        @pl.when(c > y)
        def _():
            project(pair(c), Q_COL, 2, 512)
            prepare(c, False)

        if Y == 4:
            @pl.when(t == 0)
            def _():
                take_e((y + 2) % Y)

    each(0, Y - 1, chip_step)

    att = att_v[...]
    cen = att - jnp.mean(att, axis=1, keepdims=True)
    inv = lax.rsqrt(jnp.mean(cen * cen, axis=1, keepdims=True) + EPSILON)
    normed = cen * inv
    gate = act_all[rows, pl.ds(U_COL, WIDTH)].astype(F32)
    gated = normed * gate
    gg = gg_v[...]
    gn = gg * gate
    grad_att = (
        gn - jnp.mean(gn, axis=1, keepdims=True) - normed * jnp.mean(gn * normed, axis=1, keepdims=True)
    ) * inv * live
    do_all[rows, :] = grad_att.astype(BF16)

    def d_out(c):
        return remote(do_all, ctx, d_ssem.at[c], d_rsem, c * 2 + core)

    d_sib = remote(do_all, ctx, d_ssem.at[y], d_rsem, sib)
    d_sib.start()
    each(0, y, lambda c: d_out(c).start())

    turned = jnp.transpose(gated).reshape(Z, X, RD, R)
    for to in range(X):
        gt_send[to] = turned[:, to].reshape(Z * RD, R).astype(BF16)

    def gt_part(s):
        return gt_all.at[:, block(s)]

    def gt_piece(s):
        return pl.ds(pl.multiple_of((s % 2) * (ZH * RD), ZH * RD), ZH * RD)

    def gt_out(k):
        s = (mine + k) % S
        return pltpu.make_async_remote_copy(
            src_ref=gt_send.at[s // 2, gt_piece(s)], dst_ref=gt_part(mine),
            send_sem=gt_ssem.at[k], recv_sem=gt_rsem.at[mine],
            device_id=(z * X + s // 2, y * 2 + s % 2), device_id_type=MESH,
        )

    def gt_in(k):
        s = (mine + k) % S
        return pltpu.make_async_remote_copy(
            src_ref=gt_send.at[s // 2, gt_piece(s)], dst_ref=gt_part(s),
            send_sem=gt_ssem.at[k], recv_sem=gt_rsem.at[s],
            device_id=(z * X + s // 2, y * 2 + s % 2), device_id_type=MESH,
        )

    each(1, S, lambda k: gt_out(k).start())
    gt_all[:, block(mine)] = gt_send[x, gt_piece(mine), :]
    out_v[...] = mul(gated.astype(BF16), w_out_v[...]).astype(BF16)
    out_copy = pltpu.make_async_copy(out_v, out, local_sem.at[7])
    out_copy.start()
    gu_v[...] = gg * normed

    dq_v[...] = jnp.zeros_like(dq_v)
    dk_v[...] = jnp.zeros_like(dk_v)
    dv_v[...] = jnp.zeros_like(dv_v)

    def query_step(c):
        for h in range(HEADS):
            gw = mul_t(do_all[rows, head(0, h)], act_all[pair(c), head(V_COL, h)])
            gs = (gw * g_v[c, h]).astype(BF16)
            dq_v[:, head(0, h)] += mul(gs, act_all[pair(c), head(K_COL, h)])

    each(0, y + 1, query_step)

    each(1, S, lambda k: cot_in(k).wait_recv())
    each(1, S, lambda k: gt_in(k).wait_recv())
    gram = mul(gt_all[...], cot_all[...]).reshape(ZH, RD, D)
    z_send[...] = jnp.concatenate([gram[:, :, : D // 2], gram[:, :, D // 2 :]], axis=1).astype(BF16)

    def z_out(k):
        return pltpu.make_async_remote_copy(
            src_ref=z_send.at[k], dst_ref=z_recv.at[z], send_sem=z_ssem.at[k], recv_sem=z_rsem.at[z],
            device_id=((core * ZH + k) * X + x, ctx), device_id_type=MESH,
        )

    def z_in(k):
        return pltpu.make_async_remote_copy(
            src_ref=z_send.at[0], dst_ref=z_recv.at[k], send_sem=z_ssem.at[0], recv_sem=z_rsem.at[k],
            device_id=(k * X + x, ctx), device_id_type=MESH,
        )

    def z_start(k):
        @pl.when(core * ZH + k != z)
        def _():
            z_out(k).start()

    each(0, ZH, z_start)

    def back(grad, base):
        cols = pl.ds(base, WIDTH)
        return mul_t((grad * slope_v[:, cols]).astype(BF16), w_in_v[:, cols])

    ge_v[...] = back(gu_v[...], U_COL) + back(dq_v[...], Q_COL)

    def key_step(c):
        for h in range(HEADS):
            do_h = do_all[pair(c), head(0, h)]
            gw = mul_t(act_all[rows, head(V_COL, h)], do_h)
            gs = (gw * g_v[c + 1, h]).astype(BF16)
            dv_v[:, head(0, h)] += mul(p_v[c, h], do_h)
            dk_v[:, head(0, h)] += mul(gs, act_all[pair(c), head(Q_COL, h)])

    arrived(do_all, sib, d_ssem, d_rsem)
    key_step(y)

    def later_chip(c):
        arrived(do_all, c * 2 + core, d_ssem, d_rsem)
        hand_over(do_all, c, d_ssem, d_rsem).start()
        arrived(do_all, c * 2 + other, d_ssem, d_rsem)
        key_step(c)

    each(y + 1, Y, later_chip)

    gev_v[...] = (ge_v[...] + back(dv_v[...], V_COL) + back(dk_v[...], K_COL)).astype(BF16)
    gev_copy = pltpu.make_async_copy(gev_v, grad_events, local_sem.at[8])
    gev_copy.start()

    holder = z // ZH

    def c_out(k):
        return pltpu.make_async_remote_copy(
            src_ref=c_recv.at[y], dst_ref=c_recv.at[y], send_sem=c_ssem.at[k], recv_sem=c_rsem.at[y],
            device_id=(dp, (ctx + k) % (2 * Y)), device_id_type=MESH,
        )

    def c_in(k):
        return pltpu.make_async_remote_copy(
            src_ref=c_recv.at[k], dst_ref=c_recv.at[k], send_sem=c_ssem.at[0], recv_sem=c_rsem.at[k],
            device_id=(dp, sib), device_id_type=MESH,
        )

    @pl.when(core == holder)
    def _():
        z_recv[z] = z_send[z % ZH]

        def wait_z(k):
            @pl.when(k != z)
            def _():
                z_in(k).wait_recv()

        each(0, Z, wait_z)
        total = jnp.sum(z_recv[...].astype(F32), axis=0)
        c_recv[y] = jnp.concatenate([total[:RD], total[RD:]], axis=1)
        each(1, 2 * Y, lambda k: c_out(k).start())

    def wait_c(k):
        @pl.when(k * 2 + holder != ctx)
        def _():
            c_in(k).wait_recv()

    each(0, Y, wait_c)
    tokens = R * 2 * Y * Z * X
    gram_v[...] = jnp.sum(c_recv[...], axis=0) * (1.0 / math.sqrt(tokens))
    gram_copy = pltpu.make_async_copy(gram_v, grad_w_out, local_sem.at[9])
    gram_copy.start()

    remote(e_all, ctx, e_ssem.at[0], e_rsem, sib).wait_send()

    def e_done(d):
        e_out(d).wait_send()
        hand_over(e_all, (y + d) % Y, e_ssem, e_rsem).wait_send()

    each(1, Y, e_done)
    each(1, S, lambda k: cot_out(k).wait_send())
    d_sib.wait_send()
    each(0, y, lambda c: d_out(c).wait_send())
    each(y + 1, Y, lambda c: hand_over(do_all, c, d_ssem, d_rsem).wait_send())
    each(1, S, lambda k: gt_out(k).wait_send())

    def z_done(k):
        @pl.when(core * ZH + k != z)
        def _():
            z_out(k).wait_send()

    each(0, ZH, z_done)

    @pl.when(core == holder)
    def _():
        each(1, 2 * Y, lambda k: c_out(k).wait_send())

    out_copy.wait()
    gev_copy.wait()
    gram_copy.wait()


def store(*refs):
    copies = [pltpu.make_async_copy(refs[n], refs[3 + n], refs[6].at[n]) for n in range(3)]
    for copy in copies:
        copy.start()
    for copy in copies:
        copy.wait()


def build(mesh, X):
    Z, Y = mesh.shape["dp"] // X, mesh.shape["ctx"] // 2

    def per_device(events, keep, lengths, cotangent, w_in, w_out):
        R, D = events.shape[1:]
        L = R * 2 * Y
        S = 2 * X
        ZH, RD = Z // 2, D // (Z * X)
        anywhere = pl.BlockSpec(memory_space=pl.ANY)
        hbm = pl.BlockSpec(memory_space=pltpu.HBM)
        dma = pltpu.SemaphoreType.DMA
        output, grad_events, grad_w_out = pl.pallas_call(
            functools.partial(kernel, Z, X, Y),
            out_shape=(
                jax.ShapeDtypeStruct((R, D), BF16),
                jax.ShapeDtypeStruct((R, D), BF16),
                jax.ShapeDtypeStruct((RD, D), F32),
            ),
            in_specs=[hbm] * 6,
            out_specs=(anywhere, anywhere, anywhere),
            scratch_shapes=[
                pltpu.VMEM((1, R), jnp.int32),
                pltpu.SMEM((1,), jnp.int32),
                pltpu.VMEM((L, D), BF16),
                pltpu.VMEM((L, 4 * WIDTH), BF16),
                pltpu.VMEM((L, WIDTH), BF16),
                pltpu.VMEM((S * R, D), BF16),
                pltpu.VMEM((D, 4 * WIDTH), BF16),
                pltpu.VMEM((WIDTH, D), BF16),
                pltpu.VMEM((R, 4 * WIDTH), F32),
                pltpu.VMEM((R, WIDTH), F32),
                pltpu.VMEM((R, WIDTH), F32),
                pltpu.VMEM((R, WIDTH), F32),
                pltpu.VMEM((R, WIDTH), F32),
                pltpu.VMEM((R, WIDTH), F32),
                pltpu.VMEM((R, WIDTH), F32),
                pltpu.VMEM((R, D), F32),
                pltpu.VMEM((Y + 1, HEADS, R, 2 * R), F32),
                pltpu.VMEM((Y, HEADS, R, 2 * R), BF16),
                pltpu.VMEM((R, D), BF16),
                pltpu.VMEM((R, D), BF16),
                pltpu.VMEM((X, Z * RD, R), BF16),
                pltpu.VMEM((ZH * RD, S * R), BF16),
                pltpu.VMEM((ZH, 2 * RD, D // 2), BF16),
                pltpu.VMEM((Z, 2 * RD, D // 2), BF16),
                pltpu.VMEM((Y, RD, D), F32),
                pltpu.VMEM((RD, D), F32),
                dma((12,)),
                dma((2 * Y,)), dma((2 * Y,)),
                dma((2 * Y,)), dma((2 * Y,)),
                dma((S,)), dma((S,)),
                dma((S,)), dma((S,)),
                dma((ZH,)), dma((Z,)),
                dma((2 * Y,)), dma((Y,)),
            ],
            compiler_params=pltpu.CompilerParams(
                collective_id=0, has_side_effects=True, vmem_limit_bytes=60 * 1024 * 1024
            ),
            name="layer",
        )(events[0], keep, lengths, cotangent[0], w_in, w_out)
        output, grad_events, grad_w_out = pl.pallas_call(
            store,
            out_shape=(
                jax.ShapeDtypeStruct((R, D), BF16),
                jax.ShapeDtypeStruct((R, D), BF16),
                jax.ShapeDtypeStruct((RD, D), F32),
            ),
            in_specs=[anywhere] * 3,
            out_specs=(hbm, hbm, hbm),
            scratch_shapes=[dma((3,))],
            compiler_params=pltpu.CompilerParams(vmem_limit_bytes=60 * 1024 * 1024),
            name="store",
        )(output, grad_events, grad_w_out)
        return (output[None], grad_events[None], grad_w_out)

    return jax.shard_map(
        per_device,
        mesh=mesh,
        in_specs=(P("dp", "ctx", None), P("dp", "ctx"), P("dp"), P("dp", "ctx", None), P(), P()),
        out_specs=(P("dp", "ctx", None), P("dp", "ctx", None), P("dp", None)),
        check_vma=False,
    )


def solution(mesh):
    return build(mesh, X_CHIPS)
```

```python
import functools
import math

import jax
import jax.numpy as jnp
from jax import lax
from jax.experimental import pallas as pl
from jax.experimental.pallas import tpu as pltpu
from jax.sharding import PartitionSpec as P

HEADS = 4
DH = 128
WIDTH = HEADS * DH
X_CHIPS = 4
EPSILON = 1e-06
MESH = pl.DeviceIdType.MESH
F32 = jnp.float32
BF16 = jnp.bfloat16
U_COL, V_COL, Q_COL, K_COL = 0, WIDTH, 2 * WIDTH, 3 * WIDTH


def silu_parts(v):
    s = 0.5 * jnp.tanh(0.5 * v) + 0.5
    a = v * s
    return a, s + a * (1.0 - s)


def mul(a, b):
    return jnp.dot(a, b, preferred_element_type=F32)


def mul_t(a, b):
    return lax.dot_general(a, b, (((1,), (1,)), ((), ())), preferred_element_type=F32)


def kernel(
    Z, X, Y,
    events, keep, lengths, cotangent, w_in, w_out,
    out, grad_events, grad_w_out,
    keep_v, e_all, act_all, do_all, cot_all, w_in_v, w_out_v, slope_v, gg_v, gu_v, att_v, dq_v, dk_v, dv_v, ge_v,
    g_v, p_v, gt_send, gt_all, z_send, z_recv, c_recv,
    local_sem, e_ssem, e_rsem, d_ssem, d_rsem, cot_ssem, cot_rsem, gt_ssem, gt_rsem, z_ssem, z_rsem, c_ssem, c_rsem,
):
    R = events.shape[0]
    D = events.shape[1]
    PAIR = 2 * R
    S = 2 * X
    ZH = Z // 2
    RD = D // (Z * X)
    scale = 1.0 / math.sqrt(DH)
    dp, ctx = lax.axis_index("dp"), lax.axis_index("ctx")
    z, x = dp // X, dp % X
    y, core = ctx // 2, ctx % 2
    other = 1 - core
    sib = y * 2 + other
    mine = x * 2 + core

    def block(b):
        return pl.ds(pl.multiple_of(b * R, R), R)

    def pair(c):
        return pl.ds(pl.multiple_of(c * PAIR, PAIR), PAIR)

    rows = block(ctx)

    ev_copy = pltpu.make_async_copy(events, e_all.at[rows], local_sem.at[0])
    ev_copy.start()
    keep_copy = pltpu.make_async_copy(keep, keep_v, local_sem.at[7])
    keep_copy.start()
    cot_copy = pltpu.make_async_copy(cotangent, cot_all.at[block(mine)], local_sem.at[1])
    cot_copy.start()
    w_copies = []
    for g in range(4):
        cols = pl.ds(g * WIDTH, WIDTH)
        w_copies.append(pltpu.make_async_copy(w_in.at[:, cols], w_in_v.at[:, cols], local_sem.at[2 + g]))
    for copy in w_copies:
        copy.start()
    wo_copy = pltpu.make_async_copy(w_out, w_out_v, local_sem.at[6])
    wo_copy.start()

    barrier = pltpu.get_barrier_semaphore()

    def greet(dp_to, ctx_to):
        pl.semaphore_signal(barrier, inc=1, device_id=(dp_to, ctx_to), device_id_type=MESH)

    def greet_ctx(k, _):
        greet(dp, (ctx + k) % (2 * Y))
        return _

    def greet_x(k, _):
        greet(z * X + (x + k) % X, ctx)
        greet(z * X + (x + k) % X, sib)
        return _

    def greet_z(k, _):
        greet(((z + k) % Z) * X + x, ctx)
        return _

    lax.fori_loop(1, 2 * Y, greet_ctx, 0)
    lax.fori_loop(1, X, greet_x, 0)
    lax.fori_loop(1, Z, greet_z, 0)

    ev_copy.wait()
    keep_copy.wait()
    lane = lax.broadcasted_iota(jnp.int32, (1, R), 1)
    live_row = jnp.where((keep_v[...] == 1) & (ctx * R + lane < lengths[0]), 1.0, 0.0)
    eye = lax.broadcasted_iota(jnp.int32, (R, R), 0) == lax.broadcasted_iota(jnp.int32, (R, R), 1)
    live = jnp.sum(jnp.where(eye, live_row, 0.0), axis=1, keepdims=True)
    e_all[rows, :] = (e_all[rows, :].astype(F32) * live).astype(BF16)
    pl.semaphore_wait(barrier, (2 * Y - 1) + 2 * (X - 1) + (Z - 1))

    def remote(buf, b, ssem, rsem, ctx_to):
        return pltpu.make_async_remote_copy(
            src_ref=buf.at[block(b)], dst_ref=buf.at[block(b)], send_sem=ssem, recv_sem=rsem.at[b],
            device_id=(dp, ctx_to), device_id_type=MESH,
        )

    def e_out(d):
        return remote(e_all, ctx, e_ssem.at[d], e_rsem, ((y + d) % Y) * 2 + core)

    e_order = [1, 3, 2] if Y == 4 else list(range(1, Y))
    remote(e_all, ctx, e_ssem.at[0], e_rsem, sib).start()
    for d in e_order:
        e_out(d).start()

    def hand_over(buf, c, ssem, rsem):
        return remote(buf, c * 2 + core, ssem.at[Y + c], rsem, sib)

    def arrived(buf, b, ssem, rsem):
        remote(buf, b, ssem.at[0], rsem, sib).wait_recv()

    cot_copy.wait()

    def cot_out(k):
        s = (mine + k) % S
        return pltpu.make_async_remote_copy(
            src_ref=cot_all.at[block(mine)], dst_ref=cot_all.at[block(mine)],
            send_sem=cot_ssem.at[k], recv_sem=cot_rsem.at[mine],
            device_id=(z * X + s // 2, y * 2 + s % 2), device_id_type=MESH,
        )

    def cot_in(k):
        s = (mine + k) % S
        return pltpu.make_async_remote_copy(
            src_ref=cot_all.at[block(s)], dst_ref=cot_all.at[block(s)],
            send_sem=cot_ssem.at[k], recv_sem=cot_rsem.at[s],
            device_id=(z * X + s // 2, y * 2 + s % 2), device_id_type=MESH,
        )

    def each(low, high, body):
        def step(k, _):
            body(k)
            return _
        lax.fori_loop(low, high, step, 0)

    each(1, S, lambda k: cot_out(k).start())

    own = e_all[rows, :]
    for g in range(4):
        w_copies[g].wait()
        for half in range(2):
            cols = pl.ds(g * WIDTH + half * 256, 256)
            a, slope = silu_parts(mul(own, w_in_v[:, cols]))
            act_all[rows, cols] = a.astype(BF16)
            slope_v[:, cols] = slope
    wo_copy.wait()
    gg_v[...] = mul_t(cot_all[block(mine), :], w_out_v[...])

    def project(row_slice, first, count, stride):
        def body(n):
            off = pl.multiple_of(first + (n % 2) * 256 + (n // 2) * stride, 256)
            a, _ = silu_parts(mul(e_all[row_slice, :], w_in_v[:, pl.ds(off, 256)]))
            act_all[row_slice, pl.ds(off, 256)] = a.astype(BF16)
        each(0, count, body)

    def head(base, h):
        return pl.ds(base + h * DH, DH)

    def allowed(query_major):
        first = lax.broadcasted_iota(jnp.int32, (R, PAIR), 0) + core * R
        second = lax.broadcasted_iota(jnp.int32, (R, PAIR), 1)
        return first >= second if query_major else second >= first

    def forward(c, masked):
        for h in range(HEADS):
            s = mul_t(act_all[rows, head(Q_COL, h)], act_all[pair(c), head(K_COL, h)]) * scale
            a, slope = silu_parts(s)
            slope = slope * scale
            if masked:
                ok = allowed(True)
                a, slope = jnp.where(ok, a, 0.0), jnp.where(ok, slope, 0.0)
            g_v[c, h] = slope
            part = mul(a.astype(BF16), act_all[pair(c), head(V_COL, h)])
            if masked:
                att_v[:, head(0, h)] = part
            else:
                att_v[:, head(0, h)] += part

    def prepare(c, masked):
        for h in range(HEADS):
            s = mul_t(act_all[rows, head(K_COL, h)], act_all[pair(c), head(Q_COL, h)]) * scale
            a, slope = silu_parts(s)
            slope = slope * scale
            if masked:
                ok = allowed(False)
                a, slope = jnp.where(ok, a, 0.0), jnp.where(ok, slope, 0.0)
            g_v[c + 1, h] = slope
            p_v[c, h] = a.astype(BF16)

    def take_e(c):
        arrived(e_all, c * 2 + core, e_ssem, e_rsem)
        hand_over(e_all, c, e_ssem, e_rsem).start()

    arrived(e_all, sib, e_ssem, e_rsem)
    project(block(sib), V_COL, 6, 512)
    for d in e_order[:2]:
        take_e((y + d) % Y)
    forward(y, True)
    prepare(y, True)

    def chip_step(t):
        c = (y + 1 + (2 * t) % (Y - 1 if Y > 2 else 1)) % Y
        arrived(e_all, c * 2 + other, e_ssem, e_rsem)

        @pl.when(c < y)
        def _():
            project(pair(c), V_COL, 4, 1024)
            forward(c, False)

        @pl.when(c > y)
        def _():
            project(pair(c), Q_COL, 2, 512)
            prepare(c, False)

        if Y == 4:
            @pl.when(t == 0)
            def _():
                take_e((y + 2) % Y)

    each(0, Y - 1, chip_step)

    att = att_v[...]
    cen = att - jnp.mean(att, axis=1, keepdims=True)
    inv = lax.rsqrt(jnp.mean(cen * cen, axis=1, keepdims=True) + EPSILON)
    normed = cen * inv
    gate = act_all[rows, pl.ds(U_COL, WIDTH)].astype(F32)
    gated = normed * gate

    turned = jnp.transpose(gated).reshape(Z, X, RD, R)
    for to in range(X):
        gt_send[to] = turned[:, to].reshape(Z * RD, R).astype(BF16)

    def gt_part(s):
        return gt_all.at[:, block(s)]

    def gt_piece(s):
        return pl.ds(pl.multiple_of((s % 2) * (ZH * RD), ZH * RD), ZH * RD)

    def gt_out(k):
        s = (mine + k) % S
        return pltpu.make_async_remote_copy(
            src_ref=gt_send.at[s // 2, gt_piece(s)], dst_ref=gt_part(mine),
            send_sem=gt_ssem.at[k], recv_sem=gt_rsem.at[mine],
            device_id=(z * X + s // 2, y * 2 + s % 2), device_id_type=MESH,
        )

    def gt_in(k):
        s = (mine + k) % S
        return pltpu.make_async_remote_copy(
            src_ref=gt_send.at[s // 2, gt_piece(s)], dst_ref=gt_part(s),
            send_sem=gt_ssem.at[k], recv_sem=gt_rsem.at[s],
            device_id=(z * X + s // 2, y * 2 + s % 2), device_id_type=MESH,
        )

    each(1, S, lambda k: gt_out(k).start())
    gt_all[:, block(mine)] = gt_send[x, gt_piece(mine), :]

    gg = gg_v[...]
    gn = gg * gate
    grad_att = (
        gn - jnp.mean(gn, axis=1, keepdims=True) - normed * jnp.mean(gn * normed, axis=1, keepdims=True)
    ) * inv * live
    do_all[rows, :] = grad_att.astype(BF16)

    def d_out(c):
        return remote(do_all, ctx, d_ssem.at[c], d_rsem, c * 2 + core)

    d_sib = remote(do_all, ctx, d_ssem.at[y], d_rsem, sib)
    d_sib.start()
    each(0, y, lambda c: d_out(c).start())


    each(1, S, lambda k: cot_in(k).wait_recv())
    each(1, S, lambda k: gt_in(k).wait_recv())
    gram = mul(gt_all[...], cot_all[...]).reshape(ZH, RD, D)
    z_send[...] = jnp.concatenate([gram[:, :, : D // 2], gram[:, :, D // 2 :]], axis=1).astype(BF16)

    def z_out(k):
        return pltpu.make_async_remote_copy(
            src_ref=z_send.at[k], dst_ref=z_recv.at[z], send_sem=z_ssem.at[k], recv_sem=z_rsem.at[z],
            device_id=((core * ZH + k) * X + x, ctx), device_id_type=MESH,
        )

    def z_in(k):
        return pltpu.make_async_remote_copy(
            src_ref=z_send.at[0], dst_ref=z_recv.at[k], send_sem=z_ssem.at[0], recv_sem=z_rsem.at[k],
            device_id=(k * X + x, ctx), device_id_type=MESH,
        )

    def z_start(k):
        @pl.when(core * ZH + k != z)
        def _():
            z_out(k).start()

    each(0, ZH, z_start)

    out[...] = mul(gated.astype(BF16), w_out_v[...]).astype(BF16)
    gu_v[...] = gg * normed

    dq_v[...] = jnp.zeros_like(dq_v)
    dk_v[...] = jnp.zeros_like(dk_v)
    dv_v[...] = jnp.zeros_like(dv_v)

    def query_step(c):
        for h in range(HEADS):
            gw = mul_t(do_all[rows, head(0, h)], act_all[pair(c), head(V_COL, h)])
            gs = (gw * g_v[c, h]).astype(BF16)
            dq_v[:, head(0, h)] += mul(gs, act_all[pair(c), head(K_COL, h)])

    each(0, y + 1, query_step)

    def back(grad, base):
        cols = pl.ds(base, WIDTH)
        return mul_t((grad * slope_v[:, cols]).astype(BF16), w_in_v[:, cols])

    ge_v[...] = back(gu_v[...], U_COL) + back(dq_v[...], Q_COL)

    def key_step(c):
        for h in range(HEADS):
            do_h = do_all[pair(c), head(0, h)]
            gw = mul_t(act_all[rows, head(V_COL, h)], do_h)
            gs = (gw * g_v[c + 1, h]).astype(BF16)
            dv_v[:, head(0, h)] += mul(p_v[c, h], do_h)
            dk_v[:, head(0, h)] += mul(gs, act_all[pair(c), head(Q_COL, h)])

    arrived(do_all, sib, d_ssem, d_rsem)
    key_step(y)

    def later_chip(c):
        arrived(do_all, c * 2 + core, d_ssem, d_rsem)
        hand_over(do_all, c, d_ssem, d_rsem).start()
        arrived(do_all, c * 2 + other, d_ssem, d_rsem)
        key_step(c)

    each(y + 1, Y, later_chip)

    grad_events[...] = (ge_v[...] + back(dv_v[...], V_COL) + back(dk_v[...], K_COL)).astype(BF16)

    holder = z // ZH

    def c_out(k):
        return pltpu.make_async_remote_copy(
            src_ref=c_recv.at[y], dst_ref=c_recv.at[y], send_sem=c_ssem.at[k], recv_sem=c_rsem.at[y],
            device_id=(dp, (ctx + k) % (2 * Y)), device_id_type=MESH,
        )

    def c_in(k):
        return pltpu.make_async_remote_copy(
            src_ref=c_recv.at[k], dst_ref=c_recv.at[k], send_sem=c_ssem.at[0], recv_sem=c_rsem.at[k],
            device_id=(dp, sib), device_id_type=MESH,
        )

    @pl.when(core == holder)
    def _():
        z_recv[z] = z_send[z % ZH]

        def wait_z(k):
            @pl.when(k != z)
            def _():
                z_in(k).wait_recv()

        each(0, Z, wait_z)
        total = jnp.sum(z_recv[...].astype(F32), axis=0)
        c_recv[y] = jnp.concatenate([total[:RD], total[RD:]], axis=1)
        each(1, 2 * Y, lambda k: c_out(k).start())

    def wait_c(k):
        @pl.when(k * 2 + holder != ctx)
        def _():
            c_in(k).wait_recv()

    each(0, Y, wait_c)
    tokens = R * 2 * Y * Z * X
    grad_w_out[...] = jnp.sum(c_recv[...], axis=0) * (1.0 / math.sqrt(tokens))

    remote(e_all, ctx, e_ssem.at[0], e_rsem, sib).wait_send()

    def e_done(d):
        e_out(d).wait_send()
        hand_over(e_all, (y + d) % Y, e_ssem, e_rsem).wait_send()

    each(1, Y, e_done)
    each(1, S, lambda k: cot_out(k).wait_send())
    d_sib.wait_send()
    each(0, y, lambda c: d_out(c).wait_send())
    each(y + 1, Y, lambda c: hand_over(do_all, c, d_ssem, d_rsem).wait_send())
    each(1, S, lambda k: gt_out(k).wait_send())

    def z_done(k):
        @pl.when(core * ZH + k != z)
        def _():
            z_out(k).wait_send()

    each(0, ZH, z_done)

    @pl.when(core == holder)
    def _():
        each(1, 2 * Y, lambda k: c_out(k).wait_send())


def in_hbm(a):
    return pltpu.with_memory_space_constraint(a, pltpu.HBM)


def store(*refs):
    copies = [pltpu.make_async_copy(refs[n], refs[3 + n], refs[6].at[n]) for n in range(3)]
    for copy in copies:
        copy.start()
    for copy in copies:
        copy.wait()


def build(mesh, X):
    Z, Y = mesh.shape["dp"] // X, mesh.shape["ctx"] // 2

    def per_device(events, keep, lengths, cotangent, w_in, w_out):
        R, D = events.shape[1:]
        L = R * 2 * Y
        S = 2 * X
        ZH, RD = Z // 2, D // (Z * X)
        vmem = pl.BlockSpec(memory_space=pltpu.VMEM)
        hbm = pl.BlockSpec(memory_space=pltpu.HBM)
        dma = pltpu.SemaphoreType.DMA
        output, grad_events, grad_w_out = pl.pallas_call(
            functools.partial(kernel, Z, X, Y),
            out_shape=(pltpu.VMEM((R, D), BF16), pltpu.VMEM((R, D), BF16), pltpu.VMEM((RD, D), F32)),
            in_specs=[hbm, hbm, pl.BlockSpec(memory_space=pltpu.SMEM), hbm, hbm, hbm],
            out_specs=[vmem] * 3,
            scratch_shapes=[
                pltpu.VMEM((1, R), jnp.int32),
                pltpu.VMEM((L, D), BF16),
                pltpu.VMEM((L, 4 * WIDTH), BF16),
                pltpu.VMEM((L, WIDTH), BF16),
                pltpu.VMEM((S * R, D), BF16),
                pltpu.VMEM((D, 4 * WIDTH), BF16),
                pltpu.VMEM((WIDTH, D), BF16),
                pltpu.VMEM((R, 4 * WIDTH), F32),
                pltpu.VMEM((R, WIDTH), F32),
                pltpu.VMEM((R, WIDTH), F32),
                pltpu.VMEM((R, WIDTH), F32),
                pltpu.VMEM((R, WIDTH), F32),
                pltpu.VMEM((R, WIDTH), F32),
                pltpu.VMEM((R, WIDTH), F32),
                pltpu.VMEM((R, D), F32),
                pltpu.VMEM((Y + 1, HEADS, R, 2 * R), F32),
                pltpu.VMEM((Y, HEADS, R, 2 * R), BF16),
                pltpu.VMEM((X, Z * RD, R), BF16),
                pltpu.VMEM((ZH * RD, S * R), BF16),
                pltpu.VMEM((ZH, 2 * RD, D // 2), BF16),
                pltpu.VMEM((Z, 2 * RD, D // 2), BF16),
                pltpu.VMEM((Y, RD, D), F32),
                dma((8,)),
                dma((2 * Y,)), dma((2 * Y,)),
                dma((2 * Y,)), dma((2 * Y,)),
                dma((S,)), dma((S,)),
                dma((S,)), dma((S,)),
                dma((ZH,)), dma((Z,)),
                dma((2 * Y,)), dma((Y,)),
            ],
            compiler_params=pltpu.CompilerParams(
                collective_id=0, has_side_effects=True, vmem_limit_bytes=56 * 1024 * 1024
            ),
            name="layer",
        )(in_hbm(events[0]), in_hbm(keep), lengths, in_hbm(cotangent[0]), in_hbm(w_in), in_hbm(w_out))
        output, grad_events, grad_w_out = pl.pallas_call(
            store,
            out_shape=(
                jax.ShapeDtypeStruct((R, D), BF16),
                jax.ShapeDtypeStruct((R, D), BF16),
                jax.ShapeDtypeStruct((RD, D), F32),
            ),
            in_specs=[vmem] * 3,
            out_specs=(hbm, hbm, hbm),
            scratch_shapes=[dma((3,))],
            name="store",
        )(output, grad_events, grad_w_out)
        return (output[None], grad_events[None], grad_w_out)

    return jax.shard_map(
        per_device,
        mesh=mesh,
        in_specs=(P("dp", "ctx", None), P("dp", "ctx"), P("dp"), P("dp", "ctx", None), P(), P()),
        out_specs=(P("dp", "ctx", None), P("dp", "ctx", None), P("dp", None)),
        check_vma=False,
    )


def solution(mesh):
    return build(mesh, X_CHIPS)
```

```python
import functools
import math

import jax
import jax.numpy as jnp
from jax import lax
from jax.experimental import pallas as pl
from jax.experimental.pallas import tpu as pltpu
from jax.sharding import PartitionSpec as P

HEADS = 4
DH = 128
WIDTH = HEADS * DH
X_CHIPS = 4
EPSILON = 1e-06
MESH = pl.DeviceIdType.MESH
F32 = jnp.float32
BF16 = jnp.bfloat16
U_COL, V_COL, Q_COL, K_COL = 0, WIDTH, 2 * WIDTH, 3 * WIDTH


def silu_parts(v):
    s = 0.5 * jnp.tanh(0.5 * v) + 0.5
    a = v * s
    return a, s + a * (1.0 - s)


def mul(a, b):
    return jnp.dot(a, b, preferred_element_type=F32)


def mul_t(a, b):
    return lax.dot_general(a, b, (((1,), (1,)), ((), ())), preferred_element_type=F32)


class Ring:
    def __init__(self, buf, rows, n, pos, core, ssem, rsem, place):
        self.buf, self.rows, self.n, self.pos, self.core = buf, rows, n, pos, core
        self.ssem, self.rsem = ssem, rsem
        self.sib = place(pos, 1 - core)
        self.right, self.left = place((pos + 1) % n, core), place((pos + n - 1) % n, core)
        self.l, self.r, self.f = (pos + n - 1) % n, (pos + 1) % n, (pos + 2) % n

    def copy(self, chip, core, first, count, k, sem, to):
        rows = self.rows // 4
        start = pl.multiple_of((chip * 2 + core) * self.rows + first * rows, rows)
        part = self.buf.at[pl.ds(start, count * rows)]
        return pltpu.make_async_remote_copy(
            src_ref=part, dst_ref=part, send_sem=self.ssem.at[k], recv_sem=self.rsem.at[sem],
            device_id=to, device_id_type=MESH,
        )

    def quarter(self, chip, q, k, to):
        return self.copy(chip, self.core, q, 1, k, chip * 4 + q, to)

    def hand(self, chip, half, k):
        return self.copy(chip, self.core, half * 2, 2, k, 4 * self.n + chip * 2 + half, self.sib)

    def own(self):
        near = []
        if self.n > 1:
            for n in range(4):
                near.append(self.quarter(self.pos, n, 2 + n, self.right))
                near.append(self.quarter(self.pos, (n + 2) % 4, 6 + n, self.left))
        return near + [self.hand(self.pos, half, half) for half in range(2)]

    def passed(self):
        steps = []
        for n in range(2):
            steps.append((self.l, n, self.quarter(self.l, n, 10 + n, self.right)))
            steps.append((self.r, 2 + n, self.quarter(self.r, 2 + n, 12 + n, self.left)))
        return steps

    def wait(self, chip, first, count=1):
        for q in range(first, first + count):
            self.quarter(chip, q, 0, self.sib).wait_recv()

    def wait_other(self, chip):
        for half in range(2):
            self.copy(chip, 1 - self.core, half * 2, 2, 0, 4 * self.n + chip * 2 + half, self.sib).wait_recv()

    def start(self):
        for copy in self.own():
            copy.start()

    def relay(self):
        for chip, q, copy in self.passed():
            self.wait(chip, q)
            copy.start()

    def hand_near(self):
        self.hand(self.l, 0, 14).start()
        self.hand(self.r, 1, 17).start()
        self.wait(self.l, 2, 2)
        self.hand(self.l, 1, 15).start()
        self.wait(self.r, 0, 2)
        self.hand(self.r, 0, 16).start()

    def hand_far(self):
        for half in range(2):
            self.wait(self.f, half * 2, 2)
            self.hand(self.f, half, 18 + half).start()

    def done(self):
        for copy in self.own():
            copy.wait_send()
        if self.n > 1:
            for _, _, copy in self.passed():
                copy.wait_send()
            for n, chip in enumerate((self.l, self.r, self.f)):
                for half in range(2):
                    self.hand(chip, half, 14 + 2 * n + half).wait_send()


def kernel(
    Z, X, Y,
    events, keep, lengths, cotangent, w_in, w_out,
    out, grad_events, grad_w_out,
    keep_v, e_all, act_all, do_all, cot_all, w_in_v, w_out_v, slope_v, gg_v, gu_v, att_v, dq_v, dk_v, dv_v, ge_v,
    g_v, p_v, w_v, gt_send, gt_all, z_send, z_recv, c_recv,
    local_sem, e_ssem, e_rsem, d_ssem, d_rsem, cot_ssem, cot_rsem, gt_ssem, gt_rsem, z_ssem, z_rsem, c_ssem, c_rsem,
):
    R = events.shape[0]
    D = events.shape[1]
    PAIR = 2 * R
    S = 2 * X
    ZH = Z // 2
    RD = D // (Z * X)
    scale = 1.0 / math.sqrt(DH)
    dp, ctx = lax.axis_index("dp"), lax.axis_index("ctx")
    z, x = dp // X, dp % X
    y, core = ctx // 2, ctx % 2
    other = 1 - core
    sib = y * 2 + other
    mine = x * 2 + core

    def block(b):
        return pl.ds(pl.multiple_of(b * R, R), R)

    def pair(c):
        return pl.ds(pl.multiple_of(c * PAIR, PAIR), PAIR)

    rows = block(ctx)

    ev_copy = pltpu.make_async_copy(events, e_all.at[rows], local_sem.at[0])
    ev_copy.start()
    keep_copy = pltpu.make_async_copy(keep, keep_v, local_sem.at[7])
    keep_copy.start()
    cot_copy = pltpu.make_async_copy(cotangent, cot_all.at[block(mine)], local_sem.at[1])
    cot_copy.start()
    w_copies = []
    for g in range(4):
        cols = pl.ds(g * WIDTH, WIDTH)
        w_copies.append(pltpu.make_async_copy(w_in.at[:, cols], w_in_v.at[:, cols], local_sem.at[2 + g]))
    for copy in w_copies:
        copy.start()
    wo_copy = pltpu.make_async_copy(w_out, w_out_v, local_sem.at[6])
    wo_copy.start()

    barrier = pltpu.get_barrier_semaphore()

    def greet(dp_to, ctx_to):
        pl.semaphore_signal(barrier, inc=1, device_id=(dp_to, ctx_to), device_id_type=MESH)

    def greet_ctx(k, _):
        greet(dp, (ctx + k) % (2 * Y))
        return _

    def greet_x(k, _):
        greet(z * X + (x + k) % X, ctx)
        greet(z * X + (x + k) % X, sib)
        return _

    def greet_z(k, _):
        greet(((z + k) % Z) * X + x, ctx)
        return _

    lax.fori_loop(1, 2 * Y, greet_ctx, 0)
    lax.fori_loop(1, X, greet_x, 0)
    lax.fori_loop(1, Z, greet_z, 0)

    ev_copy.wait()
    keep_copy.wait()
    lane = lax.broadcasted_iota(jnp.int32, (1, R), 1)
    live_row = jnp.where((keep_v[...] == 1) & (ctx * R + lane < lengths[0]), 1.0, 0.0)
    eye = lax.broadcasted_iota(jnp.int32, (R, R), 0) == lax.broadcasted_iota(jnp.int32, (R, R), 1)
    live = jnp.sum(jnp.where(eye, live_row, 0.0), axis=1, keepdims=True)
    e_all[rows, :] = (e_all[rows, :].astype(F32) * live).astype(BF16)
    pl.semaphore_wait(barrier, (2 * Y - 1) + 2 * (X - 1) + (Z - 1))

    def remote(buf, b, ssem, rsem, ctx_to):
        return pltpu.make_async_remote_copy(
            src_ref=buf.at[block(b)], dst_ref=buf.at[block(b)], send_sem=ssem, recv_sem=rsem.at[b],
            device_id=(dp, ctx_to), device_id_type=MESH,
        )

    def arrived(buf, b, ssem, rsem):
        remote(buf, b, ssem.at[0], rsem, sib).wait_recv()

    def each(low, high, body):
        def step(k, _):
            body(k)
            return _
        lax.fori_loop(low, high, step, 0)

    e_ring = Ring(e_all, R, Y, y, core, e_ssem, e_rsem, lambda chip, c: (dp, chip * 2 + c))
    c_ring = Ring(cot_all, R, X, x, core, cot_ssem, cot_rsem, lambda chip, c: (z * X + chip, y * 2 + c))
    e_ring.start()
    cot_copy.wait()
    c_ring.start()

    own = e_all[rows, :]
    for g in range(4):
        w_copies[g].wait()
        for half in range(2):
            cols = pl.ds(g * WIDTH + half * 256, 256)
            a, slope = silu_parts(mul(own, w_in_v[:, cols]))
            act_all[rows, cols] = a.astype(BF16)
            slope_v[:, cols] = slope
    wo_copy.wait()
    gg_v[...] = mul_t(cot_all[block(mine), :], w_out_v[...])

    def project(b, *bases):
        for base in bases:
            for half in range(2):
                cols = pl.ds(base + half * 256, 256)
                a, _ = silu_parts(mul(e_all[block(b), :], w_in_v[:, cols]))
                act_all[block(b), cols] = a.astype(BF16)

    def project_chip(c, k):
        @pl.when(c < y)
        def _():
            project(c * 2 + k, V_COL, K_COL)

        @pl.when(c > y)
        def _():
            project(c * 2 + k, Q_COL)

    def head(base, h):
        return pl.ds(base + h * DH, DH)

    def allowed(query_major):
        first = lax.broadcasted_iota(jnp.int32, (R, PAIR), 0) + core * R
        second = lax.broadcasted_iota(jnp.int32, (R, PAIR), 1)
        return first >= second if query_major else second >= first

    def forward(c, masked):
        for h in range(HEADS):
            s = mul_t(act_all[rows, head(Q_COL, h)], act_all[pair(c), head(K_COL, h)]) * scale
            a, slope = silu_parts(s)
            slope = slope * scale
            if masked:
                ok = allowed(True)
                a, slope = jnp.where(ok, a, 0.0), jnp.where(ok, slope, 0.0)
            g_v[c, h] = slope
            w_v[h] = a.astype(BF16)
        part = jnp.concatenate([mul(w_v[h], act_all[pair(c), head(V_COL, h)]) for h in range(HEADS)], axis=1)
        if masked:
            att_v[...] = part
        else:
            att_v[...] += part

    def prepare(c, masked):
        for h in range(HEADS):
            s = mul_t(act_all[rows, head(K_COL, h)], act_all[pair(c), head(Q_COL, h)]) * scale
            a, slope = silu_parts(s)
            slope = slope * scale
            if masked:
                ok = allowed(False)
                a, slope = jnp.where(ok, a, 0.0), jnp.where(ok, slope, 0.0)
            g_v[c + 1, h] = slope
            p_v[c, h] = a.astype(BF16)

    e_ring.wait_other(y)
    project(sib, V_COL, Q_COL, K_COL)
    forward(y, True)
    prepare(y, True)
    if Y > 1:
        e_ring.relay()
    if X > 1:
        c_ring.relay()
    if Y > 1:
        e_ring.hand_near()

    def chip_at(t):
        return (y + 1 + (2 * t) % 3) % Y

    def chip_step(t):
        c = chip_at(t)

        @pl.when(t == 2)
        def _():
            e_ring.hand_far()
            project_chip(c, core)

        e_ring.wait_other(c)
        project_chip(c, other)

        @pl.when(c < y)
        def _():
            forward(c, False)

        @pl.when(c > y)
        def _():
            prepare(c, False)

    if Y > 1:
        each(0, 2, lambda t: project_chip(chip_at(t), core))
    if X > 1:
        c_ring.hand_near()
    each(0, Y - 1, chip_step)

    att = att_v[...]
    cen = att - jnp.mean(att, axis=1, keepdims=True)
    inv = lax.rsqrt(jnp.mean(cen * cen, axis=1, keepdims=True) + EPSILON)
    normed = cen * inv
    gate = act_all[rows, pl.ds(U_COL, WIDTH)].astype(F32)
    gated = normed * gate

    turned = jnp.transpose(gated).reshape(Z, X, RD, R)
    for to in range(X):
        gt_send[to] = turned[:, to].reshape(Z * RD, R).astype(BF16)

    def gt_part(s):
        return gt_all.at[:, block(s)]

    def gt_piece(s):
        return pl.ds(pl.multiple_of((s % 2) * (ZH * RD), ZH * RD), ZH * RD)

    def gt_out(k):
        s = (mine + k) % S
        return pltpu.make_async_remote_copy(
            src_ref=gt_send.at[s // 2, gt_piece(s)], dst_ref=gt_part(mine),
            send_sem=gt_ssem.at[k], recv_sem=gt_rsem.at[mine],
            device_id=(z * X + s // 2, y * 2 + s % 2), device_id_type=MESH,
        )

    def gt_in(k):
        s = (mine + k) % S
        return pltpu.make_async_remote_copy(
            src_ref=gt_send.at[s // 2, gt_piece(s)], dst_ref=gt_part(s),
            send_sem=gt_ssem.at[k], recv_sem=gt_rsem.at[s],
            device_id=(z * X + s // 2, y * 2 + s % 2), device_id_type=MESH,
        )

    each(1, S, lambda k: gt_out(k).start())
    gt_all[:, block(mine)] = gt_send[x, gt_piece(mine), :]

    gg = gg_v[...]
    gn = gg * gate
    grad_att = (
        gn - jnp.mean(gn, axis=1, keepdims=True) - normed * jnp.mean(gn * normed, axis=1, keepdims=True)
    ) * inv * live
    do_all[rows, :] = grad_att.astype(BF16)

    def d_out(c):
        return remote(do_all, ctx, d_ssem.at[c], d_rsem, c * 2 + core)

    d_sib = remote(do_all, ctx, d_ssem.at[y], d_rsem, sib)
    d_sib.start()
    each(0, y, lambda c: d_out(c).start())


    c_ring.wait_other(x)
    if X > 1:
        c_ring.hand_far()
        each(1, X, lambda d: c_ring.wait_other((x + d) % X))
    each(1, S, lambda k: gt_in(k).wait_recv())
    gram = mul(gt_all[...], cot_all[...]).reshape(ZH, RD, D)
    z_send[...] = jnp.concatenate([gram[:, :, : D // 2], gram[:, :, D // 2 :]], axis=1).astype(BF16)

    def z_out(k):
        return pltpu.make_async_remote_copy(
            src_ref=z_send.at[k], dst_ref=z_recv.at[z], send_sem=z_ssem.at[k], recv_sem=z_rsem.at[z],
            device_id=((core * ZH + k) * X + x, ctx), device_id_type=MESH,
        )

    def z_in(k):
        return pltpu.make_async_remote_copy(
            src_ref=z_send.at[0], dst_ref=z_recv.at[k], send_sem=z_ssem.at[0], recv_sem=z_rsem.at[k],
            device_id=(k * X + x, ctx), device_id_type=MESH,
        )

    def z_start(k):
        @pl.when(core * ZH + k != z)
        def _():
            z_out(k).start()

    each(0, ZH, z_start)

    out[...] = mul(gated.astype(BF16), w_out_v[...]).astype(BF16)
    gu_v[...] = gg * normed

    dq_v[...] = jnp.zeros_like(dq_v)
    dk_v[...] = jnp.zeros_like(dk_v)
    dv_v[...] = jnp.zeros_like(dv_v)

    def query_step(c):
        for h in range(HEADS):
            gw = mul_t(do_all[rows, head(0, h)], act_all[pair(c), head(V_COL, h)])
            gs = (gw * g_v[c, h]).astype(BF16)
            dq_v[:, head(0, h)] += mul(gs, act_all[pair(c), head(K_COL, h)])

    each(0, y + 1, query_step)

    def back(grad, base):
        cols = pl.ds(base, WIDTH)
        return mul_t((grad * slope_v[:, cols]).astype(BF16), w_in_v[:, cols])

    ge_v[...] = back(gu_v[...], U_COL) + back(dq_v[...], Q_COL)

    def key_step(c):
        for h in range(HEADS):
            do_h = do_all[pair(c), head(0, h)]
            gw = mul_t(act_all[rows, head(V_COL, h)], do_h)
            gs = (gw * g_v[c + 1, h]).astype(BF16)
            dv_v[:, head(0, h)] += mul(p_v[c, h], do_h)
            dk_v[:, head(0, h)] += mul(gs, act_all[pair(c), head(Q_COL, h)])

    arrived(do_all, sib, d_ssem, d_rsem)
    key_step(y)

    def hand_over(c):
        return remote(do_all, c * 2 + core, d_ssem.at[Y + c], d_rsem, sib)

    def later_chip(c):
        arrived(do_all, c * 2 + core, d_ssem, d_rsem)
        hand_over(c).start()
        arrived(do_all, c * 2 + other, d_ssem, d_rsem)
        key_step(c)

    each(y + 1, Y, later_chip)

    grad_events[...] = (ge_v[...] + back(dv_v[...], V_COL) + back(dk_v[...], K_COL)).astype(BF16)

    holder = z // ZH

    def c_out(k):
        return pltpu.make_async_remote_copy(
            src_ref=c_recv.at[y], dst_ref=c_recv.at[y], send_sem=c_ssem.at[k], recv_sem=c_rsem.at[y],
            device_id=(dp, (ctx + k) % (2 * Y)), device_id_type=MESH,
        )

    def c_in(k):
        return pltpu.make_async_remote_copy(
            src_ref=c_recv.at[k], dst_ref=c_recv.at[k], send_sem=c_ssem.at[0], recv_sem=c_rsem.at[k],
            device_id=(dp, sib), device_id_type=MESH,
        )

    e_ring.done()
    c_ring.done()
    d_sib.wait_send()
    each(0, y, lambda c: d_out(c).wait_send())
    each(y + 1, Y, lambda c: hand_over(c).wait_send())
    each(1, S, lambda k: gt_out(k).wait_send())

    def z_done(k):
        @pl.when(core * ZH + k != z)
        def _():
            z_out(k).wait_send()

    each(0, ZH, z_done)

    @pl.when(core == holder)
    def _():
        z_recv[z] = z_send[z % ZH]

        def wait_z(k):
            @pl.when(k != z)
            def _():
                z_in(k).wait_recv()

        each(0, Z, wait_z)
        total = jnp.sum(z_recv[...].astype(F32), axis=0)
        c_recv[y] = jnp.concatenate([total[:RD], total[RD:]], axis=1)
        each(1, 2 * Y, lambda k: c_out(k).start())

    def wait_c(k):
        @pl.when(k * 2 + holder != ctx)
        def _():
            c_in(k).wait_recv()

    each(0, Y, wait_c)
    tokens = R * 2 * Y * Z * X
    grad_w_out[...] = jnp.sum(c_recv[...], axis=0) * (1.0 / math.sqrt(tokens))

    @pl.when(core == holder)
    def _():
        each(1, 2 * Y, lambda k: c_out(k).wait_send())


def in_hbm(a):
    return pltpu.with_memory_space_constraint(a, pltpu.HBM)


def store(*refs):
    copies = [pltpu.make_async_copy(refs[n], refs[3 + n], refs[6].at[n]) for n in range(3)]
    for copy in copies:
        copy.start()
    for copy in copies:
        copy.wait()


def build(mesh, X):
    Z, Y = mesh.shape["dp"] // X, mesh.shape["ctx"] // 2

    def per_device(events, keep, lengths, cotangent, w_in, w_out):
        R, D = events.shape[1:]
        L = R * 2 * Y
        S = 2 * X
        ZH, RD = Z // 2, D // (Z * X)
        vmem = pl.BlockSpec(memory_space=pltpu.VMEM)
        hbm = pl.BlockSpec(memory_space=pltpu.HBM)
        dma = pltpu.SemaphoreType.DMA
        output, grad_events, grad_w_out = pl.pallas_call(
            functools.partial(kernel, Z, X, Y),
            out_shape=(pltpu.VMEM((R, D), BF16), pltpu.VMEM((R, D), BF16), pltpu.VMEM((RD, D), F32)),
            in_specs=[hbm, hbm, pl.BlockSpec(memory_space=pltpu.SMEM), hbm, hbm, hbm],
            out_specs=[vmem] * 3,
            scratch_shapes=[
                pltpu.VMEM((1, R), jnp.int32),
                pltpu.VMEM((L, D), BF16),
                pltpu.VMEM((L, 4 * WIDTH), BF16),
                pltpu.VMEM((L, WIDTH), BF16),
                pltpu.VMEM((S * R, D), BF16),
                pltpu.VMEM((D, 4 * WIDTH), BF16),
                pltpu.VMEM((WIDTH, D), BF16),
                pltpu.VMEM((R, 4 * WIDTH), F32),
                pltpu.VMEM((R, WIDTH), F32),
                pltpu.VMEM((R, WIDTH), F32),
                pltpu.VMEM((R, WIDTH), F32),
                pltpu.VMEM((R, WIDTH), F32),
                pltpu.VMEM((R, WIDTH), F32),
                pltpu.VMEM((R, WIDTH), F32),
                pltpu.VMEM((R, D), F32),
                pltpu.VMEM((Y + 1, HEADS, R, 2 * R), F32),
                pltpu.VMEM((Y, HEADS, R, 2 * R), BF16),
                pltpu.VMEM((HEADS, R, 2 * R), BF16),
                pltpu.VMEM((X, Z * RD, R), BF16),
                pltpu.VMEM((ZH * RD, S * R), BF16),
                pltpu.VMEM((ZH, 2 * RD, D // 2), BF16),
                pltpu.VMEM((Z, 2 * RD, D // 2), BF16),
                pltpu.VMEM((Y, RD, D), F32),
                dma((8,)),
                dma((20,)), dma((6 * Y,)),
                dma((2 * Y,)), dma((2 * Y,)),
                dma((20,)), dma((6 * X,)),
                dma((S,)), dma((S,)),
                dma((ZH,)), dma((Z,)),
                dma((2 * Y,)), dma((Y,)),
            ],
            compiler_params=pltpu.CompilerParams(
                collective_id=0, has_side_effects=True, vmem_limit_bytes=56 * 1024 * 1024
            ),
            name="layer",
        )(in_hbm(events[0]), in_hbm(keep), lengths, in_hbm(cotangent[0]), in_hbm(w_in), in_hbm(w_out))
        output, grad_events, grad_w_out = pl.pallas_call(
            store,
            out_shape=(
                jax.ShapeDtypeStruct((R, D), BF16),
                jax.ShapeDtypeStruct((R, D), BF16),
                jax.ShapeDtypeStruct((RD, D), F32),
            ),
            in_specs=[vmem] * 3,
            out_specs=(hbm, hbm, hbm),
            scratch_shapes=[dma((3,))],
            name="store",
        )(*[pltpu.with_memory_space_constraint(a, pltpu.VMEM) for a in (output, grad_events, grad_w_out)])
        return (output[None], grad_events[None], grad_w_out)

    return jax.shard_map(
        per_device,
        mesh=mesh,
        in_specs=(P("dp", "ctx", None), P("dp", "ctx"), P("dp"), P("dp", "ctx", None), P(), P()),
        out_specs=(P("dp", "ctx", None), P("dp", "ctx", None), P("dp", None)),
        check_vma=False,
    )


def solution(mesh):
    return build(mesh, X_CHIPS)
```

```python
import functools
import math

import jax
import jax.numpy as jnp
from jax import lax
from jax.experimental import pallas as pl
from jax.experimental.pallas import tpu as pltpu
from jax.sharding import PartitionSpec as P

HEADS = 4
DH = 128
WIDTH = HEADS * DH
X_CHIPS = 4
EPSILON = 1e-06
MESH = pl.DeviceIdType.MESH
F32 = jnp.float32
BF16 = jnp.bfloat16
U_COL, V_COL, Q_COL, K_COL = 0, WIDTH, 2 * WIDTH, 3 * WIDTH


def silu_parts(v):
    s = 0.5 * jnp.tanh(0.5 * v) + 0.5
    a = v * s
    return a, s + a * (1.0 - s)


def mul(a, b):
    return jnp.dot(a, b, preferred_element_type=F32)


def mul_t(a, b):
    return lax.dot_general(a, b, (((1,), (1,)), ((), ())), preferred_element_type=F32)


class Ring:
    def __init__(self, buf, rows, n, pos, core, ssem, rsem, place):
        self.buf, self.rows, self.n, self.pos, self.core = buf, rows, n, pos, core
        self.ssem, self.rsem = ssem, rsem
        self.sib = place(pos, 1 - core)
        self.right, self.left = place((pos + 1) % n, core), place((pos + n - 1) % n, core)
        self.l, self.r, self.f = (pos + n - 1) % n, (pos + 1) % n, (pos + 2) % n

    def copy(self, chip, core, first, count, k, sem, to):
        rows = self.rows // 4
        start = pl.multiple_of((chip * 2 + core) * self.rows + first * rows, rows)
        part = self.buf.at[pl.ds(start, count * rows)]
        return pltpu.make_async_remote_copy(
            src_ref=part, dst_ref=part, send_sem=self.ssem.at[k], recv_sem=self.rsem.at[sem],
            device_id=to, device_id_type=MESH,
        )

    def quarter(self, chip, q, k, to):
        return self.copy(chip, self.core, q, 1, k, chip * 4 + q, to)

    def hand(self, chip, half, k):
        return self.copy(chip, self.core, half * 2, 2, k, 4 * self.n + chip * 2 + half, self.sib)

    def first(self):
        near = []
        if self.n > 1:
            for n in range(2):
                near.append(self.quarter(self.pos, n, 2 + n, self.right))
                near.append(self.quarter(self.pos, n + 2, 6 + n, self.left))
        return near + [self.hand(self.pos, half, half) for half in range(2)]

    def second(self):
        near = []
        if self.n > 1:
            for n in range(2):
                near.append(self.quarter(self.pos, n + 2, 4 + n, self.right))
                near.append(self.quarter(self.pos, n, 8 + n, self.left))
        return near

    def passed(self):
        steps = []
        for n in range(2):
            steps.append((self.l, n, self.quarter(self.l, n, 10 + n, self.right)))
            steps.append((self.r, 2 + n, self.quarter(self.r, 2 + n, 12 + n, self.left)))
        return steps

    def wait(self, chip, first, count=1):
        for q in range(first, first + count):
            self.quarter(chip, q, 0, self.sib).wait_recv()

    def wait_other(self, chip):
        for half in range(2):
            self.copy(chip, 1 - self.core, half * 2, 2, 0, 4 * self.n + chip * 2 + half, self.sib).wait_recv()

    def start(self, copies):
        for copy in copies:
            copy.start()

    def relay(self):
        for chip, q, copy in self.passed():
            self.wait(chip, q)
            copy.start()

    def hand_near(self):
        self.hand(self.l, 0, 14).start()
        self.hand(self.r, 1, 17).start()
        self.wait(self.l, 2, 2)
        self.hand(self.l, 1, 15).start()
        self.wait(self.r, 0, 2)
        self.hand(self.r, 0, 16).start()

    def hand_far(self):
        for half in range(2):
            self.wait(self.f, half * 2, 2)
            self.hand(self.f, half, 18 + half).start()

    def done(self):
        for copy in self.first() + self.second():
            copy.wait_send()
        if self.n > 1:
            for _, _, copy in self.passed():
                copy.wait_send()
            for n, chip in enumerate((self.l, self.r, self.f)):
                for half in range(2):
                    self.hand(chip, half, 14 + 2 * n + half).wait_send()


def kernel(
    Z, X, Y,
    events, keep, lengths, cotangent, w_in, w_out,
    out, grad_events, grad_w_out,
    keep_v, e_all, act_all, do_all, cot_all, w_in_v, w_out_v, slope_v, gg_v, gu_v, att_v, dq_v, dk_v, dv_v, ge_v,
    g_v, p_v, w_v, gt_send, gt_all, z_send, z_recv, c_recv,
    local_sem, e_ssem, e_rsem, d_ssem, d_rsem, cot_ssem, cot_rsem, gt_ssem, gt_rsem, z_ssem, z_rsem, c_ssem, c_rsem,
):
    R = events.shape[0]
    D = events.shape[1]
    PAIR = 2 * R
    S = 2 * X
    ZH = Z // 2
    RD = D // (Z * X)
    scale = 1.0 / math.sqrt(DH)
    dp, ctx = lax.axis_index("dp"), lax.axis_index("ctx")
    z, x = dp // X, dp % X
    y, core = ctx // 2, ctx % 2
    other = 1 - core
    sib = y * 2 + other
    mine = x * 2 + core

    def block(b):
        return pl.ds(pl.multiple_of(b * R, R), R)

    def pair(c):
        return pl.ds(pl.multiple_of(c * PAIR, PAIR), PAIR)

    rows = block(ctx)

    ev_copy = pltpu.make_async_copy(events, e_all.at[rows], local_sem.at[0])
    ev_copy.start()
    keep_copy = pltpu.make_async_copy(keep, keep_v, local_sem.at[7])
    keep_copy.start()
    barrier = pltpu.get_barrier_semaphore()

    def greet(dp_to, ctx_to):
        pl.semaphore_signal(barrier, inc=1, device_id=(dp_to, ctx_to), device_id_type=MESH)

    def greet_ctx(k, _):
        greet(dp, (ctx + k) % (2 * Y))
        return _

    def greet_x(k, _):
        greet(z * X + (x + k) % X, ctx)
        greet(z * X + (x + k) % X, sib)
        return _

    def greet_z(k, _):
        greet(((z + k) % Z) * X + x, ctx)
        return _

    lax.fori_loop(1, 2 * Y, greet_ctx, 0)
    lax.fori_loop(1, X, greet_x, 0)

    @pl.when(core == z // ZH)
    def _():
        lax.fori_loop(1, Z, greet_z, 0)

    cot_copy = pltpu.make_async_copy(cotangent, cot_all.at[block(mine)], local_sem.at[1])
    cot_copy.start()
    w_copies = []
    for g in range(4):
        cols = pl.ds(g * WIDTH, WIDTH)
        w_copies.append(pltpu.make_async_copy(w_in.at[:, cols], w_in_v.at[:, cols], local_sem.at[2 + g]))
    for copy in w_copies:
        copy.start()
    wo_copy = pltpu.make_async_copy(w_out, w_out_v, local_sem.at[6])
    wo_copy.start()

    ev_copy.wait()
    keep_copy.wait()
    lane = lax.broadcasted_iota(jnp.int32, (1, R), 1)
    live_row = jnp.where((keep_v[...] == 1) & (ctx * R + lane < lengths[0]), 1.0, 0.0)
    eye = lax.broadcasted_iota(jnp.int32, (R, R), 0) == lax.broadcasted_iota(jnp.int32, (R, R), 1)
    live = jnp.sum(jnp.where(eye, live_row, 0.0), axis=1, keepdims=True)
    e_all[rows, :] = (e_all[rows, :].astype(F32) * live).astype(BF16)
    pl.semaphore_wait(barrier, (2 * Y - 1) + 2 * (X - 1) + ZH - (core == z // ZH).astype(jnp.int32))

    def remote(buf, b, ssem, rsem, ctx_to):
        return pltpu.make_async_remote_copy(
            src_ref=buf.at[block(b)], dst_ref=buf.at[block(b)], send_sem=ssem, recv_sem=rsem.at[b],
            device_id=(dp, ctx_to), device_id_type=MESH,
        )

    def arrived(buf, b, ssem, rsem):
        remote(buf, b, ssem.at[0], rsem, sib).wait_recv()

    def each(low, high, body):
        def step(k, _):
            body(k)
            return _
        lax.fori_loop(low, high, step, 0)

    e_ring = Ring(e_all, R, Y, y, core, e_ssem, e_rsem, lambda chip, c: (dp, chip * 2 + c))
    c_ring = Ring(cot_all, R, X, x, core, cot_ssem, cot_rsem, lambda chip, c: (z * X + chip, y * 2 + c))
    e_ring.start(e_ring.first())
    cot_copy.wait()

    own = e_all[rows, :]
    for g in range(4):
        w_copies[g].wait()
        for half in range(2):
            cols = pl.ds(g * WIDTH + half * 256, 256)
            a, slope = silu_parts(mul(own, w_in_v[:, cols]))
            act_all[rows, cols] = a.astype(BF16)
            slope_v[:, cols] = slope
    e_ring.start(e_ring.second())
    c_ring.start(c_ring.first())
    wo_copy.wait()
    gg_v[...] = mul_t(cot_all[block(mine), :], w_out_v[...])

    def project(b, *bases):
        for base in bases:
            for half in range(2):
                cols = pl.ds(base + half * 256, 256)
                a, _ = silu_parts(mul(e_all[block(b), :], w_in_v[:, cols]))
                act_all[block(b), cols] = a.astype(BF16)

    def project_chip(c, k):
        @pl.when(c < y)
        def _():
            project(c * 2 + k, V_COL, K_COL)

        @pl.when(c > y)
        def _():
            project(c * 2 + k, Q_COL)

    def head(base, h):
        return pl.ds(base + h * DH, DH)

    def allowed(query_major):
        first = lax.broadcasted_iota(jnp.int32, (R, PAIR), 0) + core * R
        second = lax.broadcasted_iota(jnp.int32, (R, PAIR), 1)
        return first >= second if query_major else second >= first

    def forward(c, masked):
        for h in range(HEADS):
            s = mul_t(act_all[rows, head(Q_COL, h)], act_all[pair(c), head(K_COL, h)]) * scale
            a, slope = silu_parts(s)
            slope = slope * scale
            if masked:
                ok = allowed(True)
                a, slope = jnp.where(ok, a, 0.0), jnp.where(ok, slope, 0.0)
            g_v[c, h] = slope
            w_v[h] = a.astype(BF16)
        part = jnp.concatenate([mul(w_v[h], act_all[pair(c), head(V_COL, h)]) for h in range(HEADS)], axis=1)
        if masked:
            att_v[...] = part
        else:
            att_v[...] += part

    def forward_block(c, k):
        cols = pl.ds(pl.multiple_of(k * R, R), R)
        keys = block(c * 2 + k)
        for h in range(HEADS):
            a, slope = silu_parts(mul_t(act_all[rows, head(Q_COL, h)], act_all[keys, head(K_COL, h)]) * scale)
            g_v[c, h, :, cols] = slope * scale
            w_v[h, :, pl.ds(0, R)] = a.astype(BF16)
        att_v[...] += jnp.concatenate(
            [mul(w_v[h, :, pl.ds(0, R)], act_all[keys, head(V_COL, h)]) for h in range(HEADS)], axis=1
        )

    def prepare(c, masked):
        for h in range(HEADS):
            s = mul_t(act_all[rows, head(K_COL, h)], act_all[pair(c), head(Q_COL, h)]) * scale
            a, slope = silu_parts(s)
            slope = slope * scale
            if masked:
                ok = allowed(False)
                a, slope = jnp.where(ok, a, 0.0), jnp.where(ok, slope, 0.0)
            g_v[c + 1, h] = slope
            p_v[c, h] = a.astype(BF16)

    e_ring.wait_other(y)
    project(sib, V_COL, Q_COL, K_COL)
    c_ring.start(c_ring.second())
    forward(y, True)
    prepare(y, True)
    if Y > 1:
        e_ring.relay()
        e_ring.hand_near()

    def chip_at(t):
        return (y + 1 + (2 * t) % 3) % Y

    def near_step(t):
        c = chip_at(t)
        e_ring.wait_other(c)
        project_chip(c, other)

        @pl.when(c < y)
        def _():
            forward(c, False)

        @pl.when(c > y)
        def _():
            prepare(c, False)

    def far_step(k):
        project_chip(e_ring.f, k)

        @pl.when(e_ring.f < y)
        def _():
            forward_block(e_ring.f, k)

    if Y > 1:
        each(0, 2, lambda t: project_chip(chip_at(t), core))
    if X > 1:
        c_ring.relay()
    if Y > 1:
        each(0, 2, near_step)
        e_ring.hand_far()
        far_step(core)
    if X > 1:
        c_ring.hand_near()
    if Y > 1:
        e_ring.wait_other(e_ring.f)
        far_step(other)

        @pl.when(e_ring.f > y)
        def _():
            prepare(e_ring.f, False)

    att = att_v[...]
    cen = att - jnp.mean(att, axis=1, keepdims=True)
    inv = lax.rsqrt(jnp.mean(cen * cen, axis=1, keepdims=True) + EPSILON)
    normed = cen * inv
    gate = act_all[rows, pl.ds(U_COL, WIDTH)].astype(F32)
    gated = normed * gate

    turned = jnp.transpose(gated).reshape(Z, X, RD, R)
    for to in range(X):
        gt_send[to] = turned[:, to].reshape(Z * RD, R).astype(BF16)

    def gt_part(s):
        return gt_all.at[:, block(s)]

    def gt_piece(s):
        return pl.ds(pl.multiple_of((s % 2) * (ZH * RD), ZH * RD), ZH * RD)

    def gt_out(k):
        s = (mine + k) % S
        return pltpu.make_async_remote_copy(
            src_ref=gt_send.at[s // 2, gt_piece(s)], dst_ref=gt_part(mine),
            send_sem=gt_ssem.at[k], recv_sem=gt_rsem.at[mine],
            device_id=(z * X + s // 2, y * 2 + s % 2), device_id_type=MESH,
        )

    def gt_in(k):
        s = (mine + k) % S
        return pltpu.make_async_remote_copy(
            src_ref=gt_send.at[s // 2, gt_piece(s)], dst_ref=gt_part(s),
            send_sem=gt_ssem.at[k], recv_sem=gt_rsem.at[s],
            device_id=(z * X + s // 2, y * 2 + s % 2), device_id_type=MESH,
        )

    each(1, S, lambda k: gt_out(k).start())
    gt_all[:, block(mine)] = gt_send[x, gt_piece(mine), :]

    gg = gg_v[...]
    gn = gg * gate
    grad_att = (
        gn - jnp.mean(gn, axis=1, keepdims=True) - normed * jnp.mean(gn * normed, axis=1, keepdims=True)
    ) * inv * live
    do_all[rows, :] = grad_att.astype(BF16)

    def d_out(c):
        return remote(do_all, ctx, d_ssem.at[c], d_rsem, c * 2 + core)

    d_sib = remote(do_all, ctx, d_ssem.at[y], d_rsem, sib)
    d_sib.start()
    each(0, y, lambda c: d_out(c).start())


    c_ring.wait_other(x)
    if X > 1:
        c_ring.hand_far()
        each(1, X, lambda d: c_ring.wait_other((x + d) % X))
    each(1, S, lambda k: gt_in(k).wait_recv())
    gram = mul(gt_all[...], cot_all[...]).reshape(ZH, RD, D)
    z_send[...] = jnp.concatenate([gram[:, :, : D // 2], gram[:, :, D // 2 :]], axis=1).astype(BF16)

    def z_out(k):
        return pltpu.make_async_remote_copy(
            src_ref=z_send.at[k], dst_ref=z_recv.at[z], send_sem=z_ssem.at[k], recv_sem=z_rsem.at[z],
            device_id=((core * ZH + k) * X + x, ctx), device_id_type=MESH,
        )

    def z_in(k):
        return pltpu.make_async_remote_copy(
            src_ref=z_send.at[0], dst_ref=z_recv.at[k], send_sem=z_ssem.at[0], recv_sem=z_rsem.at[k],
            device_id=(k * X + x, ctx), device_id_type=MESH,
        )

    def z_start(distances):
        for d in distances:
            to = (z + d) % Z

            @pl.when(to // ZH == core)
            def _():
                z_out(to % ZH).start()

    z_order = sorted(range(1, Z), key=lambda d: -min(d, Z - d))
    z_start(z_order[:5])

    out[...] = mul(gated.astype(BF16), w_out_v[...]).astype(BF16)
    gu_v[...] = gg * normed
    z_start(z_order[5:9])

    dq_v[...] = jnp.zeros_like(dq_v)
    dk_v[...] = jnp.zeros_like(dk_v)
    dv_v[...] = jnp.zeros_like(dv_v)

    def query_step(c):
        for h in range(HEADS):
            gw = mul_t(do_all[rows, head(0, h)], act_all[pair(c), head(V_COL, h)])
            gs = (gw * g_v[c, h]).astype(BF16)
            dq_v[:, head(0, h)] += mul(gs, act_all[pair(c), head(K_COL, h)])

    each(0, y + 1, query_step)

    z_start(z_order[9:])

    def back(grad, base):
        cols = pl.ds(base, WIDTH)
        return mul_t((grad * slope_v[:, cols]).astype(BF16), w_in_v[:, cols])

    ge_v[...] = back(gu_v[...], U_COL) + back(dq_v[...], Q_COL)

    def key_step(c):
        for h in range(HEADS):
            do_h = do_all[pair(c), head(0, h)]
            gw = mul_t(act_all[rows, head(V_COL, h)], do_h)
            gs = (gw * g_v[c + 1, h]).astype(BF16)
            dv_v[:, head(0, h)] += mul(p_v[c, h], do_h)
            dk_v[:, head(0, h)] += mul(gs, act_all[pair(c), head(Q_COL, h)])

    arrived(do_all, sib, d_ssem, d_rsem)
    key_step(y)

    def hand_over(c):
        return remote(do_all, c * 2 + core, d_ssem.at[Y + c], d_rsem, sib)

    def later_chip(c):
        arrived(do_all, c * 2 + core, d_ssem, d_rsem)
        hand_over(c).start()
        arrived(do_all, c * 2 + other, d_ssem, d_rsem)
        key_step(c)

    each(y + 1, Y, later_chip)

    grad_events[...] = (ge_v[...] + back(dv_v[...], V_COL) + back(dk_v[...], K_COL)).astype(BF16)

    holder = z // ZH
    c_order = sorted(range(1, 2 * Y), key=lambda k: -min(k, 2 * Y - k))

    def c_out(k):
        return pltpu.make_async_remote_copy(
            src_ref=c_recv.at[y], dst_ref=c_recv.at[y], send_sem=c_ssem.at[k], recv_sem=c_rsem.at[y],
            device_id=(dp, (ctx + k) % (2 * Y)), device_id_type=MESH,
        )

    def c_in(k):
        return pltpu.make_async_remote_copy(
            src_ref=c_recv.at[k], dst_ref=c_recv.at[k], send_sem=c_ssem.at[0], recv_sem=c_rsem.at[k],
            device_id=(dp, sib), device_id_type=MESH,
        )

    e_ring.done()
    c_ring.done()
    d_sib.wait_send()
    each(0, y, lambda c: d_out(c).wait_send())
    each(y + 1, Y, lambda c: hand_over(c).wait_send())
    each(1, S, lambda k: gt_out(k).wait_send())

    def z_done(k):
        @pl.when(core * ZH + k != z)
        def _():
            z_out(k).wait_send()

    each(0, ZH, z_done)

    @pl.when(core == holder)
    def _():
        z_recv[z] = z_send[z % ZH]

        def wait_z(k):
            @pl.when(k != z)
            def _():
                z_in(k).wait_recv()

        each(0, Z, wait_z)
        total = jnp.sum(z_recv[...].astype(F32), axis=0)
        c_recv[y] = jnp.concatenate([total[:RD], total[RD:]], axis=1)
        for k in c_order:
            c_out(k).start()

    def wait_c(k):
        @pl.when(k * 2 + holder != ctx)
        def _():
            c_in(k).wait_recv()

    each(0, Y, wait_c)
    tokens = R * 2 * Y * Z * X
    grad_w_out[...] = jnp.sum(c_recv[...], axis=0) * (1.0 / math.sqrt(tokens))

    @pl.when(core == holder)
    def _():
        each(1, 2 * Y, lambda k: c_out(k).wait_send())


def in_hbm(a):
    return pltpu.with_memory_space_constraint(a, pltpu.HBM)


def store(*refs):
    copies = [pltpu.make_async_copy(refs[n], refs[3 + n], refs[6].at[n]) for n in range(3)]
    for copy in copies:
        copy.start()
    for copy in copies:
        copy.wait()


def build(mesh, X):
    Z, Y = mesh.shape["dp"] // X, mesh.shape["ctx"] // 2

    def per_device(events, keep, lengths, cotangent, w_in, w_out):
        R, D = events.shape[1:]
        L = R * 2 * Y
        S = 2 * X
        ZH, RD = Z // 2, D // (Z * X)
        vmem = pl.BlockSpec(memory_space=pltpu.VMEM)
        hbm = pl.BlockSpec(memory_space=pltpu.HBM)
        dma = pltpu.SemaphoreType.DMA
        output, grad_events, grad_w_out = pl.pallas_call(
            functools.partial(kernel, Z, X, Y),
            out_shape=(pltpu.VMEM((R, D), BF16), pltpu.VMEM((R, D), BF16), pltpu.VMEM((RD, D), F32)),
            in_specs=[hbm, hbm, pl.BlockSpec(memory_space=pltpu.SMEM), hbm, hbm, hbm],
            out_specs=[vmem] * 3,
            scratch_shapes=[
                pltpu.VMEM((1, R), jnp.int32),
                pltpu.VMEM((L, D), BF16),
                pltpu.VMEM((L, 4 * WIDTH), BF16),
                pltpu.VMEM((L, WIDTH), BF16),
                pltpu.VMEM((S * R, D), BF16),
                pltpu.VMEM((D, 4 * WIDTH), BF16),
                pltpu.VMEM((WIDTH, D), BF16),
                pltpu.VMEM((R, 4 * WIDTH), F32),
                pltpu.VMEM((R, WIDTH), F32),
                pltpu.VMEM((R, WIDTH), F32),
                pltpu.VMEM((R, WIDTH), F32),
                pltpu.VMEM((R, WIDTH), F32),
                pltpu.VMEM((R, WIDTH), F32),
                pltpu.VMEM((R, WIDTH), F32),
                pltpu.VMEM((R, D), F32),
                pltpu.VMEM((Y + 1, HEADS, R, 2 * R), F32),
                pltpu.VMEM((Y, HEADS, R, 2 * R), BF16),
                pltpu.VMEM((HEADS, R, 2 * R), BF16),
                pltpu.VMEM((X, Z * RD, R), BF16),
                pltpu.VMEM((ZH * RD, S * R), BF16),
                pltpu.VMEM((ZH, 2 * RD, D // 2), BF16),
                pltpu.VMEM((Z, 2 * RD, D // 2), BF16),
                pltpu.VMEM((Y, RD, D), F32),
                dma((8,)),
                dma((20,)), dma((6 * Y,)),
                dma((2 * Y,)), dma((2 * Y,)),
                dma((20,)), dma((6 * X,)),
                dma((S,)), dma((S,)),
                dma((ZH,)), dma((Z,)),
                dma((2 * Y,)), dma((Y,)),
            ],
            compiler_params=pltpu.CompilerParams(
                collective_id=0, has_side_effects=True, vmem_limit_bytes=56 * 1024 * 1024
            ),
            name="layer",
        )(in_hbm(events[0]), in_hbm(keep), lengths, in_hbm(cotangent[0]), in_hbm(w_in), in_hbm(w_out))
        output, grad_events, grad_w_out = pl.pallas_call(
            store,
            out_shape=(
                jax.ShapeDtypeStruct((R, D), BF16),
                jax.ShapeDtypeStruct((R, D), BF16),
                jax.ShapeDtypeStruct((RD, D), F32),
            ),
            in_specs=[vmem] * 3,
            out_specs=(hbm, hbm, hbm),
            scratch_shapes=[dma((3,))],
            name="store",
        )(*[pltpu.with_memory_space_constraint(a, pltpu.VMEM) for a in (output, grad_events, grad_w_out)])
        return (output[None], grad_events[None], grad_w_out)

    return jax.shard_map(
        per_device,
        mesh=mesh,
        in_specs=(P("dp", "ctx", None), P("dp", "ctx"), P("dp"), P("dp", "ctx", None), P(), P()),
        out_specs=(P("dp", "ctx", None), P("dp", "ctx", None), P("dp", None)),
        check_vma=False,
    )


def solution(mesh):
    return build(mesh, X_CHIPS)
```

```python
import functools
import math

import jax
import jax.numpy as jnp
from jax import lax
from jax.experimental import pallas as pl
from jax.experimental.pallas import tpu as pltpu
from jax.sharding import PartitionSpec as P

HEADS = 4
DH = 128
WIDTH = HEADS * DH
X_CHIPS = 4
EPSILON = 1e-06
MESH = pl.DeviceIdType.MESH
F32 = jnp.float32
BF16 = jnp.bfloat16
U_COL, V_COL, Q_COL, K_COL = 0, WIDTH, 2 * WIDTH, 3 * WIDTH


def silu_parts(v):
    s = 0.5 * jnp.tanh(0.5 * v) + 0.5
    a = v * s
    return a, s + a * (1.0 - s)


def mul(a, b):
    return jnp.dot(a, b, preferred_element_type=F32)


def mul_t(a, b):
    return lax.dot_general(a, b, (((1,), (1,)), ((), ())), preferred_element_type=F32)


class Ring:
    def __init__(self, buf, rows, n, pos, core, ssem, rsem, place):
        self.buf, self.rows, self.n, self.pos, self.core = buf, rows, n, pos, core
        self.ssem, self.rsem = ssem, rsem
        self.sib = place(pos, 1 - core)
        self.right, self.left = place((pos + 1) % n, core), place((pos + n - 1) % n, core)
        self.l, self.r, self.f = (pos + n - 1) % n, (pos + 1) % n, (pos + 2) % n

    def copy(self, chip, core, first, count, k, sem, to):
        rows = self.rows // 4
        start = pl.multiple_of((chip * 2 + core) * self.rows + first * rows, rows)
        part = self.buf.at[pl.ds(start, count * rows)]
        return pltpu.make_async_remote_copy(
            src_ref=part, dst_ref=part, send_sem=self.ssem.at[k], recv_sem=self.rsem.at[sem],
            device_id=to, device_id_type=MESH,
        )

    def quarter(self, chip, q, k, to):
        return self.copy(chip, self.core, q, 1, k, chip * 4 + q, to)

    def hand(self, chip, half, k):
        return self.copy(chip, self.core, half * 2, 2, k, 4 * self.n + chip * 2 + half, self.sib)

    def first(self):
        near = []
        if self.n > 1:
            for n in range(2):
                near.append(self.quarter(self.pos, n, 2 + n, self.right))
                near.append(self.quarter(self.pos, n + 2, 6 + n, self.left))
        return near + [self.hand(self.pos, half, half) for half in range(2)]

    def second(self):
        near = []
        if self.n > 1:
            for n in range(2):
                near.append(self.quarter(self.pos, n + 2, 4 + n, self.right))
                near.append(self.quarter(self.pos, n, 8 + n, self.left))
        return near

    def passed(self):
        steps = []
        for n in range(2):
            steps.append((self.l, n, self.quarter(self.l, n, 10 + n, self.right)))
            steps.append((self.r, 2 + n, self.quarter(self.r, 2 + n, 12 + n, self.left)))
        return steps

    def wait(self, chip, first, count=1):
        for q in range(first, first + count):
            self.quarter(chip, q, 0, self.sib).wait_recv()

    def wait_other(self, chip):
        for half in range(2):
            self.copy(chip, 1 - self.core, half * 2, 2, 0, 4 * self.n + chip * 2 + half, self.sib).wait_recv()

    def start(self, copies):
        for copy in copies:
            copy.start()

    def relay(self):
        for chip, q, copy in self.passed():
            self.wait(chip, q)
            copy.start()

    def hand_near(self):
        self.hand(self.l, 0, 14).start()
        self.hand(self.r, 1, 17).start()
        self.wait(self.l, 2, 2)
        self.hand(self.l, 1, 15).start()
        self.wait(self.r, 0, 2)
        self.hand(self.r, 0, 16).start()

    def hand_far(self):
        for half in range(2):
            self.wait(self.f, half * 2, 2)
            self.hand(self.f, half, 18 + half).start()

    def done(self):
        for copy in self.first() + self.second():
            copy.wait_send()
        if self.n > 1:
            for _, _, copy in self.passed():
                copy.wait_send()
            for n, chip in enumerate((self.l, self.r, self.f)):
                for half in range(2):
                    self.hand(chip, half, 14 + 2 * n + half).wait_send()


def kernel(
    Z, X, Y,
    events, keep, lengths, cotangent, w_in, w_out,
    out, grad_events, grad_w_out,
    keep_v, e_all, act_all, do_all, cot_all, w_in_v, w_out_v, slope_v, gg_v, gu_v, att_v, dq_v, dk_v, dv_v, ge_v,
    g_v, p_v, w_v, gt_send, gt_all, z_send, z_recv, c_recv,
    plane_sem, z_sem, local_sem, e_ssem, e_rsem, d_ssem, d_rsem, cot_ssem, cot_rsem, gt_ssem, gt_rsem, z_ssem, z_rsem, c_ssem, c_rsem,
):
    R = events.shape[0]
    D = events.shape[1]
    PAIR = 2 * R
    S = 2 * X
    ZH = Z // 2
    RD = D // (Z * X)
    scale = 1.0 / math.sqrt(DH)
    dp, ctx = lax.axis_index("dp"), lax.axis_index("ctx")
    z, x = dp // X, dp % X
    y, core = ctx // 2, ctx % 2
    other = 1 - core
    sib = y * 2 + other
    mine = x * 2 + core

    def block(b):
        return pl.ds(pl.multiple_of(b * R, R), R)

    def pair(c):
        return pl.ds(pl.multiple_of(c * PAIR, PAIR), PAIR)

    rows = block(ctx)

    ev_copy = pltpu.make_async_copy(events, e_all.at[rows], local_sem.at[0])
    ev_copy.start()
    keep_copy = pltpu.make_async_copy(keep, keep_v, local_sem.at[7])
    keep_copy.start()
    barrier = pltpu.get_barrier_semaphore()

    def greet(dp_to, ctx_to):
        pl.semaphore_signal(barrier, inc=1, device_id=(dp_to, ctx_to), device_id_type=MESH)

    for k in range(1, Y):
        greet(dp, ((y + k) % Y) * 2)
    for k in range(1, X):
        greet(z * X + (x + k) % X, y * 2)

    @pl.when(core == 1)
    def _():
        greet(dp, y * 2)

    @pl.when(core == z // ZH)
    def _():
        for k in range(1, Z):
            greet(((z + k) % Z) * X + x, y * 2 + 1)

    cot_copy = pltpu.make_async_copy(cotangent, cot_all.at[block(mine)], local_sem.at[1])
    cot_copy.start()
    w_copies = []
    for g in range(4):
        cols = pl.ds(g * WIDTH, WIDTH)
        w_copies.append(pltpu.make_async_copy(w_in.at[:, cols], w_in_v.at[:, cols], local_sem.at[2 + g]))
    for copy in w_copies:
        copy.start()
    wo_copy = pltpu.make_async_copy(w_out, w_out_v, local_sem.at[6])
    wo_copy.start()

    ev_copy.wait()
    keep_copy.wait()
    lane = lax.broadcasted_iota(jnp.int32, (1, R), 1)
    live_row = jnp.where((keep_v[...] == 1) & (ctx * R + lane < lengths[0]), 1.0, 0.0)
    eye = lax.broadcasted_iota(jnp.int32, (R, R), 0) == lax.broadcasted_iota(jnp.int32, (R, R), 1)
    live = jnp.sum(jnp.where(eye, live_row, 0.0), axis=1, keepdims=True)
    e_all[rows, :] = (e_all[rows, :].astype(F32) * live).astype(BF16)

    @pl.when(core == 0)
    def _():
        pl.semaphore_wait(barrier, 2 * (Y - 1) + 2 * (X - 1) + 1)
        pl.semaphore_signal(plane_sem, inc=1, device_id=(dp, sib), device_id_type=MESH)

    @pl.when(core == 1)
    def _():
        pl.semaphore_wait(plane_sem, 1)


    def remote(buf, b, ssem, rsem, ctx_to):
        return pltpu.make_async_remote_copy(
            src_ref=buf.at[block(b)], dst_ref=buf.at[block(b)], send_sem=ssem, recv_sem=rsem.at[b],
            device_id=(dp, ctx_to), device_id_type=MESH,
        )

    def arrived(buf, b, ssem, rsem):
        remote(buf, b, ssem.at[0], rsem, sib).wait_recv()

    def each(low, high, body):
        def step(k, _):
            body(k)
            return _
        lax.fori_loop(low, high, step, 0)

    e_ring = Ring(e_all, R, Y, y, core, e_ssem, e_rsem, lambda chip, c: (dp, chip * 2 + c))
    c_ring = Ring(cot_all, R, X, x, core, cot_ssem, cot_rsem, lambda chip, c: (z * X + chip, y * 2 + c))
    e_ring.start(e_ring.first())
    cot_copy.wait()

    own = e_all[rows, :]
    for g in range(4):
        w_copies[g].wait()
        for half in range(2):
            cols = pl.ds(g * WIDTH + half * 256, 256)
            a, slope = silu_parts(mul(own, w_in_v[:, cols]))
            act_all[rows, cols] = a.astype(BF16)
            slope_v[:, cols] = slope
    e_ring.start(e_ring.second())
    c_ring.start(c_ring.first())
    wo_copy.wait()
    gg_v[...] = mul_t(cot_all[block(mine), :], w_out_v[...])

    def project(b, *bases):
        for base in bases:
            for half in range(2):
                cols = pl.ds(base + half * 256, 256)
                a, _ = silu_parts(mul(e_all[block(b), :], w_in_v[:, cols]))
                act_all[block(b), cols] = a.astype(BF16)

    def project_chip(c, k):
        @pl.when(c < y)
        def _():
            project(c * 2 + k, V_COL, K_COL)

        @pl.when(c > y)
        def _():
            project(c * 2 + k, Q_COL)

    def head(base, h):
        return pl.ds(base + h * DH, DH)

    def allowed(query_major):
        first = lax.broadcasted_iota(jnp.int32, (R, PAIR), 0) + core * R
        second = lax.broadcasted_iota(jnp.int32, (R, PAIR), 1)
        return first >= second if query_major else second >= first

    def forward(c, masked):
        for h in range(HEADS):
            s = mul_t(act_all[rows, head(Q_COL, h)], act_all[pair(c), head(K_COL, h)]) * scale
            a, slope = silu_parts(s)
            slope = slope * scale
            if masked:
                ok = allowed(True)
                a, slope = jnp.where(ok, a, 0.0), jnp.where(ok, slope, 0.0)
            g_v[c, h] = slope
            w_v[h] = a.astype(BF16)
        part = jnp.concatenate([mul(w_v[h], act_all[pair(c), head(V_COL, h)]) for h in range(HEADS)], axis=1)
        if masked:
            att_v[...] = part
        else:
            att_v[...] += part

    def forward_block(c, k):
        cols = pl.ds(pl.multiple_of(k * R, R), R)
        keys = block(c * 2 + k)
        for h in range(HEADS):
            a, slope = silu_parts(mul_t(act_all[rows, head(Q_COL, h)], act_all[keys, head(K_COL, h)]) * scale)
            g_v[c, h, :, cols] = slope * scale
            w_v[h, :, pl.ds(0, R)] = a.astype(BF16)
        att_v[...] += jnp.concatenate(
            [mul(w_v[h, :, pl.ds(0, R)], act_all[keys, head(V_COL, h)]) for h in range(HEADS)], axis=1
        )

    def prepare(c, masked):
        for h in range(HEADS):
            s = mul_t(act_all[rows, head(K_COL, h)], act_all[pair(c), head(Q_COL, h)]) * scale
            a, slope = silu_parts(s)
            slope = slope * scale
            if masked:
                ok = allowed(False)
                a, slope = jnp.where(ok, a, 0.0), jnp.where(ok, slope, 0.0)
            g_v[c + 1, h] = slope
            p_v[c, h] = a.astype(BF16)

    e_ring.wait_other(y)
    project(sib, V_COL, Q_COL, K_COL)
    c_ring.start(c_ring.second())
    forward(y, True)
    prepare(y, True)
    if Y > 1:
        e_ring.relay()
        e_ring.hand_near()

    def chip_at(t):
        return (y + 1 + (2 * t) % 3) % Y

    def near_step(t):
        c = chip_at(t)
        e_ring.wait_other(c)
        project_chip(c, other)

        @pl.when(c < y)
        def _():
            forward(c, False)

        @pl.when(c > y)
        def _():
            prepare(c, False)

    def far_step(k):
        project_chip(e_ring.f, k)

        @pl.when(e_ring.f < y)
        def _():
            forward_block(e_ring.f, k)

    if Y > 1:
        each(0, 2, lambda t: project_chip(chip_at(t), core))
    if X > 1:
        c_ring.relay()
    if Y > 1:
        each(0, 2, near_step)
        e_ring.hand_far()
        far_step(core)
    if X > 1:
        c_ring.hand_near()
    if Y > 1:
        e_ring.wait_other(e_ring.f)
        far_step(other)

        @pl.when(e_ring.f > y)
        def _():
            prepare(e_ring.f, False)

    att = att_v[...]
    cen = att - jnp.mean(att, axis=1, keepdims=True)
    inv = lax.rsqrt(jnp.mean(cen * cen, axis=1, keepdims=True) + EPSILON)
    normed = cen * inv
    gate = act_all[rows, pl.ds(U_COL, WIDTH)].astype(F32)
    gated = normed * gate

    turned = jnp.transpose(gated).reshape(Z, X, RD, R)
    for to in range(X):
        gt_send[to] = turned[:, to].reshape(Z * RD, R).astype(BF16)

    def gt_part(s):
        return gt_all.at[:, block(s)]

    def gt_piece(s):
        return pl.ds(pl.multiple_of((s % 2) * (ZH * RD), ZH * RD), ZH * RD)

    def gt_out(k):
        s = (mine + k) % S
        return pltpu.make_async_remote_copy(
            src_ref=gt_send.at[s // 2, gt_piece(s)], dst_ref=gt_part(mine),
            send_sem=gt_ssem.at[k], recv_sem=gt_rsem.at[mine],
            device_id=(z * X + s // 2, y * 2 + s % 2), device_id_type=MESH,
        )

    def gt_in(k):
        s = (mine + k) % S
        return pltpu.make_async_remote_copy(
            src_ref=gt_send.at[s // 2, gt_piece(s)], dst_ref=gt_part(s),
            send_sem=gt_ssem.at[k], recv_sem=gt_rsem.at[s],
            device_id=(z * X + s // 2, y * 2 + s % 2), device_id_type=MESH,
        )

    each(1, S, lambda k: gt_out(k).start())
    gt_all[:, block(mine)] = gt_send[x, gt_piece(mine), :]

    gg = gg_v[...]
    gn = gg * gate
    grad_att = (
        gn - jnp.mean(gn, axis=1, keepdims=True) - normed * jnp.mean(gn * normed, axis=1, keepdims=True)
    ) * inv * live
    do_all[rows, :] = grad_att.astype(BF16)

    def d_out(c):
        return remote(do_all, ctx, d_ssem.at[c], d_rsem, c * 2 + core)

    d_sib = remote(do_all, ctx, d_ssem.at[y], d_rsem, sib)
    d_sib.start()
    each(0, y, lambda c: d_out(c).start())


    @pl.when(core == 1)
    def _():
        pl.semaphore_wait(barrier, Z - 1)
        pl.semaphore_signal(z_sem, inc=1, device_id=(dp, sib), device_id_type=MESH)

    c_ring.wait_other(x)
    if X > 1:
        c_ring.hand_far()
        each(1, X, lambda d: c_ring.wait_other((x + d) % X))
    each(1, S, lambda k: gt_in(k).wait_recv())
    gram = mul(gt_all[...], cot_all[...]).reshape(ZH, RD, D)
    z_send[...] = jnp.concatenate([gram[:, :, : D // 2], gram[:, :, D // 2 :]], axis=1).astype(BF16)

    def z_out(k):
        return pltpu.make_async_remote_copy(
            src_ref=z_send.at[k], dst_ref=z_recv.at[z], send_sem=z_ssem.at[k], recv_sem=z_rsem.at[z],
            device_id=((core * ZH + k) * X + x, ctx), device_id_type=MESH,
        )

    def z_in(k):
        return pltpu.make_async_remote_copy(
            src_ref=z_send.at[0], dst_ref=z_recv.at[k], send_sem=z_ssem.at[0], recv_sem=z_rsem.at[k],
            device_id=(k * X + x, ctx), device_id_type=MESH,
        )

    def z_start(distances):
        for d in distances:
            to = (z + d) % Z

            @pl.when(to // ZH == core)
            def _():
                z_out(to % ZH).start()

    z_order = sorted(range(1, Z), key=lambda d: -min(d, Z - d))

    @pl.when(core == 0)
    def _():
        pl.semaphore_wait(z_sem, 1)

    z_start(z_order[:5])

    out[...] = mul(gated.astype(BF16), w_out_v[...]).astype(BF16)
    gu_v[...] = gg * normed
    z_start(z_order[5:9])

    dq_v[...] = jnp.zeros_like(dq_v)
    dk_v[...] = jnp.zeros_like(dk_v)
    dv_v[...] = jnp.zeros_like(dv_v)

    def query_step(c):
        for h in range(HEADS):
            gw = mul_t(do_all[rows, head(0, h)], act_all[pair(c), head(V_COL, h)])
            gs = (gw * g_v[c, h]).astype(BF16)
            dq_v[:, head(0, h)] += mul(gs, act_all[pair(c), head(K_COL, h)])

    each(0, y + 1, query_step)

    z_start(z_order[9:])

    def back(grad, base):
        cols = pl.ds(base, WIDTH)
        return mul_t((grad * slope_v[:, cols]).astype(BF16), w_in_v[:, cols])

    ge_v[...] = back(gu_v[...], U_COL) + back(dq_v[...], Q_COL)

    def key_step(c):
        for h in range(HEADS):
            do_h = do_all[pair(c), head(0, h)]
            gw = mul_t(act_all[rows, head(V_COL, h)], do_h)
            gs = (gw * g_v[c + 1, h]).astype(BF16)
            dv_v[:, head(0, h)] += mul(p_v[c, h], do_h)
            dk_v[:, head(0, h)] += mul(gs, act_all[pair(c), head(Q_COL, h)])

    arrived(do_all, sib, d_ssem, d_rsem)
    key_step(y)

    def hand_over(c):
        return remote(do_all, c * 2 + core, d_ssem.at[Y + c], d_rsem, sib)

    def later_chip(c):
        arrived(do_all, c * 2 + core, d_ssem, d_rsem)
        hand_over(c).start()
        arrived(do_all, c * 2 + other, d_ssem, d_rsem)
        key_step(c)

    each(y + 1, Y, later_chip)

    grad_events[...] = (ge_v[...] + back(dv_v[...], V_COL) + back(dk_v[...], K_COL)).astype(BF16)

    holder = z // ZH
    c_order = sorted(range(1, 2 * Y), key=lambda k: -min(k, 2 * Y - k))

    def c_out(k):
        return pltpu.make_async_remote_copy(
            src_ref=c_recv.at[y], dst_ref=c_recv.at[y], send_sem=c_ssem.at[k], recv_sem=c_rsem.at[y],
            device_id=(dp, (ctx + k) % (2 * Y)), device_id_type=MESH,
        )

    def c_in(k):
        return pltpu.make_async_remote_copy(
            src_ref=c_recv.at[k], dst_ref=c_recv.at[k], send_sem=c_ssem.at[0], recv_sem=c_rsem.at[k],
            device_id=(dp, sib), device_id_type=MESH,
        )

    e_ring.done()
    c_ring.done()
    d_sib.wait_send()
    each(0, y, lambda c: d_out(c).wait_send())
    each(y + 1, Y, lambda c: hand_over(c).wait_send())
    each(1, S, lambda k: gt_out(k).wait_send())

    def z_done(k):
        @pl.when(core * ZH + k != z)
        def _():
            z_out(k).wait_send()

    each(0, ZH, z_done)

    @pl.when(core == holder)
    def _():
        z_recv[z] = z_send[z % ZH]

        def wait_z(k):
            @pl.when(k != z)
            def _():
                z_in(k).wait_recv()

        each(0, Z, wait_z)
        total = jnp.sum(z_recv[...].astype(F32), axis=0)
        c_recv[y] = jnp.concatenate([total[:RD], total[RD:]], axis=1)
        for k in c_order:
            c_out(k).start()

    def wait_c(k):
        @pl.when(k * 2 + holder != ctx)
        def _():
            c_in(k).wait_recv()

    each(0, Y, wait_c)
    tokens = R * 2 * Y * Z * X
    grad_w_out[...] = jnp.sum(c_recv[...], axis=0) * (1.0 / math.sqrt(tokens))

    @pl.when(core == holder)
    def _():
        each(1, 2 * Y, lambda k: c_out(k).wait_send())


def in_hbm(a):
    return pltpu.with_memory_space_constraint(a, pltpu.HBM)


def store(*refs):
    copies = [pltpu.make_async_copy(refs[n], refs[3 + n], refs[6].at[n]) for n in range(3)]
    for copy in copies:
        copy.start()
    for copy in copies:
        copy.wait()


def build(mesh, X):
    Z, Y = mesh.shape["dp"] // X, mesh.shape["ctx"] // 2

    def per_device(events, keep, lengths, cotangent, w_in, w_out):
        R, D = events.shape[1:]
        L = R * 2 * Y
        S = 2 * X
        ZH, RD = Z // 2, D // (Z * X)
        vmem = pl.BlockSpec(memory_space=pltpu.VMEM)
        hbm = pl.BlockSpec(memory_space=pltpu.HBM)
        dma = pltpu.SemaphoreType.DMA
        output, grad_events, grad_w_out = pl.pallas_call(
            functools.partial(kernel, Z, X, Y),
            out_shape=(pltpu.VMEM((R, D), BF16), pltpu.VMEM((R, D), BF16), pltpu.VMEM((RD, D), F32)),
            in_specs=[hbm, hbm, pl.BlockSpec(memory_space=pltpu.SMEM), hbm, hbm, hbm],
            out_specs=[vmem] * 3,
            scratch_shapes=[
                pltpu.VMEM((1, R), jnp.int32),
                pltpu.VMEM((L, D), BF16),
                pltpu.VMEM((L, 4 * WIDTH), BF16),
                pltpu.VMEM((L, WIDTH), BF16),
                pltpu.VMEM((S * R, D), BF16),
                pltpu.VMEM((D, 4 * WIDTH), BF16),
                pltpu.VMEM((WIDTH, D), BF16),
                pltpu.VMEM((R, 4 * WIDTH), F32),
                pltpu.VMEM((R, WIDTH), F32),
                pltpu.VMEM((R, WIDTH), F32),
                pltpu.VMEM((R, WIDTH), F32),
                pltpu.VMEM((R, WIDTH), F32),
                pltpu.VMEM((R, WIDTH), F32),
                pltpu.VMEM((R, WIDTH), F32),
                pltpu.VMEM((R, D), F32),
                pltpu.VMEM((Y + 1, HEADS, R, 2 * R), F32),
                pltpu.VMEM((Y, HEADS, R, 2 * R), BF16),
                pltpu.VMEM((HEADS, R, 2 * R), BF16),
                pltpu.VMEM((X, Z * RD, R), BF16),
                pltpu.VMEM((ZH * RD, S * R), BF16),
                pltpu.VMEM((ZH, 2 * RD, D // 2), BF16),
                pltpu.VMEM((Z, 2 * RD, D // 2), BF16),
                pltpu.VMEM((Y, RD, D), F32),
                pltpu.SemaphoreType.REGULAR, pltpu.SemaphoreType.REGULAR,
                dma((8,)),
                dma((20,)), dma((6 * Y,)),
                dma((2 * Y,)), dma((2 * Y,)),
                dma((20,)), dma((6 * X,)),
                dma((S,)), dma((S,)),
                dma((ZH,)), dma((Z,)),
                dma((2 * Y,)), dma((Y,)),
            ],
            compiler_params=pltpu.CompilerParams(
                collective_id=0, has_side_effects=True, vmem_limit_bytes=56 * 1024 * 1024
            ),
            name="layer",
        )(in_hbm(events[0]), in_hbm(keep), lengths, in_hbm(cotangent[0]), in_hbm(w_in), in_hbm(w_out))
        output, grad_events, grad_w_out = pl.pallas_call(
            store,
            out_shape=(
                jax.ShapeDtypeStruct((R, D), BF16),
                jax.ShapeDtypeStruct((R, D), BF16),
                jax.ShapeDtypeStruct((RD, D), F32),
            ),
            in_specs=[vmem] * 3,
            out_specs=(hbm, hbm, hbm),
            scratch_shapes=[dma((3,))],
            name="store",
        )(*[pltpu.with_memory_space_constraint(a, pltpu.VMEM) for a in (output, grad_events, grad_w_out)])
        return (output[None], grad_events[None], grad_w_out)

    return jax.shard_map(
        per_device,
        mesh=mesh,
        in_specs=(P("dp", "ctx", None), P("dp", "ctx"), P("dp"), P("dp", "ctx", None), P(), P()),
        out_specs=(P("dp", "ctx", None), P("dp", "ctx", None), P("dp", None)),
        check_vma=False,
    )


def solution(mesh):
    return build(mesh, X_CHIPS)
```

```python
import functools
import math

import jax
import jax.numpy as jnp
from jax import lax
from jax.experimental import pallas as pl
from jax.experimental.pallas import tpu as pltpu
from jax.sharding import PartitionSpec as P

HEADS = 4
DH = 128
WIDTH = HEADS * DH
X_CHIPS = 4
EPSILON = 1e-06
MESH = pl.DeviceIdType.MESH
F32 = jnp.float32
BF16 = jnp.bfloat16
U_COL, V_COL, Q_COL, K_COL = 0, WIDTH, 2 * WIDTH, 3 * WIDTH


def silu_parts(v):
    s = 0.5 * jnp.tanh(0.5 * v) + 0.5
    a = v * s
    return a, s + a * (1.0 - s)


def mul(a, b):
    return jnp.dot(a, b, preferred_element_type=F32)


def mul_t(a, b):
    return lax.dot_general(a, b, (((1,), (1,)), ((), ())), preferred_element_type=F32)


class Ring:
    def __init__(self, buf, rows, n, pos, core, ssem, rsem, place):
        self.buf, self.rows, self.n, self.pos, self.core = buf, rows, n, pos, core
        self.ssem, self.rsem = ssem, rsem
        self.sib = place(pos, 1 - core)
        self.right, self.left = place((pos + 1) % n, core), place((pos + n - 1) % n, core)
        self.l, self.r, self.f = (pos + n - 1) % n, (pos + 1) % n, (pos + 2) % n

    def copy(self, chip, core, first, count, k, sem, to):
        rows = self.rows // 4
        start = pl.multiple_of((chip * 2 + core) * self.rows + first * rows, rows)
        part = self.buf.at[pl.ds(start, count * rows)]
        return pltpu.make_async_remote_copy(
            src_ref=part, dst_ref=part, send_sem=self.ssem.at[k], recv_sem=self.rsem.at[sem],
            device_id=to, device_id_type=MESH,
        )

    def quarter(self, chip, q, k, to):
        return self.copy(chip, self.core, q, 1, k, chip * 4 + q, to)

    def hand(self, chip, half, k):
        return self.copy(chip, self.core, half * 2, 2, k, 4 * self.n + chip * 2 + half, self.sib)

    def first(self):
        near = []
        if self.n > 1:
            for n in range(2):
                near.append(self.quarter(self.pos, n, 2 + n, self.right))
                near.append(self.quarter(self.pos, n + 2, 6 + n, self.left))
        return near + [self.hand(self.pos, half, half) for half in range(2)]

    def second(self):
        near = []
        if self.n > 1:
            for n in range(2):
                near.append(self.quarter(self.pos, n + 2, 4 + n, self.right))
                near.append(self.quarter(self.pos, n, 8 + n, self.left))
        return near

    def passed(self):
        steps = []
        for n in range(2):
            steps.append((self.l, n, self.quarter(self.l, n, 10 + n, self.right)))
            steps.append((self.r, 2 + n, self.quarter(self.r, 2 + n, 12 + n, self.left)))
        return steps

    def wait(self, chip, first, count=1):
        for q in range(first, first + count):
            self.quarter(chip, q, 0, self.sib).wait_recv()

    def wait_other(self, chip):
        for half in range(2):
            self.copy(chip, 1 - self.core, half * 2, 2, 0, 4 * self.n + chip * 2 + half, self.sib).wait_recv()

    def start(self, copies):
        for copy in copies:
            copy.start()

    def relay(self):
        for chip, q, copy in self.passed():
            self.wait(chip, q)
            copy.start()

    def hand_near(self):
        self.hand(self.l, 0, 14).start()
        self.hand(self.r, 1, 17).start()
        self.wait(self.l, 2, 2)
        self.hand(self.l, 1, 15).start()
        self.wait(self.r, 0, 2)
        self.hand(self.r, 0, 16).start()

    def hand_far(self):
        for half in range(2):
            self.wait(self.f, half * 2, 2)
            self.hand(self.f, half, 18 + half).start()

    def done(self):
        for copy in self.first() + self.second():
            copy.wait_send()
        if self.n > 1:
            for _, _, copy in self.passed():
                copy.wait_send()
            for n, chip in enumerate((self.l, self.r, self.f)):
                for half in range(2):
                    self.hand(chip, half, 14 + 2 * n + half).wait_send()


class Star:
    def __init__(self, buf, rows, n, pos, core, ssem, rsem, place):
        self.buf, self.rows, self.n, self.pos, self.core = buf, rows, n, pos, core
        self.ssem, self.rsem, self.place = ssem, rsem, place

    def copy(self, chip, core, k, sem, to):
        start = pl.multiple_of((chip * 2 + core) * self.rows, self.rows)
        part = self.buf.at[pl.ds(start, self.rows)]
        return pltpu.make_async_remote_copy(
            src_ref=part, dst_ref=part, send_sem=self.ssem.at[k], recv_sem=self.rsem.at[sem],
            device_id=to, device_id_type=MESH,
        )

    def out(self, d):
        return self.copy(self.pos, self.core, d, self.pos, self.place((self.pos + d) % self.n, self.core))

    def hand(self, d):
        chip = (self.pos + d) % self.n
        return self.copy(chip, self.core, self.n + d, self.n + chip, self.place(self.pos, 1 - self.core))

    def start(self):
        for d in range(1, self.n):
            self.out(d).start()
        self.hand(0).start()

    def hand_over(self):
        for d in range(1, self.n):
            chip = (self.pos + d) % self.n
            self.copy(chip, self.core, 0, chip, self.place(self.pos, self.core)).wait_recv()
            self.hand(d).start()

    def wait_other(self):
        for d in range(self.n):
            chip = (self.pos + d) % self.n
            self.copy(chip, 1 - self.core, 0, self.n + chip, self.place(self.pos, self.core)).wait_recv()

    def done(self):
        for d in range(1, self.n):
            self.out(d).wait_send()
        for d in range(self.n):
            self.hand(d).wait_send()


def kernel(
    Z, X, Y,
    events, keep, lengths, cotangent, w_in, w_out,
    out, grad_events, grad_w_out,
    keep_v, e_all, act_all, do_all, cot_all, w_in_v, w_out_v, slope_v, gg_v, gu_v, att_v, dq_v, dk_v, dv_v, ge_v,
    g_v, p_v, w_v, gt_send, gt_all, z_send, z_recv, c_recv,
    plane_sem, z_sem, local_sem, e_ssem, e_rsem, d_ssem, d_rsem, cot_ssem, cot_rsem, gt_ssem, gt_rsem, z_ssem, z_rsem, c_ssem, c_rsem,
):
    R = events.shape[0]
    D = events.shape[1]
    PAIR = 2 * R
    S = 2 * X
    ZH = Z // 2
    RD = D // (Z * X)
    scale = 1.0 / math.sqrt(DH)
    dp, ctx = lax.axis_index("dp"), lax.axis_index("ctx")
    z, x = dp // X, dp % X
    y, core = ctx // 2, ctx % 2
    other = 1 - core
    sib = y * 2 + other
    mine = x * 2 + core

    def block(b):
        return pl.ds(pl.multiple_of(b * R, R), R)

    def pair(c):
        return pl.ds(pl.multiple_of(c * PAIR, PAIR), PAIR)

    rows = block(ctx)

    ev_copy = pltpu.make_async_copy(events, e_all.at[rows], local_sem.at[0])
    ev_copy.start()
    keep_copy = pltpu.make_async_copy(keep, keep_v, local_sem.at[7])
    keep_copy.start()
    barrier = pltpu.get_barrier_semaphore()

    def greet(dp_to, ctx_to):
        pl.semaphore_signal(barrier, inc=1, device_id=(dp_to, ctx_to), device_id_type=MESH)

    for k in range(1, Y):
        greet(dp, ((y + k) % Y) * 2)
    for k in range(1, X):
        greet(z * X + (x + k) % X, y * 2)

    @pl.when(core == 1)
    def _():
        greet(dp, y * 2)

    @pl.when(core == z // ZH)
    def _():
        for k in range(1, Z):
            greet(((z + k) % Z) * X + x, y * 2 + 1)

    cot_copy = pltpu.make_async_copy(cotangent, cot_all.at[block(mine)], local_sem.at[1])
    cot_copy.start()
    w_copies = []
    for g in range(4):
        cols = pl.ds(g * WIDTH, WIDTH)
        w_copies.append(pltpu.make_async_copy(w_in.at[:, cols], w_in_v.at[:, cols], local_sem.at[2 + g]))
    for copy in w_copies:
        copy.start()
    wo_copy = pltpu.make_async_copy(w_out, w_out_v, local_sem.at[6])
    wo_copy.start()

    ev_copy.wait()
    keep_copy.wait()
    lane = lax.broadcasted_iota(jnp.int32, (1, R), 1)
    live_row = jnp.where((keep_v[...] == 1) & (ctx * R + lane < lengths[0]), 1.0, 0.0)
    eye = lax.broadcasted_iota(jnp.int32, (R, R), 0) == lax.broadcasted_iota(jnp.int32, (R, R), 1)
    live = jnp.sum(jnp.where(eye, live_row, 0.0), axis=1, keepdims=True)
    e_all[rows, :] = (e_all[rows, :].astype(F32) * live).astype(BF16)

    @pl.when(core == 0)
    def _():
        pl.semaphore_wait(barrier, 2 * (Y - 1) + 2 * (X - 1) + 1)
        pl.semaphore_signal(plane_sem, inc=1, device_id=(dp, sib), device_id_type=MESH)

    @pl.when(core == 1)
    def _():
        pl.semaphore_wait(plane_sem, 1)


    def remote(buf, b, ssem, rsem, ctx_to):
        return pltpu.make_async_remote_copy(
            src_ref=buf.at[block(b)], dst_ref=buf.at[block(b)], send_sem=ssem, recv_sem=rsem.at[b],
            device_id=(dp, ctx_to), device_id_type=MESH,
        )

    def arrived(buf, b, ssem, rsem):
        remote(buf, b, ssem.at[0], rsem, sib).wait_recv()

    def each(low, high, body):
        def step(k, _):
            body(k)
            return _
        lax.fori_loop(low, high, step, 0)

    e_ring = Ring(e_all, R, Y, y, core, e_ssem, e_rsem, lambda chip, c: (dp, chip * 2 + c))
    c_star = Star(cot_all, R, X, x, core, cot_ssem, cot_rsem, lambda chip, c: (z * X + chip, y * 2 + c))
    e_ring.start(e_ring.first())
    cot_copy.wait()

    own = e_all[rows, :]
    for g in range(4):
        w_copies[g].wait()
        for half in range(2):
            cols = pl.ds(g * WIDTH + half * 256, 256)
            a, slope = silu_parts(mul(own, w_in_v[:, cols]))
            act_all[rows, cols] = a.astype(BF16)
            slope_v[:, cols] = slope
    e_ring.start(e_ring.second())
    c_star.start()
    wo_copy.wait()
    gg_v[...] = mul_t(cot_all[block(mine), :], w_out_v[...])

    def project(b, *bases):
        for base in bases:
            for half in range(2):
                cols = pl.ds(base + half * 256, 256)
                a, _ = silu_parts(mul(e_all[block(b), :], w_in_v[:, cols]))
                act_all[block(b), cols] = a.astype(BF16)

    def project_chip(c, k):
        @pl.when(c < y)
        def _():
            project(c * 2 + k, V_COL, K_COL)

        @pl.when(c > y)
        def _():
            project(c * 2 + k, Q_COL)

    def head(base, h):
        return pl.ds(base + h * DH, DH)

    def allowed(query_major):
        first = lax.broadcasted_iota(jnp.int32, (R, PAIR), 0) + core * R
        second = lax.broadcasted_iota(jnp.int32, (R, PAIR), 1)
        return first >= second if query_major else second >= first

    def forward(c, masked):
        for h in range(HEADS):
            s = mul_t(act_all[rows, head(Q_COL, h)], act_all[pair(c), head(K_COL, h)]) * scale
            a, slope = silu_parts(s)
            slope = slope * scale
            if masked:
                ok = allowed(True)
                a, slope = jnp.where(ok, a, 0.0), jnp.where(ok, slope, 0.0)
            g_v[c, h] = slope
            w_v[h] = a.astype(BF16)
        part = jnp.concatenate([mul(w_v[h], act_all[pair(c), head(V_COL, h)]) for h in range(HEADS)], axis=1)
        if masked:
            att_v[...] = part
        else:
            att_v[...] += part

    def forward_block(c, k):
        cols = pl.ds(pl.multiple_of(k * R, R), R)
        keys = block(c * 2 + k)
        for h in range(HEADS):
            a, slope = silu_parts(mul_t(act_all[rows, head(Q_COL, h)], act_all[keys, head(K_COL, h)]) * scale)
            g_v[c, h, :, cols] = slope * scale
            w_v[h, :, pl.ds(0, R)] = a.astype(BF16)
        att_v[...] += jnp.concatenate(
            [mul(w_v[h, :, pl.ds(0, R)], act_all[keys, head(V_COL, h)]) for h in range(HEADS)], axis=1
        )

    def prepare(c, masked):
        for h in range(HEADS):
            s = mul_t(act_all[rows, head(K_COL, h)], act_all[pair(c), head(Q_COL, h)]) * scale
            a, slope = silu_parts(s)
            slope = slope * scale
            if masked:
                ok = allowed(False)
                a, slope = jnp.where(ok, a, 0.0), jnp.where(ok, slope, 0.0)
            g_v[c + 1, h] = slope
            p_v[c, h] = a.astype(BF16)

    e_ring.wait_other(y)
    project(sib, V_COL, Q_COL, K_COL)
    forward(y, True)
    prepare(y, True)
    if Y > 1:
        e_ring.relay()
        e_ring.hand_near()

    def chip_at(t):
        return (y + 1 + (2 * t) % 3) % Y

    def near_step(t):
        c = chip_at(t)

        @pl.when(t == 1)
        def _():
            e_ring.hand_far()

        e_ring.wait_other(c)
        project_chip(c, other)

        @pl.when(c < y)
        def _():
            forward(c, False)

        @pl.when(c > y)
        def _():
            prepare(c, False)

    def far_step(k):
        project_chip(e_ring.f, k)

        @pl.when(e_ring.f < y)
        def _():
            forward_block(e_ring.f, k)

    if Y > 1:
        each(0, 2, lambda t: project_chip(chip_at(t), core))
    if Y > 1:
        each(0, 2, near_step)
        far_step(core)
        e_ring.wait_other(e_ring.f)
        far_step(other)

        @pl.when(e_ring.f > y)
        def _():
            prepare(e_ring.f, False)

    att = att_v[...]
    cen = att - jnp.mean(att, axis=1, keepdims=True)
    inv = lax.rsqrt(jnp.mean(cen * cen, axis=1, keepdims=True) + EPSILON)
    normed = cen * inv
    gate = act_all[rows, pl.ds(U_COL, WIDTH)].astype(F32)
    gated = normed * gate

    turned = jnp.transpose(gated).reshape(Z, X, RD, R)
    for to in range(X):
        gt_send[to] = turned[:, to].reshape(Z * RD, R).astype(BF16)

    def gt_part(s):
        return gt_all.at[:, block(s)]

    def gt_piece(s):
        return pl.ds(pl.multiple_of((s % 2) * (ZH * RD), ZH * RD), ZH * RD)

    def gt_out(k):
        s = (mine + k) % S
        return pltpu.make_async_remote_copy(
            src_ref=gt_send.at[s // 2, gt_piece(s)], dst_ref=gt_part(mine),
            send_sem=gt_ssem.at[k], recv_sem=gt_rsem.at[mine],
            device_id=(z * X + s // 2, y * 2 + s % 2), device_id_type=MESH,
        )

    def gt_in(k):
        s = (mine + k) % S
        return pltpu.make_async_remote_copy(
            src_ref=gt_send.at[s // 2, gt_piece(s)], dst_ref=gt_part(s),
            send_sem=gt_ssem.at[k], recv_sem=gt_rsem.at[s],
            device_id=(z * X + s // 2, y * 2 + s % 2), device_id_type=MESH,
        )

    each(1, S, lambda k: gt_out(k).start())
    gt_all[:, block(mine)] = gt_send[x, gt_piece(mine), :]

    gg = gg_v[...]
    gn = gg * gate
    grad_att = (
        gn - jnp.mean(gn, axis=1, keepdims=True) - normed * jnp.mean(gn * normed, axis=1, keepdims=True)
    ) * inv * live
    do_all[rows, :] = grad_att.astype(BF16)

    def d_out(c):
        return remote(do_all, ctx, d_ssem.at[c], d_rsem, c * 2 + core)

    d_sib = remote(do_all, ctx, d_ssem.at[y], d_rsem, sib)
    d_sib.start()
    each(0, y, lambda c: d_out(c).start())


    @pl.when(core == 1)
    def _():
        pl.semaphore_wait(barrier, Z - 1)
        pl.semaphore_signal(z_sem, inc=1, device_id=(dp, sib), device_id_type=MESH)

    c_star.hand_over()
    c_star.wait_other()
    each(1, S, lambda k: gt_in(k).wait_recv())
    gram = mul(gt_all[...], cot_all[...]).reshape(ZH, RD, D)
    z_send[...] = jnp.concatenate([gram[:, :, : D // 2], gram[:, :, D // 2 :]], axis=1).astype(BF16)

    def z_out(k):
        return pltpu.make_async_remote_copy(
            src_ref=z_send.at[k], dst_ref=z_recv.at[z], send_sem=z_ssem.at[k], recv_sem=z_rsem.at[z],
            device_id=((core * ZH + k) * X + x, ctx), device_id_type=MESH,
        )

    def z_in(k):
        return pltpu.make_async_remote_copy(
            src_ref=z_send.at[0], dst_ref=z_recv.at[k], send_sem=z_ssem.at[0], recv_sem=z_rsem.at[k],
            device_id=(k * X + x, ctx), device_id_type=MESH,
        )

    def z_start(distances):
        for d in distances:
            to = (z + d) % Z

            @pl.when(to // ZH == core)
            def _():
                z_out(to % ZH).start()

    z_order = sorted(range(1, Z), key=lambda d: -min(d, Z - d))

    @pl.when(core == 0)
    def _():
        pl.semaphore_wait(z_sem, 1)

    z_start(z_order[:5])

    out[...] = mul(gated.astype(BF16), w_out_v[...]).astype(BF16)
    gu_v[...] = gg * normed
    z_start(z_order[5:9])

    dq_v[...] = jnp.zeros_like(dq_v)
    dk_v[...] = jnp.zeros_like(dk_v)
    dv_v[...] = jnp.zeros_like(dv_v)

    def query_step(c):
        for h in range(HEADS):
            gw = mul_t(do_all[rows, head(0, h)], act_all[pair(c), head(V_COL, h)])
            gs = (gw * g_v[c, h]).astype(BF16)
            dq_v[:, head(0, h)] += mul(gs, act_all[pair(c), head(K_COL, h)])

    each(0, y + 1, query_step)

    z_start(z_order[9:])

    def back(grad, base):
        cols = pl.ds(base, WIDTH)
        return mul_t((grad * slope_v[:, cols]).astype(BF16), w_in_v[:, cols])

    ge_v[...] = back(gu_v[...], U_COL) + back(dq_v[...], Q_COL)

    def key_step(c):
        for h in range(HEADS):
            do_h = do_all[pair(c), head(0, h)]
            gw = mul_t(act_all[rows, head(V_COL, h)], do_h)
            gs = (gw * g_v[c + 1, h]).astype(BF16)
            dv_v[:, head(0, h)] += mul(p_v[c, h], do_h)
            dk_v[:, head(0, h)] += mul(gs, act_all[pair(c), head(Q_COL, h)])

    arrived(do_all, sib, d_ssem, d_rsem)
    key_step(y)

    def hand_over(c):
        return remote(do_all, c * 2 + core, d_ssem.at[Y + c], d_rsem, sib)

    def later_chip(c):
        arrived(do_all, c * 2 + core, d_ssem, d_rsem)
        hand_over(c).start()
        arrived(do_all, c * 2 + other, d_ssem, d_rsem)
        key_step(c)

    each(y + 1, Y, later_chip)

    grad_events[...] = (ge_v[...] + back(dv_v[...], V_COL) + back(dk_v[...], K_COL)).astype(BF16)

    holder = z // ZH
    c_order = sorted(range(1, 2 * Y), key=lambda k: -min(k, 2 * Y - k))

    def c_out(k):
        return pltpu.make_async_remote_copy(
            src_ref=c_recv.at[y], dst_ref=c_recv.at[y], send_sem=c_ssem.at[k], recv_sem=c_rsem.at[y],
            device_id=(dp, (ctx + k) % (2 * Y)), device_id_type=MESH,
        )

    def c_in(k):
        return pltpu.make_async_remote_copy(
            src_ref=c_recv.at[k], dst_ref=c_recv.at[k], send_sem=c_ssem.at[0], recv_sem=c_rsem.at[k],
            device_id=(dp, sib), device_id_type=MESH,
        )

    e_ring.done()
    c_star.done()
    d_sib.wait_send()
    each(0, y, lambda c: d_out(c).wait_send())
    each(y + 1, Y, lambda c: hand_over(c).wait_send())
    each(1, S, lambda k: gt_out(k).wait_send())

    def z_done(k):
        @pl.when(core * ZH + k != z)
        def _():
            z_out(k).wait_send()

    each(0, ZH, z_done)

    @pl.when(core == holder)
    def _():
        z_recv[z] = z_send[z % ZH]

        def wait_z(k):
            @pl.when(k != z)
            def _():
                z_in(k).wait_recv()

        each(0, Z, wait_z)
        total = jnp.sum(z_recv[...].astype(F32), axis=0)
        c_recv[y] = jnp.concatenate([total[:RD], total[RD:]], axis=1)
        for k in c_order:
            c_out(k).start()

    def wait_c(k):
        @pl.when(k * 2 + holder != ctx)
        def _():
            c_in(k).wait_recv()

    each(0, Y, wait_c)
    tokens = R * 2 * Y * Z * X
    grad_w_out[...] = jnp.sum(c_recv[...], axis=0) * (1.0 / math.sqrt(tokens))

    @pl.when(core == holder)
    def _():
        each(1, 2 * Y, lambda k: c_out(k).wait_send())


def in_hbm(a):
    return pltpu.with_memory_space_constraint(a, pltpu.HBM)


def store(*refs):
    copies = [pltpu.make_async_copy(refs[n], refs[3 + n], refs[6].at[n]) for n in range(3)]
    for copy in copies:
        copy.start()
    for copy in copies:
        copy.wait()


def build(mesh, X):
    Z, Y = mesh.shape["dp"] // X, mesh.shape["ctx"] // 2

    def per_device(events, keep, lengths, cotangent, w_in, w_out):
        R, D = events.shape[1:]
        L = R * 2 * Y
        S = 2 * X
        ZH, RD = Z // 2, D // (Z * X)
        vmem = pl.BlockSpec(memory_space=pltpu.VMEM)
        hbm = pl.BlockSpec(memory_space=pltpu.HBM)
        dma = pltpu.SemaphoreType.DMA
        output, grad_events, grad_w_out = pl.pallas_call(
            functools.partial(kernel, Z, X, Y),
            out_shape=(pltpu.VMEM((R, D), BF16), pltpu.VMEM((R, D), BF16), pltpu.VMEM((RD, D), F32)),
            in_specs=[hbm, hbm, pl.BlockSpec(memory_space=pltpu.SMEM), hbm, hbm, hbm],
            out_specs=[vmem] * 3,
            scratch_shapes=[
                pltpu.VMEM((1, R), jnp.int32),
                pltpu.VMEM((L, D), BF16),
                pltpu.VMEM((L, 4 * WIDTH), BF16),
                pltpu.VMEM((L, WIDTH), BF16),
                pltpu.VMEM((S * R, D), BF16),
                pltpu.VMEM((D, 4 * WIDTH), BF16),
                pltpu.VMEM((WIDTH, D), BF16),
                pltpu.VMEM((R, 4 * WIDTH), F32),
                pltpu.VMEM((R, WIDTH), F32),
                pltpu.VMEM((R, WIDTH), F32),
                pltpu.VMEM((R, WIDTH), F32),
                pltpu.VMEM((R, WIDTH), F32),
                pltpu.VMEM((R, WIDTH), F32),
                pltpu.VMEM((R, WIDTH), F32),
                pltpu.VMEM((R, D), F32),
                pltpu.VMEM((Y + 1, HEADS, R, 2 * R), F32),
                pltpu.VMEM((Y, HEADS, R, 2 * R), BF16),
                pltpu.VMEM((HEADS, R, 2 * R), BF16),
                pltpu.VMEM((X, Z * RD, R), BF16),
                pltpu.VMEM((ZH * RD, S * R), BF16),
                pltpu.VMEM((ZH, 2 * RD, D // 2), BF16),
                pltpu.VMEM((Z, 2 * RD, D // 2), BF16),
                pltpu.VMEM((Y, RD, D), F32),
                pltpu.SemaphoreType.REGULAR, pltpu.SemaphoreType.REGULAR,
                dma((8,)),
                dma((20,)), dma((6 * Y,)),
                dma((2 * Y,)), dma((2 * Y,)),
                dma((2 * X,)), dma((2 * X,)),
                dma((S,)), dma((S,)),
                dma((ZH,)), dma((Z,)),
                dma((2 * Y,)), dma((Y,)),
            ],
            compiler_params=pltpu.CompilerParams(
                collective_id=0, has_side_effects=True, vmem_limit_bytes=56 * 1024 * 1024
            ),
            name="layer",
        )(in_hbm(events[0]), in_hbm(keep), lengths, in_hbm(cotangent[0]), in_hbm(w_in), in_hbm(w_out))
        output, grad_events, grad_w_out = pl.pallas_call(
            store,
            out_shape=(
                jax.ShapeDtypeStruct((R, D), BF16),
                jax.ShapeDtypeStruct((R, D), BF16),
                jax.ShapeDtypeStruct((RD, D), F32),
            ),
            in_specs=[vmem] * 3,
            out_specs=(hbm, hbm, hbm),
            scratch_shapes=[dma((3,))],
            name="store",
        )(*[pltpu.with_memory_space_constraint(a, pltpu.VMEM) for a in (output, grad_events, grad_w_out)])
        return (output[None], grad_events[None], grad_w_out)

    return jax.shard_map(
        per_device,
        mesh=mesh,
        in_specs=(P("dp", "ctx", None), P("dp", "ctx"), P("dp"), P("dp", "ctx", None), P(), P()),
        out_specs=(P("dp", "ctx", None), P("dp", "ctx", None), P("dp", None)),
        check_vma=False,
    )


def solution(mesh):
    return build(mesh, X_CHIPS)
```

```python
import functools
import math

import jax
import jax.numpy as jnp
from jax import lax
from jax.experimental import pallas as pl
from jax.experimental.pallas import tpu as pltpu
from jax.sharding import PartitionSpec as P

HEADS = 4
DH = 128
WIDTH = HEADS * DH
X_CHIPS = 4
EPSILON = 1e-06
MESH = pl.DeviceIdType.MESH
F32 = jnp.float32
BF16 = jnp.bfloat16
U_COL, V_COL, Q_COL, K_COL = 0, WIDTH, 2 * WIDTH, 3 * WIDTH


def silu_parts(v):
    s = 0.5 * jnp.tanh(0.5 * v) + 0.5
    a = v * s
    return a, s + a * (1.0 - s)


def mul(a, b):
    return jnp.dot(a, b, preferred_element_type=F32)


def mul_t(a, b):
    return lax.dot_general(a, b, (((1,), (1,)), ((), ())), preferred_element_type=F32)


class Ring:
    def __init__(self, buf, rows, n, pos, core, ssem, rsem, place):
        self.buf, self.rows, self.n, self.pos, self.core = buf, rows, n, pos, core
        self.ssem, self.rsem = ssem, rsem
        self.other = 1 - core
        self.sib = place(pos, self.other)
        self.right, self.left = place((pos + 1) % n, self.other), place((pos + n - 1) % n, self.other)
        self.l, self.r, self.f = (pos + n - 1) % n, (pos + 1) % n, (pos + 2) % n

    def copy(self, chip, core, first, count, k, sem, to):
        rows = self.rows // 4
        start = pl.multiple_of((chip * 2 + core) * self.rows + first * rows, rows)
        part = self.buf.at[pl.ds(start, count * rows)]
        return pltpu.make_async_remote_copy(
            src_ref=part, dst_ref=part, send_sem=self.ssem.at[k], recv_sem=self.rsem.at[sem],
            device_id=to, device_id_type=MESH,
        )

    def quarter(self, chip, core, q, k, to):
        return self.copy(chip, core, q, 1, k, chip * 4 + q, to)

    def hand(self, chip, core, half, k):
        return self.copy(chip, core, half * 2, 2, k, 4 * self.n + chip * 2 + half, self.sib)

    def first(self):
        near = []
        if self.n > 1:
            for n in range(2):
                near.append(self.quarter(self.pos, self.core, n, 2 + n, self.right))
                near.append(self.quarter(self.pos, self.core, n + 2, 6 + n, self.left))
        return near + [self.hand(self.pos, self.core, half, half) for half in range(2)]

    def second(self):
        near = []
        if self.n > 1:
            for n in range(2):
                near.append(self.quarter(self.pos, self.core, n + 2, 4 + n, self.right))
                near.append(self.quarter(self.pos, self.core, n, 8 + n, self.left))
        return near

    def passed(self):
        steps = []
        for n in range(2):
            steps.append((self.l, n, self.quarter(self.l, self.other, n, 10 + n, self.right)))
            steps.append((self.r, 2 + n, self.quarter(self.r, self.other, 2 + n, 12 + n, self.left)))
        return steps

    def wait(self, chip, core, first, count=1):
        for q in range(first, first + count):
            self.quarter(chip, core, q, 0, self.sib).wait_recv()

    def wait_handed(self, chip, core):
        for half in range(2):
            self.hand(chip, core, half, 0).wait_recv()

    def start(self, copies):
        for copy in copies:
            copy.start()

    def relay(self):
        for chip, q, copy in self.passed():
            self.wait(chip, self.other, q)
            copy.start()

    def hand_near(self):
        self.hand(self.l, self.other, 0, 14).start()
        self.hand(self.r, self.other, 1, 17).start()
        self.wait(self.l, self.other, 2, 2)
        self.hand(self.l, self.other, 1, 15).start()
        self.wait(self.r, self.other, 0, 2)
        self.hand(self.r, self.other, 0, 16).start()

    def hand_far(self):
        for half in range(2):
            self.wait(self.f, self.core, half * 2, 2)
            self.hand(self.f, self.core, half, 18 + half).start()

    def done(self):
        for copy in self.first() + self.second():
            copy.wait_send()
        if self.n > 1:
            for _, _, copy in self.passed():
                copy.wait_send()
            for n, chip in enumerate((self.l, self.r, self.f)):
                for half in range(2):
                    self.hand(chip, self.core if n == 2 else self.other, half, 14 + 2 * n + half).wait_send()


class Star:
    def __init__(self, buf, rows, n, pos, core, ssem, rsem, place):
        self.buf, self.rows, self.n, self.pos, self.core = buf, rows, n, pos, core
        self.ssem, self.rsem, self.place = ssem, rsem, place

    def copy(self, chip, core, k, sem, to):
        start = pl.multiple_of((chip * 2 + core) * self.rows, self.rows)
        part = self.buf.at[pl.ds(start, self.rows)]
        return pltpu.make_async_remote_copy(
            src_ref=part, dst_ref=part, send_sem=self.ssem.at[k], recv_sem=self.rsem.at[sem],
            device_id=to, device_id_type=MESH,
        )

    def out(self, d):
        return self.copy(self.pos, self.core, d, self.pos, self.place((self.pos + d) % self.n, self.core))

    def hand(self, d):
        chip = (self.pos + d) % self.n
        return self.copy(chip, self.core, self.n + d, self.n + chip, self.place(self.pos, 1 - self.core))

    def start(self):
        for d in range(1, self.n):
            self.out(d).start()
        self.hand(0).start()

    def hand_over(self):
        for d in range(1, self.n):
            chip = (self.pos + d) % self.n
            self.copy(chip, self.core, 0, chip, self.place(self.pos, self.core)).wait_recv()
            self.hand(d).start()

    def wait_other(self):
        for d in range(self.n):
            chip = (self.pos + d) % self.n
            self.copy(chip, 1 - self.core, 0, self.n + chip, self.place(self.pos, self.core)).wait_recv()

    def done(self):
        for d in range(1, self.n):
            self.out(d).wait_send()
        for d in range(self.n):
            self.hand(d).wait_send()


def kernel(
    Z, X, Y,
    events, keep, lengths, cotangent, w_in, w_out,
    out, grad_events, grad_w_out,
    keep_v, e_all, act_all, do_all, cot_all, w_in_v, w_out_v, slope_v, gg_v, gu_v, att_v, dq_v, dk_v, dv_v, ge_v,
    g_v, p_v, w_v, gt_send, gt_all, z_send, z_recv, c_recv,
    plane_sem, z_sem, local_sem, e_ssem, e_rsem, d_ssem, d_rsem, cot_ssem, cot_rsem, gt_ssem, gt_rsem, z_ssem, z_rsem, c_ssem, c_rsem,
):
    R = events.shape[0]
    D = events.shape[1]
    PAIR = 2 * R
    S = 2 * X
    ZH = Z // 2
    RD = D // (Z * X)
    scale = 1.0 / math.sqrt(DH)
    dp, ctx = lax.axis_index("dp"), lax.axis_index("ctx")
    z, x = dp // X, dp % X
    y, core = ctx // 2, ctx % 2
    other = 1 - core
    sib = y * 2 + other
    mine = x * 2 + core

    def block(b):
        return pl.ds(pl.multiple_of(b * R, R), R)

    def pair(c):
        return pl.ds(pl.multiple_of(c * PAIR, PAIR), PAIR)

    rows = block(ctx)

    ev_copy = pltpu.make_async_copy(events, e_all.at[rows], local_sem.at[0])
    ev_copy.start()
    keep_copy = pltpu.make_async_copy(keep, keep_v, local_sem.at[7])
    keep_copy.start()
    barrier = pltpu.get_barrier_semaphore()

    def greet(dp_to, ctx_to):
        pl.semaphore_signal(barrier, inc=1, device_id=(dp_to, ctx_to), device_id_type=MESH)

    for k in range(1, Y):
        greet(dp, ((y + k) % Y) * 2)
    for k in range(1, X):
        greet(z * X + (x + k) % X, y * 2)

    @pl.when(core == 1)
    def _():
        greet(dp, y * 2)

    @pl.when(core == z // ZH)
    def _():
        for k in range(1, Z):
            greet(((z + k) % Z) * X + x, y * 2 + 1)

    cot_copy = pltpu.make_async_copy(cotangent, cot_all.at[block(mine)], local_sem.at[1])
    cot_copy.start()
    w_copies = []
    for g in range(4):
        cols = pl.ds(g * WIDTH, WIDTH)
        w_copies.append(pltpu.make_async_copy(w_in.at[:, cols], w_in_v.at[:, cols], local_sem.at[2 + g]))
    for copy in w_copies:
        copy.start()
    wo_copy = pltpu.make_async_copy(w_out, w_out_v, local_sem.at[6])
    wo_copy.start()

    ev_copy.wait()
    keep_copy.wait()
    lane = lax.broadcasted_iota(jnp.int32, (1, R), 1)
    live_row = jnp.where((keep_v[...] == 1) & (ctx * R + lane < lengths[0]), 1.0, 0.0)
    eye = lax.broadcasted_iota(jnp.int32, (R, R), 0) == lax.broadcasted_iota(jnp.int32, (R, R), 1)
    live = jnp.sum(jnp.where(eye, live_row, 0.0), axis=1, keepdims=True)
    e_all[rows, :] = (e_all[rows, :].astype(F32) * live).astype(BF16)

    @pl.when(core == 0)
    def _():
        pl.semaphore_wait(barrier, 2 * (Y - 1) + 2 * (X - 1) + 1)
        pl.semaphore_signal(plane_sem, inc=1, device_id=(dp, sib), device_id_type=MESH)

    @pl.when(core == 1)
    def _():
        pl.semaphore_wait(plane_sem, 1)


    def remote(buf, b, ssem, rsem, ctx_to):
        return pltpu.make_async_remote_copy(
            src_ref=buf.at[block(b)], dst_ref=buf.at[block(b)], send_sem=ssem, recv_sem=rsem.at[b],
            device_id=(dp, ctx_to), device_id_type=MESH,
        )

    def arrived(buf, b, ssem, rsem):
        remote(buf, b, ssem.at[0], rsem, sib).wait_recv()

    def each(low, high, body):
        def step(k, _):
            body(k)
            return _
        lax.fori_loop(low, high, step, 0)

    e_ring = Ring(e_all, R, Y, y, core, e_ssem, e_rsem, lambda chip, c: (dp, chip * 2 + c))
    c_star = Star(cot_all, R, X, x, core, cot_ssem, cot_rsem, lambda chip, c: (z * X + chip, y * 2 + c))
    e_ring.start(e_ring.first())
    cot_copy.wait()

    own = e_all[rows, :]
    for g in range(4):
        w_copies[g].wait()
        for half in range(2):
            cols = pl.ds(g * WIDTH + half * 256, 256)
            a, slope = silu_parts(mul(own, w_in_v[:, cols]))
            act_all[rows, cols] = a.astype(BF16)
            slope_v[:, cols] = slope
    e_ring.start(e_ring.second())
    c_star.start()
    wo_copy.wait()
    gg_v[...] = mul_t(cot_all[block(mine), :], w_out_v[...])

    def project(b, *bases):
        for base in bases:
            for half in range(2):
                cols = pl.ds(base + half * 256, 256)
                a, _ = silu_parts(mul(e_all[block(b), :], w_in_v[:, cols]))
                act_all[block(b), cols] = a.astype(BF16)

    def head(base, h):
        return pl.ds(base + h * DH, DH)

    def allowed(query_major):
        first = lax.broadcasted_iota(jnp.int32, (R, PAIR), 0) + core * R
        second = lax.broadcasted_iota(jnp.int32, (R, PAIR), 1)
        return first >= second if query_major else second >= first

    def forward(c):
        for h in range(HEADS):
            s = mul_t(act_all[rows, head(Q_COL, h)], act_all[pair(c), head(K_COL, h)]) * scale
            a, slope = silu_parts(s)
            ok = allowed(True)
            g_v[c, h] = jnp.where(ok, slope * scale, 0.0)
            w_v[h] = jnp.where(ok, a, 0.0).astype(BF16)
        att_v[...] = jnp.concatenate([mul(w_v[h], act_all[pair(c), head(V_COL, h)]) for h in range(HEADS)], axis=1)

    def forward_block(c, k):
        cols = pl.ds(pl.multiple_of(k * R, R), R)
        keys = block(c * 2 + k)
        for h in range(HEADS):
            a, slope = silu_parts(mul_t(act_all[rows, head(Q_COL, h)], act_all[keys, head(K_COL, h)]) * scale)
            g_v[c, h, :, cols] = slope * scale
            w_v[h, :, pl.ds(0, R)] = a.astype(BF16)
        att_v[...] += jnp.concatenate(
            [mul(w_v[h, :, pl.ds(0, R)], act_all[keys, head(V_COL, h)]) for h in range(HEADS)], axis=1
        )

    def prepare(c):
        for h in range(HEADS):
            s = mul_t(act_all[rows, head(K_COL, h)], act_all[pair(c), head(Q_COL, h)]) * scale
            a, slope = silu_parts(s)
            ok = allowed(False)
            g_v[c + 1, h] = jnp.where(ok, slope * scale, 0.0)
            p_v[c, h] = jnp.where(ok, a, 0.0).astype(BF16)

    def prepare_block(c, k):
        cols = pl.ds(pl.multiple_of(k * R, R), R)
        for h in range(HEADS):
            s = mul_t(act_all[rows, head(K_COL, h)], act_all[block(c * 2 + k), head(Q_COL, h)]) * scale
            a, slope = silu_parts(s)
            g_v[c + 1, h, :, cols] = slope * scale
            p_v[c, h, :, cols] = a.astype(BF16)

    e_ring.wait_handed(y, other)
    project(sib, V_COL, Q_COL, K_COL)
    forward(y)
    prepare(y)
    if Y > 1:
        e_ring.relay()
        e_ring.hand_near()

    def block_step(t):
        far = t // 4
        c = (y + (1 - far) * (1 + 2 * (t % 2)) + 2 * far) % Y
        swap = (5 - t) // 4 + t // 5
        k = core + swap * (1 - 2 * core)

        @pl.when(t == 3)
        def _():
            e_ring.hand_far()

        @pl.when((t == 2) | (t == 3) | (t == 5))
        def _():
            e_ring.wait_handed(c, k)

        @pl.when(c < y)
        def _():
            project(c * 2 + k, V_COL, K_COL)
            forward_block(c, k)

        @pl.when(c > y)
        def _():
            project(c * 2 + k, Q_COL)
            prepare_block(c, k)

    if Y > 1:
        each(0, 6, block_step)

    att = att_v[...]
    cen = att - jnp.mean(att, axis=1, keepdims=True)
    inv = lax.rsqrt(jnp.mean(cen * cen, axis=1, keepdims=True) + EPSILON)
    normed = cen * inv
    gate = act_all[rows, pl.ds(U_COL, WIDTH)].astype(F32)
    gated = normed * gate

    turned = jnp.transpose(gated).reshape(Z, X, RD, R)
    for to in range(X):
        gt_send[to] = turned[:, to].reshape(Z * RD, R).astype(BF16)

    def gt_part(s):
        return gt_all.at[:, block(s)]

    def gt_piece(c):
        return pl.ds(pl.multiple_of(c * (ZH * RD), ZH * RD), ZH * RD)

    def gt_out(d, swap):
        to = (x + d) % X
        c = other if swap else core
        return pltpu.make_async_remote_copy(
            src_ref=gt_send.at[to, gt_piece(c)], dst_ref=gt_part(mine),
            send_sem=gt_ssem.at[2 * d + swap], recv_sem=gt_rsem.at[mine],
            device_id=(z * X + to, y * 2 + c), device_id_type=MESH,
        )

    def gt_in(d, swap):
        source = ((x + d) % X) * 2 + (other if swap else core)
        return pltpu.make_async_remote_copy(
            src_ref=gt_send.at[x, gt_piece(core)], dst_ref=gt_part(source),
            send_sem=gt_ssem.at[2 * d + swap], recv_sem=gt_rsem.at[source],
            device_id=(dp, sib), device_id_type=MESH,
        )

    gt_order = [(d, swap) for d in sorted(range(1, X), key=lambda d: -min(d, X - d)) for swap in range(2)] + [(0, 1)]
    for d, swap in gt_order[:2]:
        gt_out(d, swap).start()
    gt_all[:, block(mine)] = gt_send[x, gt_piece(core), :]

    gg = gg_v[...]
    gn = gg * gate
    grad_att = (
        gn - jnp.mean(gn, axis=1, keepdims=True) - normed * jnp.mean(gn * normed, axis=1, keepdims=True)
    ) * inv * live
    do_all[rows, :] = grad_att.astype(BF16)
    for d, swap in gt_order[2:]:
        gt_out(d, swap).start()

    def d_out(c):
        return remote(do_all, ctx, d_ssem.at[c], d_rsem, c * 2 + core)

    d_sib = remote(do_all, ctx, d_ssem.at[y], d_rsem, sib)
    d_sib.start()
    each(0, y, lambda c: d_out(c).start())


    @pl.when(core == 1)
    def _():
        pl.semaphore_wait(barrier, Z - 1)
        pl.semaphore_signal(z_sem, inc=1, device_id=(dp, sib), device_id_type=MESH)

    c_star.hand_over()
    c_star.wait_other()
    for d, swap in gt_order:
        gt_in(d, swap).wait_recv()
    gram = mul(gt_all[...], cot_all[...]).reshape(ZH, RD, D)
    z_send[...] = jnp.concatenate([gram[:, :, : D // 2], gram[:, :, D // 2 :]], axis=1).astype(BF16)

    def z_out(k):
        return pltpu.make_async_remote_copy(
            src_ref=z_send.at[k], dst_ref=z_recv.at[z], send_sem=z_ssem.at[k], recv_sem=z_rsem.at[z],
            device_id=((core * ZH + k) * X + x, ctx), device_id_type=MESH,
        )

    def z_in(k):
        return pltpu.make_async_remote_copy(
            src_ref=z_send.at[0], dst_ref=z_recv.at[k], send_sem=z_ssem.at[0], recv_sem=z_rsem.at[k],
            device_id=(k * X + x, ctx), device_id_type=MESH,
        )

    def z_start(distances):
        for d in distances:
            to = (z + d) % Z

            @pl.when(to // ZH == core)
            def _():
                z_out(to % ZH).start()

    z_order = sorted(range(1, Z), key=lambda d: -min(d, Z - d))

    @pl.when(core == 0)
    def _():
        pl.semaphore_wait(z_sem, 1)

    z_start(z_order[:5])

    out[...] = mul(gated.astype(BF16), w_out_v[...]).astype(BF16)
    gu_v[...] = gg * normed
    z_start(z_order[5:9])

    dq_v[...] = jnp.zeros_like(dq_v)
    dk_v[...] = jnp.zeros_like(dk_v)
    dv_v[...] = jnp.zeros_like(dv_v)

    def query_step(c):
        for h in range(HEADS):
            gw = mul_t(do_all[rows, head(0, h)], act_all[pair(c), head(V_COL, h)])
            gs = (gw * g_v[c, h]).astype(BF16)
            dq_v[:, head(0, h)] += mul(gs, act_all[pair(c), head(K_COL, h)])

    each(0, y + 1, query_step)

    z_start(z_order[9:])

    def back(grad, base):
        cols = pl.ds(base, WIDTH)
        return mul_t((grad * slope_v[:, cols]).astype(BF16), w_in_v[:, cols])

    ge_v[...] = back(gu_v[...], U_COL) + back(dq_v[...], Q_COL)

    def key_step(c):
        for h in range(HEADS):
            do_h = do_all[pair(c), head(0, h)]
            gw = mul_t(act_all[rows, head(V_COL, h)], do_h)
            gs = (gw * g_v[c + 1, h]).astype(BF16)
            dv_v[:, head(0, h)] += mul(p_v[c, h], do_h)
            dk_v[:, head(0, h)] += mul(gs, act_all[pair(c), head(Q_COL, h)])

    arrived(do_all, sib, d_ssem, d_rsem)
    key_step(y)

    def hand_over(c):
        return remote(do_all, c * 2 + core, d_ssem.at[Y + c], d_rsem, sib)

    def later_chip(c):
        arrived(do_all, c * 2 + core, d_ssem, d_rsem)
        hand_over(c).start()
        arrived(do_all, c * 2 + other, d_ssem, d_rsem)
        key_step(c)

    each(y + 1, Y, later_chip)

    grad_events[...] = (ge_v[...] + back(dv_v[...], V_COL) + back(dk_v[...], K_COL)).astype(BF16)

    holder = z // ZH
    c_order = sorted(range(1, 2 * Y), key=lambda k: -min(k, 2 * Y - k))

    def c_out(k):
        return pltpu.make_async_remote_copy(
            src_ref=c_recv.at[y], dst_ref=c_recv.at[y], send_sem=c_ssem.at[k], recv_sem=c_rsem.at[y],
            device_id=(dp, (ctx + k) % (2 * Y)), device_id_type=MESH,
        )

    def c_in(k):
        return pltpu.make_async_remote_copy(
            src_ref=c_recv.at[k], dst_ref=c_recv.at[k], send_sem=c_ssem.at[0], recv_sem=c_rsem.at[k],
            device_id=(dp, sib), device_id_type=MESH,
        )

    e_ring.done()
    c_star.done()
    d_sib.wait_send()
    each(0, y, lambda c: d_out(c).wait_send())
    each(y + 1, Y, lambda c: hand_over(c).wait_send())
    for d, swap in gt_order:
        gt_out(d, swap).wait_send()

    def z_done(k):
        @pl.when(core * ZH + k != z)
        def _():
            z_out(k).wait_send()

    each(0, ZH, z_done)

    @pl.when(core == holder)
    def _():
        z_recv[z] = z_send[z % ZH]

        def wait_z(k):
            @pl.when(k != z)
            def _():
                z_in(k).wait_recv()

        each(0, Z, wait_z)
        total = jnp.sum(z_recv[...].astype(F32), axis=0)
        c_recv[y] = total.astype(BF16)
        for k in c_order:
            c_out(k).start()

    def wait_c(k):
        @pl.when(k * 2 + holder != ctx)
        def _():
            c_in(k).wait_recv()

    each(0, Y, wait_c)
    tokens = R * 2 * Y * Z * X
    total = jnp.sum(c_recv[...].astype(F32), axis=0) * (1.0 / math.sqrt(tokens))
    grad_w_out[...] = jnp.concatenate([total[:RD], total[RD:]], axis=1)

    @pl.when(core == holder)
    def _():
        each(1, 2 * Y, lambda k: c_out(k).wait_send())


def in_hbm(a):
    return pltpu.with_memory_space_constraint(a, pltpu.HBM)


def store(*refs):
    copies = [pltpu.make_async_copy(refs[n], refs[3 + n], refs[6].at[n]) for n in range(3)]
    for copy in copies:
        copy.start()
    for copy in copies:
        copy.wait()


def build(mesh, X):
    Z, Y = mesh.shape["dp"] // X, mesh.shape["ctx"] // 2

    def per_device(events, keep, lengths, cotangent, w_in, w_out):
        R, D = events.shape[1:]
        L = R * 2 * Y
        S = 2 * X
        ZH, RD = Z // 2, D // (Z * X)
        vmem = pl.BlockSpec(memory_space=pltpu.VMEM)
        hbm = pl.BlockSpec(memory_space=pltpu.HBM)
        dma = pltpu.SemaphoreType.DMA
        output, grad_events, grad_w_out = pl.pallas_call(
            functools.partial(kernel, Z, X, Y),
            out_shape=(pltpu.VMEM((R, D), BF16), pltpu.VMEM((R, D), BF16), pltpu.VMEM((RD, D), F32)),
            in_specs=[hbm, hbm, pl.BlockSpec(memory_space=pltpu.SMEM), hbm, hbm, hbm],
            out_specs=[vmem] * 3,
            scratch_shapes=[
                pltpu.VMEM((1, R), jnp.int32),
                pltpu.VMEM((L, D), BF16),
                pltpu.VMEM((L, 4 * WIDTH), BF16),
                pltpu.VMEM((L, WIDTH), BF16),
                pltpu.VMEM((S * R, D), BF16),
                pltpu.VMEM((D, 4 * WIDTH), BF16),
                pltpu.VMEM((WIDTH, D), BF16),
                pltpu.VMEM((R, 4 * WIDTH), F32),
                pltpu.VMEM((R, WIDTH), F32),
                pltpu.VMEM((R, WIDTH), F32),
                pltpu.VMEM((R, WIDTH), F32),
                pltpu.VMEM((R, WIDTH), F32),
                pltpu.VMEM((R, WIDTH), F32),
                pltpu.VMEM((R, WIDTH), F32),
                pltpu.VMEM((R, D), F32),
                pltpu.VMEM((Y + 1, HEADS, R, 2 * R), F32),
                pltpu.VMEM((Y, HEADS, R, 2 * R), BF16),
                pltpu.VMEM((HEADS, R, 2 * R), BF16),
                pltpu.VMEM((X, Z * RD, R), BF16),
                pltpu.VMEM((ZH * RD, S * R), BF16),
                pltpu.VMEM((ZH, 2 * RD, D // 2), BF16),
                pltpu.VMEM((Z, 2 * RD, D // 2), BF16),
                pltpu.VMEM((Y, 2 * RD, D // 2), BF16),
                pltpu.SemaphoreType.REGULAR, pltpu.SemaphoreType.REGULAR,
                dma((8,)),
                dma((20,)), dma((6 * Y,)),
                dma((2 * Y,)), dma((2 * Y,)),
                dma((2 * X,)), dma((2 * X,)),
                dma((S,)), dma((S,)),
                dma((ZH,)), dma((Z,)),
                dma((2 * Y,)), dma((Y,)),
            ],
            compiler_params=pltpu.CompilerParams(
                collective_id=0, has_side_effects=True, vmem_limit_bytes=56 * 1024 * 1024
            ),
            name="layer",
        )(in_hbm(events[0]), in_hbm(keep), lengths, in_hbm(cotangent[0]), in_hbm(w_in), in_hbm(w_out))
        output, grad_events, grad_w_out = pl.pallas_call(
            store,
            out_shape=(
                jax.ShapeDtypeStruct((R, D), BF16),
                jax.ShapeDtypeStruct((R, D), BF16),
                jax.ShapeDtypeStruct((RD, D), F32),
            ),
            in_specs=[vmem] * 3,
            out_specs=(hbm, hbm, hbm),
            scratch_shapes=[dma((3,))],
            name="store",
        )(*[pltpu.with_memory_space_constraint(a, pltpu.VMEM) for a in (output, grad_events, grad_w_out)])
        return (output[None], grad_events[None], grad_w_out)

    return jax.shard_map(
        per_device,
        mesh=mesh,
        in_specs=(P("dp", "ctx", None), P("dp", "ctx"), P("dp"), P("dp", "ctx", None), P(), P()),
        out_specs=(P("dp", "ctx", None), P("dp", "ctx", None), P("dp", None)),
        check_vma=False,
    )


def solution(mesh):
    return build(mesh, X_CHIPS)
```

```python
import functools
import math

import jax
import jax.numpy as jnp
from jax import lax
from jax.experimental import pallas as pl
from jax.experimental.pallas import tpu as pltpu
from jax.sharding import PartitionSpec as P

HEADS = 4
DH = 128
WIDTH = HEADS * DH
X_CHIPS = 4
EPSILON = 1e-06
MESH = pl.DeviceIdType.MESH
F32 = jnp.float32
BF16 = jnp.bfloat16
U_COL, V_COL, Q_COL, K_COL = 0, WIDTH, 2 * WIDTH, 3 * WIDTH


def silu_parts(v):
    s = 0.5 * jnp.tanh(0.5 * v) + 0.5
    a = v * s
    return a, s + a * (1.0 - s)


def mul(a, b):
    return jnp.dot(a, b, preferred_element_type=F32)


def mul_t(a, b):
    return lax.dot_general(a, b, (((1,), (1,)), ((), ())), preferred_element_type=F32)


class Ring:
    def __init__(self, buf, rows, n, pos, core, ssem, rsem, place):
        self.buf, self.rows, self.n, self.pos, self.core = buf, rows, n, pos, core
        self.ssem, self.rsem = ssem, rsem
        self.other = 1 - core
        self.sib = place(pos, self.other)
        self.right, self.left = place((pos + 1) % n, self.other), place((pos + n - 1) % n, self.other)
        self.l, self.r, self.f = (pos + n - 1) % n, (pos + 1) % n, (pos + 2) % n

    def copy(self, chip, core, first, count, k, sem, to):
        rows = self.rows // 4
        start = pl.multiple_of((chip * 2 + core) * self.rows + first * rows, rows)
        part = self.buf.at[pl.ds(start, count * rows)]
        return pltpu.make_async_remote_copy(
            src_ref=part, dst_ref=part, send_sem=self.ssem.at[k], recv_sem=self.rsem.at[sem],
            device_id=to, device_id_type=MESH,
        )

    def quarter(self, chip, core, q, k, to):
        return self.copy(chip, core, q, 1, k, chip * 4 + q, to)

    def hand(self, chip, core, half, k):
        return self.copy(chip, core, half * 2, 2, k, 4 * self.n + chip * 2 + half, self.sib)

    def first(self):
        near = []
        if self.n > 1:
            for n in range(2):
                near.append(self.quarter(self.pos, self.core, n, 2 + n, self.right))
                near.append(self.quarter(self.pos, self.core, n + 2, 6 + n, self.left))
        return near + [self.hand(self.pos, self.core, half, half) for half in range(2)]

    def second(self):
        near = []
        if self.n > 1:
            for n in range(2):
                near.append(self.quarter(self.pos, self.core, n + 2, 4 + n, self.right))
                near.append(self.quarter(self.pos, self.core, n, 8 + n, self.left))
        return near

    def passed(self):
        steps = []
        for n in range(2):
            steps.append((self.l, n, self.quarter(self.l, self.other, n, 10 + n, self.right)))
            steps.append((self.r, 2 + n, self.quarter(self.r, self.other, 2 + n, 12 + n, self.left)))
        return steps

    def wait(self, chip, core, first, count=1):
        for q in range(first, first + count):
            self.quarter(chip, core, q, 0, self.sib).wait_recv()

    def wait_handed(self, chip, core):
        for half in range(2):
            self.hand(chip, core, half, 0).wait_recv()

    def start(self, copies):
        for copy in copies:
            copy.start()

    def relay(self):
        for chip, q, copy in self.passed():
            self.wait(chip, self.other, q)
            copy.start()

    def hand_near(self):
        self.hand(self.l, self.other, 0, 14).start()
        self.hand(self.r, self.other, 1, 17).start()
        self.wait(self.l, self.other, 2, 2)
        self.hand(self.l, self.other, 1, 15).start()
        self.wait(self.r, self.other, 0, 2)
        self.hand(self.r, self.other, 0, 16).start()

    def hand_far(self):
        for half in range(2):
            self.wait(self.f, self.core, half * 2, 2)
            self.hand(self.f, self.core, half, 18 + half).start()

    def done(self):
        for copy in self.first() + self.second():
            copy.wait_send()
        if self.n > 1:
            for _, _, copy in self.passed():
                copy.wait_send()
            for n, chip in enumerate((self.l, self.r, self.f)):
                for half in range(2):
                    self.hand(chip, self.core if n == 2 else self.other, half, 14 + 2 * n + half).wait_send()


class Star:
    def __init__(self, buf, rows, n, pos, core, ssem, rsem, place):
        self.buf, self.rows, self.n, self.pos, self.core = buf, rows, n, pos, core
        self.ssem, self.rsem, self.place = ssem, rsem, place

    def copy(self, chip, core, k, sem, to):
        start = pl.multiple_of((chip * 2 + core) * self.rows, self.rows)
        part = self.buf.at[pl.ds(start, self.rows)]
        return pltpu.make_async_remote_copy(
            src_ref=part, dst_ref=part, send_sem=self.ssem.at[k], recv_sem=self.rsem.at[sem],
            device_id=to, device_id_type=MESH,
        )

    def out(self, d):
        return self.copy(self.pos, self.core, d, self.pos, self.place((self.pos + d) % self.n, self.core))

    def hand(self, d):
        chip = (self.pos + d) % self.n
        return self.copy(chip, self.core, self.n + d, self.n + chip, self.place(self.pos, 1 - self.core))

    def start(self):
        for d in range(1, self.n):
            self.out(d).start()
        self.hand(0).start()

    def hand_over(self):
        for d in range(1, self.n):
            chip = (self.pos + d) % self.n
            self.copy(chip, self.core, 0, chip, self.place(self.pos, self.core)).wait_recv()
            self.hand(d).start()

    def wait_other(self):
        for d in range(self.n):
            chip = (self.pos + d) % self.n
            self.copy(chip, 1 - self.core, 0, self.n + chip, self.place(self.pos, self.core)).wait_recv()

    def done(self):
        for d in range(1, self.n):
            self.out(d).wait_send()
        for d in range(self.n):
            self.hand(d).wait_send()


def kernel(
    Z, X, Y,
    events, keep, lengths, cotangent, w_in, w_out,
    out, grad_events, grad_w_out,
    keep_v, e_all, act_all, do_all, cot_all, w_in_v, w_out_v, slope_v, gg_v, gu_v, att_v, dq_v, dk_v, dv_v, ge_v,
    g_v, p_v, w_v, gt_send, gt_all, z_send, z_recv, c_recv,
    plane_sem, z_sem, local_sem, e_ssem, e_rsem, d_ssem, d_rsem, cot_ssem, cot_rsem, gt_ssem, gt_rsem, z_ssem, z_rsem, c_ssem, c_rsem,
):
    R = events.shape[0]
    D = events.shape[1]
    PAIR = 2 * R
    S = 2 * X
    ZH = Z // 2
    RD = D // (Z * X)
    scale = 1.0 / math.sqrt(DH)
    dp, ctx = lax.axis_index("dp"), lax.axis_index("ctx")
    z, x = dp // X, dp % X
    y, core = ctx // 2, ctx % 2
    other = 1 - core
    sib = y * 2 + other
    mine = x * 2 + core

    def block(b):
        return pl.ds(pl.multiple_of(b * R, R), R)

    def pair(c):
        return pl.ds(pl.multiple_of(c * PAIR, PAIR), PAIR)

    rows = block(ctx)

    ev_copy = pltpu.make_async_copy(events, e_all.at[rows], local_sem.at[0])
    ev_copy.start()
    keep_copy = pltpu.make_async_copy(keep, keep_v, local_sem.at[7])
    keep_copy.start()
    barrier = pltpu.get_barrier_semaphore()

    def greet(dp_to, ctx_to):
        pl.semaphore_signal(barrier, inc=1, device_id=(dp_to, ctx_to), device_id_type=MESH)

    for k in range(1, Y):
        greet(dp, ((y + k) % Y) * 2)
    for k in range(1, X):
        greet(z * X + (x + k) % X, y * 2)

    @pl.when(core == 1)
    def _():
        greet(dp, y * 2)

    @pl.when(core == z // ZH)
    def _():
        for k in range(1, Z):
            greet(((z + k) % Z) * X + x, y * 2 + 1)

    cot_copy = pltpu.make_async_copy(cotangent, cot_all.at[block(mine)], local_sem.at[1])
    cot_copy.start()
    w_copies = []
    for g in range(4):
        cols = pl.ds(g * WIDTH, WIDTH)
        w_copies.append(pltpu.make_async_copy(w_in.at[:, cols], w_in_v.at[:, cols], local_sem.at[2 + g]))
    for copy in w_copies:
        copy.start()
    wo_copy = pltpu.make_async_copy(w_out, w_out_v, local_sem.at[6])
    wo_copy.start()

    ev_copy.wait()
    keep_copy.wait()
    lane = lax.broadcasted_iota(jnp.int32, (1, R), 1)
    live_row = jnp.where((keep_v[...] == 1) & (ctx * R + lane < lengths[0]), 1.0, 0.0)
    eye = lax.broadcasted_iota(jnp.int32, (R, R), 0) == lax.broadcasted_iota(jnp.int32, (R, R), 1)
    live = jnp.sum(jnp.where(eye, live_row, 0.0), axis=1, keepdims=True)
    e_all[rows, :] = (e_all[rows, :].astype(F32) * live).astype(BF16)

    @pl.when(core == 0)
    def _():
        pl.semaphore_wait(barrier, 2 * (Y - 1) + 2 * (X - 1) + 1)
        pl.semaphore_signal(plane_sem, inc=1, device_id=(dp, sib), device_id_type=MESH)

    @pl.when(core == 1)
    def _():
        pl.semaphore_wait(plane_sem, 1)


    def remote(buf, b, ssem, rsem, ctx_to):
        return pltpu.make_async_remote_copy(
            src_ref=buf.at[block(b)], dst_ref=buf.at[block(b)], send_sem=ssem, recv_sem=rsem.at[b],
            device_id=(dp, ctx_to), device_id_type=MESH,
        )

    def arrived(buf, b, ssem, rsem):
        remote(buf, b, ssem.at[0], rsem, sib).wait_recv()

    def each(low, high, body):
        def step(k, _):
            body(k)
            return _
        lax.fori_loop(low, high, step, 0)

    e_ring = Ring(e_all, R, Y, y, core, e_ssem, e_rsem, lambda chip, c: (dp, chip * 2 + c))
    c_star = Star(cot_all, R, X, x, core, cot_ssem, cot_rsem, lambda chip, c: (z * X + chip, y * 2 + c))
    e_ring.start(e_ring.first())
    cot_copy.wait()

    own = e_all[rows, :]
    for g in range(4):
        w_copies[g].wait()
        for half in range(2):
            cols = pl.ds(g * WIDTH + half * 256, 256)
            a, slope = silu_parts(mul(own, w_in_v[:, cols]))
            act_all[rows, cols] = a.astype(BF16)
            slope_v[:, cols] = slope
    e_ring.start(e_ring.second())
    c_star.start()
    wo_copy.wait()
    gg_v[...] = mul_t(cot_all[block(mine), :], w_out_v[...])

    def project(b, *bases):
        for base in bases:
            for half in range(2):
                cols = pl.ds(base + half * 256, 256)
                a, _ = silu_parts(mul(e_all[block(b), :], w_in_v[:, cols]))
                act_all[block(b), cols] = a.astype(BF16)

    def head(base, h):
        return pl.ds(base + h * DH, DH)

    def allowed(query_major):
        first = lax.broadcasted_iota(jnp.int32, (R, PAIR), 0) + core * R
        second = lax.broadcasted_iota(jnp.int32, (R, PAIR), 1)
        return first >= second if query_major else second >= first

    def forward(c):
        for h in range(HEADS):
            s = mul_t(act_all[rows, head(Q_COL, h)], act_all[pair(c), head(K_COL, h)]) * scale
            a, slope = silu_parts(s)
            ok = allowed(True)
            g_v[c, h] = jnp.where(ok, slope * scale, 0.0)
            w_v[h] = jnp.where(ok, a, 0.0).astype(BF16)
        att_v[...] = jnp.concatenate([mul(w_v[h], act_all[pair(c), head(V_COL, h)]) for h in range(HEADS)], axis=1)

    def forward_block(c, k):
        cols = pl.ds(pl.multiple_of(k * R, R), R)
        keys = block(c * 2 + k)
        for h in range(HEADS):
            a, slope = silu_parts(mul_t(act_all[rows, head(Q_COL, h)], act_all[keys, head(K_COL, h)]) * scale)
            g_v[c, h, :, cols] = slope * scale
            w_v[h, :, pl.ds(0, R)] = a.astype(BF16)
        att_v[...] += jnp.concatenate(
            [mul(w_v[h, :, pl.ds(0, R)], act_all[keys, head(V_COL, h)]) for h in range(HEADS)], axis=1
        )

    def prepare(c):
        for h in range(HEADS):
            s = mul_t(act_all[rows, head(K_COL, h)], act_all[pair(c), head(Q_COL, h)]) * scale
            a, slope = silu_parts(s)
            ok = allowed(False)
            g_v[c + 1, h] = jnp.where(ok, slope * scale, 0.0)
            p_v[c, h] = jnp.where(ok, a, 0.0).astype(BF16)

    def prepare_block(c, k):
        cols = pl.ds(pl.multiple_of(k * R, R), R)
        for h in range(HEADS):
            s = mul_t(act_all[rows, head(K_COL, h)], act_all[block(c * 2 + k), head(Q_COL, h)]) * scale
            a, slope = silu_parts(s)
            g_v[c + 1, h, :, cols] = slope * scale
            p_v[c, h, :, cols] = a.astype(BF16)

    e_ring.wait_handed(y, other)
    project(sib, V_COL, Q_COL, K_COL)
    forward(y)
    prepare(y)
    if Y > 1:
        e_ring.relay()
        e_ring.hand_near()

    def take(c, k):
        @pl.when(c < y)
        def _():
            project(c * 2 + k, V_COL, K_COL)
            forward_block(c, k)

        @pl.when(c > y)
        def _():
            project(c * 2 + k, Q_COL)
            prepare_block(c, k)

    def forward_two(c, d, k):
        one, two = block(c * 2 + k), block(d * 2 + k)
        cols = pl.ds(pl.multiple_of(k * R, R), R)
        both = jnp.concatenate([e_all[one, :], e_all[two, :]], axis=0)
        for base in (K_COL, V_COL):
            for half in range(2):
                at = pl.ds(base + half * 256, 256)
                a, _ = silu_parts(mul(both, w_in_v[:, at]))
                act_all[one, at] = a[:R].astype(BF16)
                act_all[two, at] = a[R:].astype(BF16)

        def pick(base, h):
            return jnp.concatenate([act_all[one, head(base, h)], act_all[two, head(base, h)]], axis=0)

        for h in range(HEADS):
            a, slope = silu_parts(mul_t(act_all[rows, head(Q_COL, h)], pick(K_COL, h)) * scale)
            g_v[c, h, :, cols] = slope[:, :R] * scale
            g_v[d, h, :, cols] = slope[:, R:] * scale
            w_v[h] = a.astype(BF16)
        att_v[...] += jnp.concatenate([mul(w_v[h], pick(V_COL, h)) for h in range(HEADS)], axis=1)

    def near_step(j):
        k = other + j * (core - other)

        @pl.when(j == 1)
        def _():
            e_ring.wait_handed(e_ring.r, k)
            e_ring.wait_handed(e_ring.l, k)

        @pl.when(y == Y - 1)
        def _():
            forward_two(e_ring.r, e_ring.l, k)

        @pl.when(y < Y - 1)
        def _():
            each(0, 2, lambda n: take((y + 1 + 2 * n) % Y, k))

    def far_step(j):
        k = core + j * (other - core)

        @pl.when(j == 1)
        def _():
            e_ring.wait_handed(e_ring.f, k)

        take(e_ring.f, k)

    if Y > 1:
        each(0, 2, near_step)
        e_ring.hand_far()
        each(0, 2, far_step)

    att = att_v[...]
    cen = att - jnp.mean(att, axis=1, keepdims=True)
    inv = lax.rsqrt(jnp.mean(cen * cen, axis=1, keepdims=True) + EPSILON)
    normed = cen * inv
    gate = act_all[rows, pl.ds(U_COL, WIDTH)].astype(F32)
    gated = normed * gate

    turned = jnp.transpose(gated).reshape(Z, X, RD, R)
    for to in range(X):
        gt_send[to] = turned[:, to].reshape(Z * RD, R).astype(BF16)

    def gt_part(s):
        return gt_all.at[:, block(s)]

    def gt_piece(c):
        return pl.ds(pl.multiple_of(c * (ZH * RD), ZH * RD), ZH * RD)

    def gt_out(d, swap):
        to = (x + d) % X
        c = other if swap else core
        return pltpu.make_async_remote_copy(
            src_ref=gt_send.at[to, gt_piece(c)], dst_ref=gt_part(mine),
            send_sem=gt_ssem.at[2 * d + swap], recv_sem=gt_rsem.at[mine],
            device_id=(z * X + to, y * 2 + c), device_id_type=MESH,
        )

    def gt_in(d, swap):
        source = ((x + d) % X) * 2 + (other if swap else core)
        return pltpu.make_async_remote_copy(
            src_ref=gt_send.at[x, gt_piece(core)], dst_ref=gt_part(source),
            send_sem=gt_ssem.at[2 * d + swap], recv_sem=gt_rsem.at[source],
            device_id=(dp, sib), device_id_type=MESH,
        )

    gt_order = [(d, swap) for d in sorted(range(1, X), key=lambda d: -min(d, X - d)) for swap in range(2)] + [(0, 1)]
    for d, swap in gt_order[:2]:
        gt_out(d, swap).start()
    gt_all[:, block(mine)] = gt_send[x, gt_piece(core), :]

    gg = gg_v[...]
    gn = gg * gate
    grad_att = (
        gn - jnp.mean(gn, axis=1, keepdims=True) - normed * jnp.mean(gn * normed, axis=1, keepdims=True)
    ) * inv * live
    do_all[rows, :] = grad_att.astype(BF16)
    for d, swap in gt_order[2:]:
        gt_out(d, swap).start()

    def d_out(c):
        return remote(do_all, ctx, d_ssem.at[c], d_rsem, c * 2 + core)

    d_sib = remote(do_all, ctx, d_ssem.at[y], d_rsem, sib)
    d_sib.start()
    each(0, y, lambda c: d_out(c).start())


    @pl.when(core == 1)
    def _():
        pl.semaphore_wait(barrier, Z - 1)
        pl.semaphore_signal(z_sem, inc=1, device_id=(dp, sib), device_id_type=MESH)

    c_star.hand_over()
    c_star.wait_other()
    for d, swap in gt_order:
        gt_in(d, swap).wait_recv()
    gram = mul(gt_all[...], cot_all[...]).reshape(ZH, RD, D)
    z_send[...] = jnp.concatenate([gram[:, :, : D // 2], gram[:, :, D // 2 :]], axis=1).astype(BF16)

    def z_out(k):
        return pltpu.make_async_remote_copy(
            src_ref=z_send.at[k], dst_ref=z_recv.at[z], send_sem=z_ssem.at[k], recv_sem=z_rsem.at[z],
            device_id=((core * ZH + k) * X + x, ctx), device_id_type=MESH,
        )

    def z_in(k):
        return pltpu.make_async_remote_copy(
            src_ref=z_send.at[0], dst_ref=z_recv.at[k], send_sem=z_ssem.at[0], recv_sem=z_rsem.at[k],
            device_id=(k * X + x, ctx), device_id_type=MESH,
        )

    def z_start(distances):
        for d in distances:
            to = (z + d) % Z

            @pl.when(to // ZH == core)
            def _():
                z_out(to % ZH).start()

    z_order = sorted(range(1, Z), key=lambda d: -min(d, Z - d))

    @pl.when(core == 0)
    def _():
        pl.semaphore_wait(z_sem, 1)

    z_start(z_order[:5])

    out[...] = mul(gated.astype(BF16), w_out_v[...]).astype(BF16)
    gu_v[...] = gg * normed
    z_start(z_order[5:9])

    dq_v[...] = jnp.zeros_like(dq_v)
    dk_v[...] = jnp.zeros_like(dk_v)
    dv_v[...] = jnp.zeros_like(dv_v)

    def query_step(c):
        for h in range(HEADS):
            gw = mul_t(do_all[rows, head(0, h)], act_all[pair(c), head(V_COL, h)])
            gs = (gw * g_v[c, h]).astype(BF16)
            dq_v[:, head(0, h)] += mul(gs, act_all[pair(c), head(K_COL, h)])

    each(0, y + 1, query_step)

    z_start(z_order[9:])

    def back(grad, base):
        cols = pl.ds(base, WIDTH)
        return mul_t((grad * slope_v[:, cols]).astype(BF16), w_in_v[:, cols])

    ge_v[...] = back(gu_v[...], U_COL) + back(dq_v[...], Q_COL)

    def key_step(c):
        for h in range(HEADS):
            do_h = do_all[pair(c), head(0, h)]
            gw = mul_t(act_all[rows, head(V_COL, h)], do_h)
            gs = (gw * g_v[c + 1, h]).astype(BF16)
            dv_v[:, head(0, h)] += mul(p_v[c, h], do_h)
            dk_v[:, head(0, h)] += mul(gs, act_all[pair(c), head(Q_COL, h)])

    arrived(do_all, sib, d_ssem, d_rsem)
    key_step(y)

    def hand_over(c):
        return remote(do_all, c * 2 + core, d_ssem.at[Y + c], d_rsem, sib)

    def later_chip(c):
        arrived(do_all, c * 2 + core, d_ssem, d_rsem)
        hand_over(c).start()
        arrived(do_all, c * 2 + other, d_ssem, d_rsem)
        key_step(c)

    each(y + 1, Y, later_chip)

    grad_events[...] = (ge_v[...] + back(dv_v[...], V_COL) + back(dk_v[...], K_COL)).astype(BF16)

    holder = z // ZH
    c_order = sorted(range(1, 2 * Y), key=lambda k: -min(k, 2 * Y - k))

    def c_out(k):
        return pltpu.make_async_remote_copy(
            src_ref=c_recv.at[y], dst_ref=c_recv.at[y], send_sem=c_ssem.at[k], recv_sem=c_rsem.at[y],
            device_id=(dp, (ctx + k) % (2 * Y)), device_id_type=MESH,
        )

    def c_in(k):
        return pltpu.make_async_remote_copy(
            src_ref=c_recv.at[k], dst_ref=c_recv.at[k], send_sem=c_ssem.at[0], recv_sem=c_rsem.at[k],
            device_id=(dp, sib), device_id_type=MESH,
        )

    e_ring.done()
    c_star.done()
    d_sib.wait_send()
    each(0, y, lambda c: d_out(c).wait_send())
    each(y + 1, Y, lambda c: hand_over(c).wait_send())
    for d, swap in gt_order:
        gt_out(d, swap).wait_send()

    def z_done(k):
        @pl.when(core * ZH + k != z)
        def _():
            z_out(k).wait_send()

    each(0, ZH, z_done)

    @pl.when(core == holder)
    def _():
        z_recv[z] = z_send[z % ZH]

        def wait_z(k):
            @pl.when(k != z)
            def _():
                z_in(k).wait_recv()

        each(0, Z, wait_z)
        total = jnp.sum(z_recv[...].astype(F32), axis=0)
        c_recv[y] = total.astype(BF16)
        for k in c_order:
            c_out(k).start()

    def wait_c(k):
        @pl.when(k * 2 + holder != ctx)
        def _():
            c_in(k).wait_recv()

    each(0, Y, wait_c)
    tokens = R * 2 * Y * Z * X
    total = jnp.sum(c_recv[...].astype(F32), axis=0) * (1.0 / math.sqrt(tokens))
    grad_w_out[...] = jnp.concatenate([total[:RD], total[RD:]], axis=1)

    @pl.when(core == holder)
    def _():
        each(1, 2 * Y, lambda k: c_out(k).wait_send())


def in_hbm(a):
    return pltpu.with_memory_space_constraint(a, pltpu.HBM)


def store(*refs):
    copies = [pltpu.make_async_copy(refs[n], refs[3 + n], refs[6].at[n]) for n in range(3)]
    for copy in copies:
        copy.start()
    for copy in copies:
        copy.wait()


def build(mesh, X):
    Z, Y = mesh.shape["dp"] // X, mesh.shape["ctx"] // 2

    def per_device(events, keep, lengths, cotangent, w_in, w_out):
        R, D = events.shape[1:]
        L = R * 2 * Y
        S = 2 * X
        ZH, RD = Z // 2, D // (Z * X)
        vmem = pl.BlockSpec(memory_space=pltpu.VMEM)
        hbm = pl.BlockSpec(memory_space=pltpu.HBM)
        dma = pltpu.SemaphoreType.DMA
        output, grad_events, grad_w_out = pl.pallas_call(
            functools.partial(kernel, Z, X, Y),
            out_shape=(pltpu.VMEM((R, D), BF16), pltpu.VMEM((R, D), BF16), pltpu.VMEM((RD, D), F32)),
            in_specs=[hbm, hbm, pl.BlockSpec(memory_space=pltpu.SMEM), hbm, hbm, hbm],
            out_specs=[vmem] * 3,
            scratch_shapes=[
                pltpu.VMEM((1, R), jnp.int32),
                pltpu.VMEM((L, D), BF16),
                pltpu.VMEM((L, 4 * WIDTH), BF16),
                pltpu.VMEM((L, WIDTH), BF16),
                pltpu.VMEM((S * R, D), BF16),
                pltpu.VMEM((D, 4 * WIDTH), BF16),
                pltpu.VMEM((WIDTH, D), BF16),
                pltpu.VMEM((R, 4 * WIDTH), F32),
                pltpu.VMEM((R, WIDTH), F32),
                pltpu.VMEM((R, WIDTH), F32),
                pltpu.VMEM((R, WIDTH), F32),
                pltpu.VMEM((R, WIDTH), F32),
                pltpu.VMEM((R, WIDTH), F32),
                pltpu.VMEM((R, WIDTH), F32),
                pltpu.VMEM((R, D), F32),
                pltpu.VMEM((Y + 1, HEADS, R, 2 * R), F32),
                pltpu.VMEM((Y, HEADS, R, 2 * R), BF16),
                pltpu.VMEM((HEADS, R, 2 * R), BF16),
                pltpu.VMEM((X, Z * RD, R), BF16),
                pltpu.VMEM((ZH * RD, S * R), BF16),
                pltpu.VMEM((ZH, 2 * RD, D // 2), BF16),
                pltpu.VMEM((Z, 2 * RD, D // 2), BF16),
                pltpu.VMEM((Y, 2 * RD, D // 2), BF16),
                pltpu.SemaphoreType.REGULAR, pltpu.SemaphoreType.REGULAR,
                dma((8,)),
                dma((20,)), dma((6 * Y,)),
                dma((2 * Y,)), dma((2 * Y,)),
                dma((2 * X,)), dma((2 * X,)),
                dma((S,)), dma((S,)),
                dma((ZH,)), dma((Z,)),
                dma((2 * Y,)), dma((Y,)),
            ],
            compiler_params=pltpu.CompilerParams(
                collective_id=0, has_side_effects=True, vmem_limit_bytes=56 * 1024 * 1024
            ),
            name="layer",
        )(in_hbm(events[0]), in_hbm(keep), lengths, in_hbm(cotangent[0]), in_hbm(w_in), in_hbm(w_out))
        output, grad_events, grad_w_out = pl.pallas_call(
            store,
            out_shape=(
                jax.ShapeDtypeStruct((R, D), BF16),
                jax.ShapeDtypeStruct((R, D), BF16),
                jax.ShapeDtypeStruct((RD, D), F32),
            ),
            in_specs=[vmem] * 3,
            out_specs=(hbm, hbm, hbm),
            scratch_shapes=[dma((3,))],
            name="store",
        )(*[pltpu.with_memory_space_constraint(a, pltpu.VMEM) for a in (output, grad_events, grad_w_out)])
        return (output[None], grad_events[None], grad_w_out)

    return jax.shard_map(
        per_device,
        mesh=mesh,
        in_specs=(P("dp", "ctx", None), P("dp", "ctx"), P("dp"), P("dp", "ctx", None), P(), P()),
        out_specs=(P("dp", "ctx", None), P("dp", "ctx", None), P("dp", None)),
        check_vma=False,
    )


def solution(mesh):
    return build(mesh, X_CHIPS)
```

```python
import functools
import math

import jax
import jax.numpy as jnp
from jax import lax
from jax.experimental import pallas as pl
from jax.experimental.pallas import tpu as pltpu
from jax.sharding import PartitionSpec as P

HEADS = 4
DH = 128
WIDTH = HEADS * DH
X_CHIPS = 4
EPSILON = 1e-06
MESH = pl.DeviceIdType.MESH
F32 = jnp.float32
BF16 = jnp.bfloat16
U_COL, V_COL, Q_COL, K_COL = 0, WIDTH, 2 * WIDTH, 3 * WIDTH


def silu_parts(v):
    s = 0.5 * jnp.tanh(0.5 * v) + 0.5
    a = v * s
    return a, s + a * (1.0 - s)


def mul(a, b):
    return jnp.dot(a, b, preferred_element_type=F32)


def mul_t(a, b):
    return lax.dot_general(a, b, (((1,), (1,)), ((), ())), preferred_element_type=F32)


class Ring:
    def __init__(self, buf, rows, n, pos, core, ssem, rsem, place):
        self.buf, self.rows, self.n, self.pos, self.core = buf, rows, n, pos, core
        self.ssem, self.rsem = ssem, rsem
        self.other = 1 - core
        self.sib = place(pos, self.other)
        self.right, self.left = place((pos + 1) % n, self.other), place((pos + n - 1) % n, self.other)
        self.l, self.r, self.f = (pos + n - 1) % n, (pos + 1) % n, (pos + 2) % n

    def copy(self, chip, core, first, count, k, sem, to):
        rows = self.rows // 4
        start = pl.multiple_of((chip * 2 + core) * self.rows + first * rows, rows)
        part = self.buf.at[pl.ds(start, count * rows)]
        return pltpu.make_async_remote_copy(
            src_ref=part, dst_ref=part, send_sem=self.ssem.at[k], recv_sem=self.rsem.at[sem],
            device_id=to, device_id_type=MESH,
        )

    def quarter(self, chip, core, q, k, to):
        return self.copy(chip, core, q, 1, k, chip * 4 + q, to)

    def hand(self, chip, core, half, k):
        return self.copy(chip, core, half * 2, 2, k, 4 * self.n + chip * 2 + half, self.sib)

    def first(self):
        near = []
        if self.n > 1:
            for n in range(2):
                near.append(self.quarter(self.pos, self.core, n, 2 + n, self.right))
                near.append(self.quarter(self.pos, self.core, n + 2, 6 + n, self.left))
        return near + [self.hand(self.pos, self.core, half, half) for half in range(2)]

    def second(self):
        near = []
        if self.n > 1:
            for n in range(2):
                near.append(self.quarter(self.pos, self.core, n + 2, 4 + n, self.right))
                near.append(self.quarter(self.pos, self.core, n, 8 + n, self.left))
        return near

    def passed(self):
        steps = []
        for n in range(2):
            steps.append((self.l, n, self.quarter(self.l, self.other, n, 10 + n, self.right)))
            steps.append((self.r, 2 + n, self.quarter(self.r, self.other, 2 + n, 12 + n, self.left)))
        return steps

    def wait(self, chip, core, first, count=1):
        for q in range(first, first + count):
            self.quarter(chip, core, q, 0, self.sib).wait_recv()

    def wait_handed(self, chip, core):
        for half in range(2):
            self.hand(chip, core, half, 0).wait_recv()

    def start(self, copies):
        for copy in copies:
            copy.start()

    def relay(self):
        for chip, q, copy in self.passed():
            self.wait(chip, self.other, q)
            copy.start()

    def hand_near(self):
        self.hand(self.l, self.other, 0, 14).start()
        self.hand(self.r, self.other, 1, 17).start()
        self.wait(self.l, self.other, 2, 2)
        self.hand(self.l, self.other, 1, 15).start()
        self.wait(self.r, self.other, 0, 2)
        self.hand(self.r, self.other, 0, 16).start()

    def hand_far(self):
        for half in range(2):
            self.wait(self.f, self.core, half * 2, 2)
            self.hand(self.f, self.core, half, 18 + half).start()

    def done(self):
        for copy in self.first() + self.second():
            copy.wait_send()
        if self.n > 1:
            for _, _, copy in self.passed():
                copy.wait_send()
            for n, chip in enumerate((self.l, self.r, self.f)):
                for half in range(2):
                    self.hand(chip, self.core if n == 2 else self.other, half, 14 + 2 * n + half).wait_send()


class Star:
    def __init__(self, buf, rows, n, pos, core, ssem, rsem, place):
        self.buf, self.rows, self.n, self.pos, self.core = buf, rows, n, pos, core
        self.ssem, self.rsem, self.place = ssem, rsem, place

    def copy(self, chip, core, k, sem, to):
        start = pl.multiple_of((chip * 2 + core) * self.rows, self.rows)
        part = self.buf.at[pl.ds(start, self.rows)]
        return pltpu.make_async_remote_copy(
            src_ref=part, dst_ref=part, send_sem=self.ssem.at[k], recv_sem=self.rsem.at[sem],
            device_id=to, device_id_type=MESH,
        )

    def out(self, d):
        return self.copy(self.pos, self.core, d, self.pos, self.place((self.pos + d) % self.n, self.core))

    def hand(self, d):
        chip = (self.pos + d) % self.n
        return self.copy(chip, self.core, self.n + d, self.n + chip, self.place(self.pos, 1 - self.core))

    def start(self):
        for d in range(1, self.n):
            self.out(d).start()
        self.hand(0).start()

    def hand_over(self):
        for d in range(1, self.n):
            chip = (self.pos + d) % self.n
            self.copy(chip, self.core, 0, chip, self.place(self.pos, self.core)).wait_recv()
            self.hand(d).start()

    def wait_other(self):
        for d in range(self.n):
            chip = (self.pos + d) % self.n
            self.copy(chip, 1 - self.core, 0, self.n + chip, self.place(self.pos, self.core)).wait_recv()

    def done(self):
        for d in range(1, self.n):
            self.out(d).wait_send()
        for d in range(self.n):
            self.hand(d).wait_send()


def kernel(
    Z, X, Y,
    events, keep, lengths, cotangent, w_in, w_out,
    out, grad_events, grad_w_out,
    keep_v, e_all, act_all, do_all, cot_all, w_in_v, w_out_v, slope_v, gg_v, gu_v, att_v, dq_v, dk_v, dv_v, ge_v,
    g_v, p_v, w_v, gt_send, gt_all, z_send, z_recv, c_recv,
    plane_sem, z_sem, local_sem, e_ssem, e_rsem, d_ssem, d_rsem, cot_ssem, cot_rsem, gt_ssem, gt_rsem, z_ssem, z_rsem, c_ssem, c_rsem,
):
    R = events.shape[0]
    D = events.shape[1]
    PAIR = 2 * R
    S = 2 * X
    ZH = Z // 2
    RD = D // (Z * X)
    scale = 1.0 / math.sqrt(DH)
    dp, ctx = lax.axis_index("dp"), lax.axis_index("ctx")
    z, x = dp // X, dp % X
    y, core = ctx // 2, ctx % 2
    other = 1 - core
    sib = y * 2 + other
    mine = x * 2 + core

    def block(b):
        return pl.ds(pl.multiple_of(b * R, R), R)

    def pair(c):
        return pl.ds(pl.multiple_of(c * PAIR, PAIR), PAIR)

    rows = block(ctx)

    ev_copy = pltpu.make_async_copy(events, e_all.at[rows], local_sem.at[0])
    ev_copy.start()
    keep_copy = pltpu.make_async_copy(keep, keep_v, local_sem.at[7])
    keep_copy.start()
    barrier = pltpu.get_barrier_semaphore()

    def greet(dp_to, ctx_to):
        pl.semaphore_signal(barrier, inc=1, device_id=(dp_to, ctx_to), device_id_type=MESH)

    for k in range(1, Y):
        greet(dp, ((y + k) % Y) * 2)
    for k in range(1, X):
        greet(z * X + (x + k) % X, y * 2)

    @pl.when(core == 1)
    def _():
        greet(dp, y * 2)

    cot_copy = pltpu.make_async_copy(cotangent, cot_all.at[block(mine)], local_sem.at[1])
    cot_copy.start()
    w_copies = []
    for g in range(4):
        cols = pl.ds(g * WIDTH, WIDTH)
        w_copies.append(pltpu.make_async_copy(w_in.at[:, cols], w_in_v.at[:, cols], local_sem.at[2 + g]))
    for copy in w_copies:
        copy.start()
    wo_copy = pltpu.make_async_copy(w_out, w_out_v, local_sem.at[6])
    wo_copy.start()

    ev_copy.wait()
    keep_copy.wait()
    lane = lax.broadcasted_iota(jnp.int32, (1, R), 1)
    live_row = jnp.where((keep_v[...] == 1) & (ctx * R + lane < lengths[0]), 1.0, 0.0)
    eye = lax.broadcasted_iota(jnp.int32, (R, R), 0) == lax.broadcasted_iota(jnp.int32, (R, R), 1)
    live = jnp.sum(jnp.where(eye, live_row, 0.0), axis=1, keepdims=True)
    e_all[rows, :] = (e_all[rows, :].astype(F32) * live).astype(BF16)

    @pl.when(core == 0)
    def _():
        pl.semaphore_wait(barrier, 2 * (Y - 1) + 2 * (X - 1) + 1)
        pl.semaphore_signal(plane_sem, inc=1, device_id=(dp, sib), device_id_type=MESH)

    @pl.when(core == 1)
    def _():
        pl.semaphore_wait(plane_sem, 1)


    def remote(buf, b, ssem, rsem, ctx_to):
        return pltpu.make_async_remote_copy(
            src_ref=buf.at[block(b)], dst_ref=buf.at[block(b)], send_sem=ssem, recv_sem=rsem.at[b],
            device_id=(dp, ctx_to), device_id_type=MESH,
        )

    def arrived(buf, b, ssem, rsem):
        remote(buf, b, ssem.at[0], rsem, sib).wait_recv()

    def each(low, high, body):
        def step(k, _):
            body(k)
            return _
        lax.fori_loop(low, high, step, 0)

    e_ring = Ring(e_all, R, Y, y, core, e_ssem, e_rsem, lambda chip, c: (dp, chip * 2 + c))
    c_star = Star(cot_all, R, X, x, core, cot_ssem, cot_rsem, lambda chip, c: (z * X + chip, y * 2 + c))
    e_ring.start(e_ring.first())

    @pl.when(core == z // ZH)
    def _():
        for k in range(1, Z):
            greet(((z + k) % Z) * X + x, y * 2 + 1)

    cot_copy.wait()

    own = e_all[rows, :]
    for g in range(4):
        w_copies[g].wait()
        for half in range(2):
            cols = pl.ds(g * WIDTH + half * 256, 256)
            a, slope = silu_parts(mul(own, w_in_v[:, cols]))
            act_all[rows, cols] = a.astype(BF16)
            slope_v[:, cols] = slope
    e_ring.start(e_ring.second())
    c_star.start()

    def project(b, *bases):
        for base in bases:
            for half in range(2):
                cols = pl.ds(base + half * 256, 256)
                a, _ = silu_parts(mul(e_all[block(b), :], w_in_v[:, cols]))
                act_all[block(b), cols] = a.astype(BF16)

    def head(base, h):
        return pl.ds(base + h * DH, DH)

    def allowed(query_major):
        first = lax.broadcasted_iota(jnp.int32, (R, PAIR), 0) + core * R
        second = lax.broadcasted_iota(jnp.int32, (R, PAIR), 1)
        return first >= second if query_major else second >= first

    def forward(c):
        for h in range(HEADS):
            s = mul_t(act_all[rows, head(Q_COL, h)], act_all[pair(c), head(K_COL, h)]) * scale
            a, slope = silu_parts(s)
            ok = allowed(True)
            g_v[c, h] = jnp.where(ok, slope * scale, 0.0)
            w_v[h] = jnp.where(ok, a, 0.0).astype(BF16)
        att_v[...] = jnp.concatenate([mul(w_v[h], act_all[pair(c), head(V_COL, h)]) for h in range(HEADS)], axis=1)

    def forward_block(c, k):
        cols = pl.ds(pl.multiple_of(k * R, R), R)
        keys = block(c * 2 + k)
        for h in range(HEADS):
            a, slope = silu_parts(mul_t(act_all[rows, head(Q_COL, h)], act_all[keys, head(K_COL, h)]) * scale)
            g_v[c, h, :, cols] = slope * scale
            w_v[h, :, pl.ds(0, R)] = a.astype(BF16)
        att_v[...] += jnp.concatenate(
            [mul(w_v[h, :, pl.ds(0, R)], act_all[keys, head(V_COL, h)]) for h in range(HEADS)], axis=1
        )

    def prepare(c):
        for h in range(HEADS):
            s = mul_t(act_all[rows, head(K_COL, h)], act_all[pair(c), head(Q_COL, h)]) * scale
            a, slope = silu_parts(s)
            ok = allowed(False)
            g_v[c + 1, h] = jnp.where(ok, slope * scale, 0.0)
            p_v[c, h] = jnp.where(ok, a, 0.0).astype(BF16)

    def prepare_block(c, k):
        cols = pl.ds(pl.multiple_of(k * R, R), R)
        for h in range(HEADS):
            s = mul_t(act_all[rows, head(K_COL, h)], act_all[block(c * 2 + k), head(Q_COL, h)]) * scale
            a, slope = silu_parts(s)
            g_v[c + 1, h, :, cols] = slope * scale
            p_v[c, h, :, cols] = a.astype(BF16)

    e_ring.wait_handed(y, other)
    project(sib, V_COL, Q_COL, K_COL)
    if Y > 1:
        e_ring.relay()
    forward(y)
    prepare(y)
    wo_copy.wait()
    gg_v[...] = mul_t(cot_all[block(mine), :], w_out_v[...])
    if Y > 1:
        e_ring.hand_near()

    def take(c, k):
        @pl.when(c < y)
        def _():
            project(c * 2 + k, V_COL, K_COL)
            forward_block(c, k)

        @pl.when(c > y)
        def _():
            project(c * 2 + k, Q_COL)
            prepare_block(c, k)

    def forward_two(c, d, k):
        one, two = block(c * 2 + k), block(d * 2 + k)
        cols = pl.ds(pl.multiple_of(k * R, R), R)
        both = jnp.concatenate([e_all[one, :], e_all[two, :]], axis=0)
        for base in (K_COL, V_COL):
            for half in range(2):
                at = pl.ds(base + half * 256, 256)
                a, _ = silu_parts(mul(both, w_in_v[:, at]))
                act_all[one, at] = a[:R].astype(BF16)
                act_all[two, at] = a[R:].astype(BF16)

        def pick(base, h):
            return jnp.concatenate([act_all[one, head(base, h)], act_all[two, head(base, h)]], axis=0)

        for h in range(HEADS):
            a, slope = silu_parts(mul_t(act_all[rows, head(Q_COL, h)], pick(K_COL, h)) * scale)
            g_v[c, h, :, cols] = slope[:, :R] * scale
            g_v[d, h, :, cols] = slope[:, R:] * scale
            w_v[h] = a.astype(BF16)
        att_v[...] += jnp.concatenate([mul(w_v[h], pick(V_COL, h)) for h in range(HEADS)], axis=1)

    def near_step(j):
        k = other + j * (core - other)

        @pl.when(j == 1)
        def _():
            e_ring.wait_handed(e_ring.r, k)
            e_ring.wait_handed(e_ring.l, k)

        @pl.when(y == Y - 1)
        def _():
            forward_two(e_ring.r, e_ring.l, k)

        @pl.when(y < Y - 1)
        def _():
            each(0, 2, lambda n: take((y + 1 + 2 * n) % Y, k))

    def far_step(j):
        k = core + j * (other - core)

        @pl.when(j == 1)
        def _():
            e_ring.wait_handed(e_ring.f, k)

        take(e_ring.f, k)

    if Y > 1:
        each(0, 2, near_step)
        e_ring.hand_far()
        each(0, 2, far_step)

    att = att_v[...]
    cen = att - jnp.mean(att, axis=1, keepdims=True)
    inv = lax.rsqrt(jnp.mean(cen * cen, axis=1, keepdims=True) + EPSILON)
    normed = cen * inv
    gate = act_all[rows, pl.ds(U_COL, WIDTH)].astype(F32)
    gated = normed * gate

    turned = jnp.transpose(gated).reshape(Z, X, RD, R)
    for to in range(X):
        gt_send[to] = turned[:, to].reshape(Z * RD, R).astype(BF16)

    def gt_part(s):
        return gt_all.at[:, block(s)]

    def gt_piece(c):
        return pl.ds(pl.multiple_of(c * (ZH * RD), ZH * RD), ZH * RD)

    def gt_out(d, swap):
        to = (x + d) % X
        c = other if swap else core
        return pltpu.make_async_remote_copy(
            src_ref=gt_send.at[to, gt_piece(c)], dst_ref=gt_part(mine),
            send_sem=gt_ssem.at[2 * d + swap], recv_sem=gt_rsem.at[mine],
            device_id=(z * X + to, y * 2 + c), device_id_type=MESH,
        )

    def gt_in(d, swap):
        source = ((x + d) % X) * 2 + (other if swap else core)
        return pltpu.make_async_remote_copy(
            src_ref=gt_send.at[x, gt_piece(core)], dst_ref=gt_part(source),
            send_sem=gt_ssem.at[2 * d + swap], recv_sem=gt_rsem.at[source],
            device_id=(dp, sib), device_id_type=MESH,
        )

    gt_order = [(d, swap) for d in sorted(range(1, X), key=lambda d: -min(d, X - d)) for swap in range(2)] + [(0, 1)]
    for d, swap in gt_order[:2]:
        gt_out(d, swap).start()
    gt_all[:, block(mine)] = gt_send[x, gt_piece(core), :]

    gg = gg_v[...]
    gn = gg * gate
    grad_att = (
        gn - jnp.mean(gn, axis=1, keepdims=True) - normed * jnp.mean(gn * normed, axis=1, keepdims=True)
    ) * inv * live
    do_all[rows, :] = grad_att.astype(BF16)
    for d, swap in gt_order[2:]:
        gt_out(d, swap).start()

    def d_out(c):
        return remote(do_all, ctx, d_ssem.at[c], d_rsem, c * 2 + core)

    d_sib = remote(do_all, ctx, d_ssem.at[y], d_rsem, sib)
    d_sib.start()
    each(0, y, lambda c: d_out(c).start())


    @pl.when(core == 1)
    def _():
        pl.semaphore_wait(barrier, Z - 1)
        pl.semaphore_signal(z_sem, inc=1, device_id=(dp, sib), device_id_type=MESH)

    c_star.hand_over()
    c_star.wait_other()
    for d, swap in gt_order:
        gt_in(d, swap).wait_recv()
    gram = mul(gt_all[...], cot_all[...]).reshape(ZH, RD, D)
    z_send[...] = jnp.concatenate([gram[:, :, : D // 2], gram[:, :, D // 2 :]], axis=1).astype(BF16)

    def z_out(k):
        return pltpu.make_async_remote_copy(
            src_ref=z_send.at[k], dst_ref=z_recv.at[z], send_sem=z_ssem.at[k], recv_sem=z_rsem.at[z],
            device_id=((core * ZH + k) * X + x, ctx), device_id_type=MESH,
        )

    def z_in(k):
        return pltpu.make_async_remote_copy(
            src_ref=z_send.at[0], dst_ref=z_recv.at[k], send_sem=z_ssem.at[0], recv_sem=z_rsem.at[k],
            device_id=(k * X + x, ctx), device_id_type=MESH,
        )

    def z_start(distances):
        for d in distances:
            to = (z + d) % Z

            @pl.when(to // ZH == core)
            def _():
                z_out(to % ZH).start()

    z_order = sorted(range(1, Z), key=lambda d: -min(d, Z - d))

    @pl.when(core == 0)
    def _():
        pl.semaphore_wait(z_sem, 1)

    z_start(z_order[:7])

    out[...] = mul(gated.astype(BF16), w_out_v[...]).astype(BF16)
    gu_v[...] = gg * normed
    z_start(z_order[7:9])

    dq_v[...] = jnp.zeros_like(dq_v)
    dk_v[...] = jnp.zeros_like(dk_v)
    dv_v[...] = jnp.zeros_like(dv_v)

    def query_step(c):
        for h in range(HEADS):
            gw = mul_t(do_all[rows, head(0, h)], act_all[pair(c), head(V_COL, h)])
            gs = (gw * g_v[c, h]).astype(BF16)
            dq_v[:, head(0, h)] += mul(gs, act_all[pair(c), head(K_COL, h)])

    each(0, y + 1, query_step)

    z_start(z_order[9:])

    def back(grad, base):
        cols = pl.ds(base, WIDTH)
        return mul_t((grad * slope_v[:, cols]).astype(BF16), w_in_v[:, cols])

    ge_v[...] = back(gu_v[...], U_COL) + back(dq_v[...], Q_COL)

    def key_step(c):
        for h in range(HEADS):
            do_h = do_all[pair(c), head(0, h)]
            gw = mul_t(act_all[rows, head(V_COL, h)], do_h)
            gs = (gw * g_v[c + 1, h]).astype(BF16)
            dv_v[:, head(0, h)] += mul(p_v[c, h], do_h)
            dk_v[:, head(0, h)] += mul(gs, act_all[pair(c), head(Q_COL, h)])

    arrived(do_all, sib, d_ssem, d_rsem)
    key_step(y)

    def hand_over(c):
        return remote(do_all, c * 2 + core, d_ssem.at[Y + c], d_rsem, sib)

    def later_chip(c):
        arrived(do_all, c * 2 + core, d_ssem, d_rsem)
        hand_over(c).start()
        arrived(do_all, c * 2 + other, d_ssem, d_rsem)
        key_step(c)

    each(y + 1, Y, later_chip)

    grad_events[...] = (ge_v[...] + back(dv_v[...], V_COL) + back(dk_v[...], K_COL)).astype(BF16)

    holder = z // ZH
    c_order = sorted(range(1, 2 * Y), key=lambda k: -min(k, 2 * Y - k))

    def c_out(k):
        return pltpu.make_async_remote_copy(
            src_ref=c_recv.at[y], dst_ref=c_recv.at[y], send_sem=c_ssem.at[k], recv_sem=c_rsem.at[y],
            device_id=(dp, (ctx + k) % (2 * Y)), device_id_type=MESH,
        )

    def c_in(k):
        return pltpu.make_async_remote_copy(
            src_ref=c_recv.at[k], dst_ref=c_recv.at[k], send_sem=c_ssem.at[0], recv_sem=c_rsem.at[k],
            device_id=(dp, sib), device_id_type=MESH,
        )

    e_ring.done()
    c_star.done()
    d_sib.wait_send()
    each(0, y, lambda c: d_out(c).wait_send())
    each(y + 1, Y, lambda c: hand_over(c).wait_send())
    for d, swap in gt_order:
        gt_out(d, swap).wait_send()

    def z_done(k):
        @pl.when(core * ZH + k != z)
        def _():
            z_out(k).wait_send()

    each(0, ZH, z_done)

    @pl.when(core == holder)
    def _():
        z_recv[z] = z_send[z % ZH]

        def wait_z(k):
            @pl.when(k != z)
            def _():
                z_in(k).wait_recv()

        each(0, Z, wait_z)
        total = jnp.sum(z_recv[...].astype(F32), axis=0)
        c_recv[y] = total.astype(BF16)
        for k in c_order:
            c_out(k).start()

    def wait_c(k):
        @pl.when(k * 2 + holder != ctx)
        def _():
            c_in(k).wait_recv()

    each(0, Y, wait_c)
    tokens = R * 2 * Y * Z * X
    total = jnp.sum(c_recv[...].astype(F32), axis=0) * (1.0 / math.sqrt(tokens))
    grad_w_out[...] = jnp.concatenate([total[:RD], total[RD:]], axis=1)

    @pl.when(core == holder)
    def _():
        each(1, 2 * Y, lambda k: c_out(k).wait_send())


def in_hbm(a):
    return pltpu.with_memory_space_constraint(a, pltpu.HBM)


def store(*refs):
    copies = [pltpu.make_async_copy(refs[n], refs[3 + n], refs[6].at[n]) for n in range(3)]
    for copy in copies:
        copy.start()
    for copy in copies:
        copy.wait()


def build(mesh, X):
    Z, Y = mesh.shape["dp"] // X, mesh.shape["ctx"] // 2

    def per_device(events, keep, lengths, cotangent, w_in, w_out):
        R, D = events.shape[1:]
        L = R * 2 * Y
        S = 2 * X
        ZH, RD = Z // 2, D // (Z * X)
        vmem = pl.BlockSpec(memory_space=pltpu.VMEM)
        hbm = pl.BlockSpec(memory_space=pltpu.HBM)
        dma = pltpu.SemaphoreType.DMA
        output, grad_events, grad_w_out = pl.pallas_call(
            functools.partial(kernel, Z, X, Y),
            out_shape=(pltpu.VMEM((R, D), BF16), pltpu.VMEM((R, D), BF16), pltpu.VMEM((RD, D), F32)),
            in_specs=[hbm, hbm, pl.BlockSpec(memory_space=pltpu.SMEM), hbm, hbm, hbm],
            out_specs=[vmem] * 3,
            scratch_shapes=[
                pltpu.VMEM((1, R), jnp.int32),
                pltpu.VMEM((L, D), BF16),
                pltpu.VMEM((L, 4 * WIDTH), BF16),
                pltpu.VMEM((L, WIDTH), BF16),
                pltpu.VMEM((S * R, D), BF16),
                pltpu.VMEM((D, 4 * WIDTH), BF16),
                pltpu.VMEM((WIDTH, D), BF16),
                pltpu.VMEM((R, 4 * WIDTH), F32),
                pltpu.VMEM((R, WIDTH), F32),
                pltpu.VMEM((R, WIDTH), F32),
                pltpu.VMEM((R, WIDTH), F32),
                pltpu.VMEM((R, WIDTH), F32),
                pltpu.VMEM((R, WIDTH), F32),
                pltpu.VMEM((R, WIDTH), F32),
                pltpu.VMEM((R, D), F32),
                pltpu.VMEM((Y + 1, HEADS, R, 2 * R), F32),
                pltpu.VMEM((Y, HEADS, R, 2 * R), BF16),
                pltpu.VMEM((HEADS, R, 2 * R), BF16),
                pltpu.VMEM((X, Z * RD, R), BF16),
                pltpu.VMEM((ZH * RD, S * R), BF16),
                pltpu.VMEM((ZH, 2 * RD, D // 2), BF16),
                pltpu.VMEM((Z, 2 * RD, D // 2), BF16),
                pltpu.VMEM((Y, 2 * RD, D // 2), BF16),
                pltpu.SemaphoreType.REGULAR, pltpu.SemaphoreType.REGULAR,
                dma((8,)),
                dma((20,)), dma((6 * Y,)),
                dma((2 * Y,)), dma((2 * Y,)),
                dma((2 * X,)), dma((2 * X,)),
                dma((S,)), dma((S,)),
                dma((ZH,)), dma((Z,)),
                dma((2 * Y,)), dma((Y,)),
            ],
            compiler_params=pltpu.CompilerParams(
                collective_id=0, has_side_effects=True, vmem_limit_bytes=56 * 1024 * 1024
            ),
            name="layer",
        )(in_hbm(events[0]), in_hbm(keep), lengths, in_hbm(cotangent[0]), in_hbm(w_in), in_hbm(w_out))
        output, grad_events, grad_w_out = pl.pallas_call(
            store,
            out_shape=(
                jax.ShapeDtypeStruct((R, D), BF16),
                jax.ShapeDtypeStruct((R, D), BF16),
                jax.ShapeDtypeStruct((RD, D), F32),
            ),
            in_specs=[vmem] * 3,
            out_specs=(hbm, hbm, hbm),
            scratch_shapes=[dma((3,))],
            name="store",
        )(*[pltpu.with_memory_space_constraint(a, pltpu.VMEM) for a in (output, grad_events, grad_w_out)])
        return (output[None], grad_events[None], grad_w_out)

    return jax.shard_map(
        per_device,
        mesh=mesh,
        in_specs=(P("dp", "ctx", None), P("dp", "ctx"), P("dp"), P("dp", "ctx", None), P(), P()),
        out_specs=(P("dp", "ctx", None), P("dp", "ctx", None), P("dp", None)),
        check_vma=False,
    )


def solution(mesh):
    return build(mesh, X_CHIPS)
```

```python
import functools
import math

import jax
import jax.numpy as jnp
from jax import lax
from jax.experimental import pallas as pl
from jax.experimental.pallas import tpu as pltpu
from jax.sharding import PartitionSpec as P

HEADS = 4
DH = 128
WIDTH = HEADS * DH
X_CHIPS = 4
EPSILON = 1e-06
MESH = pl.DeviceIdType.MESH
F32 = jnp.float32
BF16 = jnp.bfloat16
U_COL, V_COL, Q_COL, K_COL = 0, WIDTH, 2 * WIDTH, 3 * WIDTH


def silu_parts(v):
    s = 0.5 * jnp.tanh(0.5 * v) + 0.5
    a = v * s
    return a, s + a * (1.0 - s)


def mul(a, b):
    return jnp.dot(a, b, preferred_element_type=F32)


def mul_t(a, b):
    return lax.dot_general(a, b, (((1,), (1,)), ((), ())), preferred_element_type=F32)


class Ring:
    def __init__(self, buf, rows, n, pos, core, ssem, rsem, place):
        self.buf, self.rows, self.n, self.pos, self.core = buf, rows, n, pos, core
        self.ssem, self.rsem = ssem, rsem
        self.other = 1 - core
        self.sib = place(pos, self.other)
        self.right, self.left = place((pos + 1) % n, self.other), place((pos + n - 1) % n, self.other)
        self.l, self.r, self.f = (pos + n - 1) % n, (pos + 1) % n, (pos + 2) % n

    def copy(self, chip, core, first, count, k, sem, to):
        rows = self.rows // 4
        start = pl.multiple_of((chip * 2 + core) * self.rows + first * rows, rows)
        part = self.buf.at[pl.ds(start, count * rows)]
        return pltpu.make_async_remote_copy(
            src_ref=part, dst_ref=part, send_sem=self.ssem.at[k], recv_sem=self.rsem.at[sem],
            device_id=to, device_id_type=MESH,
        )

    def quarter(self, chip, core, q, k, to):
        return self.copy(chip, core, q, 1, k, chip * 4 + q, to)

    def hand(self, chip, core, half, k):
        return self.copy(chip, core, half * 2, 2, k, 4 * self.n + chip * 2 + half, self.sib)

    def first(self):
        near = []
        if self.n > 1:
            for n in range(2):
                near.append(self.quarter(self.pos, self.core, n, 2 + n, self.right))
                near.append(self.quarter(self.pos, self.core, n + 2, 6 + n, self.left))
        return near + [self.hand(self.pos, self.core, half, half) for half in range(2)]

    def second(self):
        near = []
        if self.n > 1:
            for n in range(2):
                near.append(self.quarter(self.pos, self.core, n + 2, 4 + n, self.right))
                near.append(self.quarter(self.pos, self.core, n, 8 + n, self.left))
        return near

    def passed(self):
        steps = []
        for n in range(2):
            steps.append((self.l, n, self.quarter(self.l, self.other, n, 10 + n, self.right)))
            steps.append((self.r, 2 + n, self.quarter(self.r, self.other, 2 + n, 12 + n, self.left)))
        return steps

    def wait(self, chip, core, first, count=1):
        for q in range(first, first + count):
            self.quarter(chip, core, q, 0, self.sib).wait_recv()

    def wait_handed(self, chip, core):
        for half in range(2):
            self.hand(chip, core, half, 0).wait_recv()

    def start(self, copies):
        for copy in copies:
            copy.start()

    def relay(self):
        for chip, q, copy in self.passed():
            self.wait(chip, self.other, q)
            copy.start()

    def hand_near(self):
        self.hand(self.l, self.other, 0, 14).start()
        self.hand(self.r, self.other, 1, 17).start()
        self.wait(self.l, self.other, 2, 2)
        self.hand(self.l, self.other, 1, 15).start()
        self.wait(self.r, self.other, 0, 2)
        self.hand(self.r, self.other, 0, 16).start()

    def hand_far(self):
        for half in range(2):
            self.wait(self.f, self.core, half * 2, 2)
            self.hand(self.f, self.core, half, 18 + half).start()

    def done(self):
        for copy in self.first() + self.second():
            copy.wait_send()
        if self.n > 1:
            for _, _, copy in self.passed():
                copy.wait_send()
            for n, chip in enumerate((self.l, self.r, self.f)):
                for half in range(2):
                    self.hand(chip, self.core if n == 2 else self.other, half, 14 + 2 * n + half).wait_send()


class Star:
    def __init__(self, buf, rows, n, pos, core, ssem, rsem, place):
        self.buf, self.rows, self.n, self.pos, self.core = buf, rows, n, pos, core
        self.ssem, self.rsem, self.place = ssem, rsem, place

    def copy(self, chip, core, k, sem, to):
        start = pl.multiple_of((chip * 2 + core) * self.rows, self.rows)
        part = self.buf.at[pl.ds(start, self.rows)]
        return pltpu.make_async_remote_copy(
            src_ref=part, dst_ref=part, send_sem=self.ssem.at[k], recv_sem=self.rsem.at[sem],
            device_id=to, device_id_type=MESH,
        )

    def out(self, d):
        return self.copy(self.pos, self.core, d, self.pos, self.place((self.pos + d) % self.n, self.core))

    def hand(self, d):
        chip = (self.pos + d) % self.n
        return self.copy(chip, self.core, self.n + d, self.n + chip, self.place(self.pos, 1 - self.core))

    def start(self):
        for d in range(1, self.n):
            self.out(d).start()
        self.hand(0).start()

    def hand_over(self):
        for d in range(1, self.n):
            chip = (self.pos + d) % self.n
            self.copy(chip, self.core, 0, chip, self.place(self.pos, self.core)).wait_recv()
            self.hand(d).start()

    def wait_other(self):
        for d in range(self.n):
            chip = (self.pos + d) % self.n
            self.copy(chip, 1 - self.core, 0, self.n + chip, self.place(self.pos, self.core)).wait_recv()

    def done(self):
        for d in range(1, self.n):
            self.out(d).wait_send()
        for d in range(self.n):
            self.hand(d).wait_send()


def kernel(
    Z, X, Y,
    events, keep, lengths, cotangent, w_in, w_out,
    out, grad_events, grad_w_out,
    keep_v, e_all, act_all, do_all, cot_all, w_in_v, w_out_v, slope_v, gg_v, gu_v, att_v, dq_v, dk_v, dv_v, ge_v,
    g_v, p_v, w_v, gt_send, gt_all, z_send, z_recv, c_recv,
    plane_sem, z_sem, local_sem, e_ssem, e_rsem, d_ssem, d_rsem, cot_ssem, cot_rsem, gt_ssem, gt_rsem, z_ssem, z_rsem, c_ssem, c_rsem,
):
    R = events.shape[0]
    D = events.shape[1]
    PAIR = 2 * R
    S = 2 * X
    ZH = Z // 2
    RD = D // (Z * X)
    scale = 1.0 / math.sqrt(DH)
    dp, ctx = lax.axis_index("dp"), lax.axis_index("ctx")
    z, x = dp // X, dp % X
    y, core = ctx // 2, ctx % 2
    other = 1 - core
    sib = y * 2 + other
    mine = x * 2 + core

    def block(b):
        return pl.ds(pl.multiple_of(b * R, R), R)

    def pair(c):
        return pl.ds(pl.multiple_of(c * PAIR, PAIR), PAIR)

    rows = block(ctx)

    ev_copy = pltpu.make_async_copy(events, e_all.at[rows], local_sem.at[0])
    ev_copy.start()
    barrier = pltpu.get_barrier_semaphore()

    def greet(dp_to, ctx_to):
        pl.semaphore_signal(barrier, inc=1, device_id=(dp_to, ctx_to), device_id_type=MESH)

    for k in range(1, Y):
        greet(dp, ((y + k) % Y) * 2)
    for k in range(1, X):
        greet(z * X + (x + k) % X, y * 2)

    @pl.when(core == 1)
    def _():
        greet(dp, y * 2)

    keep_copy = pltpu.make_async_copy(keep, keep_v, local_sem.at[7])
    keep_copy.start()
    cot_copy = pltpu.make_async_copy(cotangent, cot_all.at[block(mine)], local_sem.at[1])
    cot_copy.start()
    w_copies = []
    for g in range(4):
        cols = pl.ds(g * WIDTH, WIDTH)
        w_copies.append(pltpu.make_async_copy(w_in.at[:, cols], w_in_v.at[:, cols], local_sem.at[2 + g]))
    for copy in w_copies:
        copy.start()
    wo_copy = pltpu.make_async_copy(w_out, w_out_v, local_sem.at[6])
    wo_copy.start()

    ev_copy.wait()
    keep_copy.wait()
    lane = lax.broadcasted_iota(jnp.int32, (1, R), 1)
    live_row = jnp.where((keep_v[...] == 1) & (ctx * R + lane < lengths[0]), 1.0, 0.0)
    eye = lax.broadcasted_iota(jnp.int32, (R, R), 0) == lax.broadcasted_iota(jnp.int32, (R, R), 1)
    live = jnp.sum(jnp.where(eye, live_row, 0.0), axis=1, keepdims=True)
    e_all[rows, :] = (e_all[rows, :].astype(F32) * live).astype(BF16)

    @pl.when(core == 0)
    def _():
        pl.semaphore_wait(barrier, 2 * (Y - 1) + 2 * (X - 1) + 1)
        pl.semaphore_signal(plane_sem, inc=1, device_id=(dp, sib), device_id_type=MESH)

    @pl.when(core == 1)
    def _():
        pl.semaphore_wait(plane_sem, 1)


    def remote(buf, b, ssem, rsem, ctx_to):
        return pltpu.make_async_remote_copy(
            src_ref=buf.at[block(b)], dst_ref=buf.at[block(b)], send_sem=ssem, recv_sem=rsem.at[b],
            device_id=(dp, ctx_to), device_id_type=MESH,
        )

    def arrived(buf, b, ssem, rsem):
        remote(buf, b, ssem.at[0], rsem, sib).wait_recv()

    def each(low, high, body):
        def step(k, _):
            body(k)
            return _
        lax.fori_loop(low, high, step, 0)

    e_ring = Ring(e_all, R, Y, y, core, e_ssem, e_rsem, lambda chip, c: (dp, chip * 2 + c))
    c_star = Star(cot_all, R, X, x, core, cot_ssem, cot_rsem, lambda chip, c: (z * X + chip, y * 2 + c))
    e_ring.start(e_ring.first())

    @pl.when(core == z // ZH)
    def _():
        for k in range(1, Z):
            greet(((z + k) % Z) * X + x, y * 2 + 1)

    cot_copy.wait()

    own = e_all[rows, :]
    for g in range(4):
        w_copies[g].wait()
        for half in range(2):
            cols = pl.ds(g * WIDTH + half * 256, 256)
            a, slope = silu_parts(mul(own, w_in_v[:, cols]))
            act_all[rows, cols] = a.astype(BF16)
            slope_v[:, cols] = slope
    e_ring.start(e_ring.second())
    c_star.start()

    def project(b, *bases):
        for base in bases:
            for half in range(2):
                cols = pl.ds(base + half * 256, 256)
                a, _ = silu_parts(mul(e_all[block(b), :], w_in_v[:, cols]))
                act_all[block(b), cols] = a.astype(BF16)

    def head(base, h):
        return pl.ds(base + h * DH, DH)

    def allowed(query_major):
        first = lax.broadcasted_iota(jnp.int32, (R, PAIR), 0) + core * R
        second = lax.broadcasted_iota(jnp.int32, (R, PAIR), 1)
        return first >= second if query_major else second >= first

    def forward(c):
        for h in range(HEADS):
            s = mul_t(act_all[rows, head(Q_COL, h)], act_all[pair(c), head(K_COL, h)]) * scale
            a, slope = silu_parts(s)
            ok = allowed(True)
            g_v[c, h] = jnp.where(ok, slope * scale, 0.0)
            w_v[h] = jnp.where(ok, a, 0.0).astype(BF16)
        att_v[...] = jnp.concatenate([mul(w_v[h], act_all[pair(c), head(V_COL, h)]) for h in range(HEADS)], axis=1)

    def forward_block(c, k):
        cols = pl.ds(pl.multiple_of(k * R, R), R)
        keys = block(c * 2 + k)
        for h in range(HEADS):
            a, slope = silu_parts(mul_t(act_all[rows, head(Q_COL, h)], act_all[keys, head(K_COL, h)]) * scale)
            g_v[c, h, :, cols] = slope * scale
            w_v[h, :, pl.ds(0, R)] = a.astype(BF16)
        att_v[...] += jnp.concatenate(
            [mul(w_v[h, :, pl.ds(0, R)], act_all[keys, head(V_COL, h)]) for h in range(HEADS)], axis=1
        )

    def prepare(c):
        for h in range(HEADS):
            s = mul_t(act_all[rows, head(K_COL, h)], act_all[pair(c), head(Q_COL, h)]) * scale
            a, slope = silu_parts(s)
            ok = allowed(False)
            g_v[c + 1, h] = jnp.where(ok, slope * scale, 0.0)
            p_v[c, h] = jnp.where(ok, a, 0.0).astype(BF16)

    def prepare_block(c, k):
        cols = pl.ds(pl.multiple_of(k * R, R), R)
        for h in range(HEADS):
            s = mul_t(act_all[rows, head(K_COL, h)], act_all[block(c * 2 + k), head(Q_COL, h)]) * scale
            a, slope = silu_parts(s)
            g_v[c + 1, h, :, cols] = slope * scale
            p_v[c, h, :, cols] = a.astype(BF16)

    e_ring.wait_handed(y, other)
    project(sib, V_COL, Q_COL, K_COL)
    if Y > 1:
        e_ring.relay()
    forward(y)
    prepare(y)
    wo_copy.wait()
    gg_v[...] = mul_t(cot_all[block(mine), :], w_out_v[...])
    if Y > 1:
        e_ring.hand_near()

    def take(c, k):
        @pl.when(c < y)
        def _():
            project(c * 2 + k, V_COL, K_COL)
            forward_block(c, k)

        @pl.when(c > y)
        def _():
            project(c * 2 + k, Q_COL)
            prepare_block(c, k)

    def forward_two(c, d, k):
        one, two = block(c * 2 + k), block(d * 2 + k)
        cols = pl.ds(pl.multiple_of(k * R, R), R)
        both = jnp.concatenate([e_all[one, :], e_all[two, :]], axis=0)
        for base in (K_COL, V_COL):
            for half in range(2):
                at = pl.ds(base + half * 256, 256)
                a, _ = silu_parts(mul(both, w_in_v[:, at]))
                act_all[one, at] = a[:R].astype(BF16)
                act_all[two, at] = a[R:].astype(BF16)

        def pick(base, h):
            return jnp.concatenate([act_all[one, head(base, h)], act_all[two, head(base, h)]], axis=0)

        for h in range(HEADS):
            a, slope = silu_parts(mul_t(act_all[rows, head(Q_COL, h)], pick(K_COL, h)) * scale)
            g_v[c, h, :, cols] = slope[:, :R] * scale
            g_v[d, h, :, cols] = slope[:, R:] * scale
            w_v[h] = a.astype(BF16)
        att_v[...] += jnp.concatenate([mul(w_v[h], pick(V_COL, h)) for h in range(HEADS)], axis=1)

    def near_step(j):
        k = other + j * (core - other)

        @pl.when(j == 1)
        def _():
            e_ring.wait_handed(e_ring.r, k)
            e_ring.wait_handed(e_ring.l, k)

        @pl.when(y == Y - 1)
        def _():
            forward_two(e_ring.r, e_ring.l, k)

        @pl.when(y < Y - 1)
        def _():
            each(0, 2, lambda n: take((y + 1 + 2 * n) % Y, k))

    def far_step(j):
        k = core + j * (other - core)

        @pl.when(j == 1)
        def _():
            e_ring.wait_handed(e_ring.f, k)

        take(e_ring.f, k)

    if Y > 1:
        each(0, 2, near_step)
        e_ring.hand_far()
        each(0, 2, far_step)

    att = att_v[...]
    cen = att - jnp.mean(att, axis=1, keepdims=True)
    inv = lax.rsqrt(jnp.mean(cen * cen, axis=1, keepdims=True) + EPSILON)
    normed = cen * inv
    gate = act_all[rows, pl.ds(U_COL, WIDTH)].astype(F32)
    gated = normed * gate

    turned = jnp.transpose(gated).reshape(Z, X, RD, R)
    for to in range(X):
        gt_send[to] = turned[:, to].reshape(Z * RD, R).astype(BF16)

    def gt_part(s):
        return gt_all.at[:, block(s)]

    def gt_piece(c):
        return pl.ds(pl.multiple_of(c * (ZH * RD), ZH * RD), ZH * RD)

    def gt_out(d, swap):
        to = (x + d) % X
        c = other if swap else core
        return pltpu.make_async_remote_copy(
            src_ref=gt_send.at[to, gt_piece(c)], dst_ref=gt_part(mine),
            send_sem=gt_ssem.at[2 * d + swap], recv_sem=gt_rsem.at[mine],
            device_id=(z * X + to, y * 2 + c), device_id_type=MESH,
        )

    def gt_in(d, swap):
        source = ((x + d) % X) * 2 + (other if swap else core)
        return pltpu.make_async_remote_copy(
            src_ref=gt_send.at[x, gt_piece(core)], dst_ref=gt_part(source),
            send_sem=gt_ssem.at[2 * d + swap], recv_sem=gt_rsem.at[source],
            device_id=(dp, sib), device_id_type=MESH,
        )

    gt_order = [(d, swap) for d in sorted(range(1, X), key=lambda d: -min(d, X - d)) for swap in range(2)] + [(0, 1)]
    for d, swap in gt_order:
        gt_out(d, swap).start()
    gt_all[:, block(mine)] = gt_send[x, gt_piece(core), :]

    gg = gg_v[...]
    gn = gg * gate
    grad_att = (
        gn - jnp.mean(gn, axis=1, keepdims=True) - normed * jnp.mean(gn * normed, axis=1, keepdims=True)
    ) * inv * live
    do_all[rows, :] = grad_att.astype(BF16)

    def d_out(c):
        return remote(do_all, ctx, d_ssem.at[c], d_rsem, c * 2 + core)

    d_sib = remote(do_all, ctx, d_ssem.at[y], d_rsem, sib)
    d_sib.start()
    each(0, y, lambda c: d_out(c).start())


    @pl.when(core == 1)
    def _():
        pl.semaphore_wait(barrier, Z - 1)
        pl.semaphore_signal(z_sem, inc=1, device_id=(dp, sib), device_id_type=MESH)

    c_star.hand_over()
    c_star.wait_other()
    for d, swap in gt_order:
        gt_in(d, swap).wait_recv()
    gram = mul(gt_all[...], cot_all[...]).reshape(ZH, RD, D)
    z_send[...] = jnp.concatenate([gram[:, :, : D // 2], gram[:, :, D // 2 :]], axis=1).astype(BF16)

    def z_out(k):
        return pltpu.make_async_remote_copy(
            src_ref=z_send.at[k], dst_ref=z_recv.at[z], send_sem=z_ssem.at[k], recv_sem=z_rsem.at[z],
            device_id=((core * ZH + k) * X + x, ctx), device_id_type=MESH,
        )

    def z_in(k):
        return pltpu.make_async_remote_copy(
            src_ref=z_send.at[0], dst_ref=z_recv.at[k], send_sem=z_ssem.at[0], recv_sem=z_rsem.at[k],
            device_id=(k * X + x, ctx), device_id_type=MESH,
        )

    def z_start(distances):
        for d in distances:
            to = (z + d) % Z

            @pl.when(to // ZH == core)
            def _():
                z_out(to % ZH).start()

    z_order = sorted(range(1, Z), key=lambda d: -min(d, Z - d))

    @pl.when(core == 0)
    def _():
        pl.semaphore_wait(z_sem, 1)

    z_start(z_order[:7])

    out[...] = mul(gated.astype(BF16), w_out_v[...]).astype(BF16)
    gu_v[...] = gg * normed
    z_start(z_order[7:9])

    dq_v[...] = jnp.zeros_like(dq_v)
    dk_v[...] = jnp.zeros_like(dk_v)
    dv_v[...] = jnp.zeros_like(dv_v)

    def query_step(c):
        for h in range(HEADS):
            gw = mul_t(do_all[rows, head(0, h)], act_all[pair(c), head(V_COL, h)])
            gs = (gw * g_v[c, h]).astype(BF16)
            dq_v[:, head(0, h)] += mul(gs, act_all[pair(c), head(K_COL, h)])

    each(0, y + 1, query_step)

    z_start(z_order[9:])

    def back(grad, base):
        cols = pl.ds(base, WIDTH)
        return mul_t((grad * slope_v[:, cols]).astype(BF16), w_in_v[:, cols])

    ge_v[...] = back(gu_v[...], U_COL) + back(dq_v[...], Q_COL)

    def key_step(c):
        for h in range(HEADS):
            do_h = do_all[pair(c), head(0, h)]
            gw = mul_t(act_all[rows, head(V_COL, h)], do_h)
            gs = (gw * g_v[c + 1, h]).astype(BF16)
            dv_v[:, head(0, h)] += mul(p_v[c, h], do_h)
            dk_v[:, head(0, h)] += mul(gs, act_all[pair(c), head(Q_COL, h)])

    arrived(do_all, sib, d_ssem, d_rsem)
    key_step(y)

    def hand_over(c):
        return remote(do_all, c * 2 + core, d_ssem.at[Y + c], d_rsem, sib)

    def later_chip(c):
        arrived(do_all, c * 2 + core, d_ssem, d_rsem)
        hand_over(c).start()
        arrived(do_all, c * 2 + other, d_ssem, d_rsem)
        key_step(c)

    each(y + 1, Y, later_chip)

    grad_events[...] = (ge_v[...] + back(dv_v[...], V_COL) + back(dk_v[...], K_COL)).astype(BF16)

    holder = z // ZH
    c_order = sorted(range(1, 2 * Y), key=lambda k: -min(k, 2 * Y - k))

    def c_out(k):
        return pltpu.make_async_remote_copy(
            src_ref=c_recv.at[y], dst_ref=c_recv.at[y], send_sem=c_ssem.at[k], recv_sem=c_rsem.at[y],
            device_id=(dp, (ctx + k) % (2 * Y)), device_id_type=MESH,
        )

    def c_in(k):
        return pltpu.make_async_remote_copy(
            src_ref=c_recv.at[k], dst_ref=c_recv.at[k], send_sem=c_ssem.at[0], recv_sem=c_rsem.at[k],
            device_id=(dp, sib), device_id_type=MESH,
        )

    e_ring.done()
    c_star.done()
    d_sib.wait_send()
    each(0, y, lambda c: d_out(c).wait_send())
    each(y + 1, Y, lambda c: hand_over(c).wait_send())
    for d, swap in gt_order:
        gt_out(d, swap).wait_send()

    def z_done(k):
        @pl.when(core * ZH + k != z)
        def _():
            z_out(k).wait_send()

    each(0, ZH, z_done)

    @pl.when(core == holder)
    def _():
        z_recv[z] = z_send[z % ZH]

        def wait_z(k):
            @pl.when(k != z)
            def _():
                z_in(k).wait_recv()

        each(0, Z, wait_z)
        total = jnp.sum(z_recv[...].astype(F32), axis=0)
        c_recv[y] = total.astype(BF16)
        for k in c_order:
            c_out(k).start()

    def wait_c(k):
        @pl.when(k * 2 + holder != ctx)
        def _():
            c_in(k).wait_recv()

    each(0, Y, wait_c)
    tokens = R * 2 * Y * Z * X
    total = jnp.sum(c_recv[...].astype(F32), axis=0) * (1.0 / math.sqrt(tokens))
    grad_w_out[...] = jnp.concatenate([total[:RD], total[RD:]], axis=1)

    @pl.when(core == holder)
    def _():
        each(1, 2 * Y, lambda k: c_out(k).wait_send())


def in_hbm(a):
    return pltpu.with_memory_space_constraint(a, pltpu.HBM)


def store(*refs):
    copies = [pltpu.make_async_copy(refs[n], refs[3 + n], refs[6].at[n]) for n in range(3)]
    for copy in copies:
        copy.start()
    for copy in copies:
        copy.wait()


def build(mesh, X):
    Z, Y = mesh.shape["dp"] // X, mesh.shape["ctx"] // 2

    def per_device(events, keep, lengths, cotangent, w_in, w_out):
        R, D = events.shape[1:]
        L = R * 2 * Y
        S = 2 * X
        ZH, RD = Z // 2, D // (Z * X)
        vmem = pl.BlockSpec(memory_space=pltpu.VMEM)
        hbm = pl.BlockSpec(memory_space=pltpu.HBM)
        dma = pltpu.SemaphoreType.DMA
        output, grad_events, grad_w_out = pl.pallas_call(
            functools.partial(kernel, Z, X, Y),
            out_shape=(pltpu.VMEM((R, D), BF16), pltpu.VMEM((R, D), BF16), pltpu.VMEM((RD, D), F32)),
            in_specs=[hbm, hbm, pl.BlockSpec(memory_space=pltpu.SMEM), hbm, hbm, hbm],
            out_specs=[vmem] * 3,
            scratch_shapes=[
                pltpu.VMEM((1, R), jnp.int32),
                pltpu.VMEM((L, D), BF16),
                pltpu.VMEM((L, 4 * WIDTH), BF16),
                pltpu.VMEM((L, WIDTH), BF16),
                pltpu.VMEM((S * R, D), BF16),
                pltpu.VMEM((D, 4 * WIDTH), BF16),
                pltpu.VMEM((WIDTH, D), BF16),
                pltpu.VMEM((R, 4 * WIDTH), F32),
                pltpu.VMEM((R, WIDTH), F32),
                pltpu.VMEM((R, WIDTH), F32),
                pltpu.VMEM((R, WIDTH), F32),
                pltpu.VMEM((R, WIDTH), F32),
                pltpu.VMEM((R, WIDTH), F32),
                pltpu.VMEM((R, WIDTH), F32),
                pltpu.VMEM((R, D), F32),
                pltpu.VMEM((Y + 1, HEADS, R, 2 * R), F32),
                pltpu.VMEM((Y, HEADS, R, 2 * R), BF16),
                pltpu.VMEM((HEADS, R, 2 * R), BF16),
                pltpu.VMEM((X, Z * RD, R), BF16),
                pltpu.VMEM((ZH * RD, S * R), BF16),
                pltpu.VMEM((ZH, 2 * RD, D // 2), BF16),
                pltpu.VMEM((Z, 2 * RD, D // 2), BF16),
                pltpu.VMEM((Y, 2 * RD, D // 2), BF16),
                pltpu.SemaphoreType.REGULAR, pltpu.SemaphoreType.REGULAR,
                dma((8,)),
                dma((20,)), dma((6 * Y,)),
                dma((2 * Y,)), dma((2 * Y,)),
                dma((2 * X,)), dma((2 * X,)),
                dma((S,)), dma((S,)),
                dma((ZH,)), dma((Z,)),
                dma((2 * Y,)), dma((Y,)),
            ],
            compiler_params=pltpu.CompilerParams(
                collective_id=0, has_side_effects=True, vmem_limit_bytes=56 * 1024 * 1024
            ),
            name="layer",
        )(in_hbm(events[0]), in_hbm(keep), lengths, in_hbm(cotangent[0]), in_hbm(w_in), in_hbm(w_out))
        output, grad_events, grad_w_out = pl.pallas_call(
            store,
            out_shape=(
                jax.ShapeDtypeStruct((R, D), BF16),
                jax.ShapeDtypeStruct((R, D), BF16),
                jax.ShapeDtypeStruct((RD, D), F32),
            ),
            in_specs=[vmem] * 3,
            out_specs=(hbm, hbm, hbm),
            scratch_shapes=[dma((3,))],
            name="store",
        )(*[pltpu.with_memory_space_constraint(a, pltpu.VMEM) for a in (output, grad_events, grad_w_out)])
        return (output[None], grad_events[None], grad_w_out)

    return jax.shard_map(
        per_device,
        mesh=mesh,
        in_specs=(P("dp", "ctx", None), P("dp", "ctx"), P("dp"), P("dp", "ctx", None), P(), P()),
        out_specs=(P("dp", "ctx", None), P("dp", "ctx", None), P("dp", None)),
        check_vma=False,
    )


def solution(mesh):
    return build(mesh, X_CHIPS)
```
